32 devices in a mesh: dp: 4 (over x, core), seq: 2 (over y), tensor: 4 (over z).
Axes of the slice: x: 2, y: 2, z: 4, core: 2. Of those that a mesh axis runs over, the one named last changes fastest.
Arguments:
- hidden: bfloat16 [8, 2048, 1536], P('dp', ('seq', 'tensor')), may hold values from -6 to 6
- cotangent: bfloat16 [8, 2048, 1536], P('dp', ('seq', 'tensor')), may hold values from -6 to 6
- norm_gain: bfloat16 [1536], replicated, may hold values from 0.5 to 1.5
- w_z: bfloat16 [1536, 3072], P(('dp', 'seq'), 'tensor'), may hold values from -0.15625 to 0.15625
- w_x: bfloat16 [1536, 3072], P(('dp', 'seq'), 'tensor'), may hold values from -0.15625 to 0.15625
- w_bc: bfloat16 [1536, 256], P(('dp', 'seq')), may hold values from -0.15625 to 0.15625
- w_dt: bfloat16 [1536, 48], P(('dp', 'seq'), 'tensor'), may hold values from -0.15625 to 0.15625
- conv_x: bfloat16 [4, 3072], P(None, 'tensor'), may hold values from -3 to 3
- conv_x_bias: bfloat16 [3072], P('tensor'), may hold values from -0.5 to 0.5
- conv_bc: bfloat16 [4, 256], replicated, may hold values from -3 to 3
- conv_bc_bias: bfloat16 [256], replicated, may hold values from -0.5 to 0.5
- dt_bias: float32 [48], P('tensor'), may hold values from -7 to -2
- a_log: float32 [48], P('tensor'), may hold values from 0 to 2.77
- d_skip: float32 [48], P('tensor'), may hold values from 0.5 to 1.5
- inner_gain: bfloat16 [3072], P('tensor'), may hold values from 0.5 to 1.5
- w_out: bfloat16 [3072, 1536], P('tensor', ('dp', 'seq')), may hold values from -0.109375 to 0.109375
Outputs:
- output: bfloat16 [8, 2048, 1536], P('dp', ('seq', 'tensor'))
- grad_hidden: float32 [8, 2048, 1536], P('dp', ('seq', 'tensor'))
- grad_norm_gain: float32 [1536], replicated
- grad_w_z: float32 [1536, 3072], P(('dp', 'seq'), 'tensor')
- grad_w_x: float32 [1536, 3072], P(('dp', 'seq'), 'tensor')
- grad_w_bc: float32 [1536, 256], P(('dp', 'seq'))
- grad_w_dt: float32 [1536, 48], P(('dp', 'seq'), 'tensor')
- grad_conv_x: float32 [4, 3072], P(None, 'tensor')
- grad_conv_x_bias: float32 [3072], P('tensor')
- grad_conv_bc: float32 [4, 256], replicated
- grad_conv_bc_bias: float32 [256], replicated
- grad_dt_bias: float32 [48], P('tensor')
- grad_a_log: float32 [48], P('tensor')
- grad_d_skip: float32 [48], P('tensor')
- grad_inner_gain: float32 [3072], P('tensor')
- grad_w_out: float32 [3072, 1536], P('tensor', ('dp', 'seq'))
The draws below stay inside these ranges and needn't reach their ends.
All inputs are finite; a program needn't handle non-finite values.
Results may differ from the reference program's by a relative error of at most 0.014.
Values may be sent and summed in bfloat16 or wider, within the bound.
No kernel may reach another device: no remote copies, remote signals or barrier semaphores. Data moves between devices by JAX's collectives and lax.ppermute only.
A program may use at most 136 MiB of HBM per device.

```python
import jax
import jax.numpy as jnp
from jax import lax

D = 1536
HEADS = 48
HEAD_DIM = 64
NSTATE = 128
INNER = 3072
KCONV = 4
BLOCK = 256
LEN = 2048
SEQS = 8


def level_of(key, extent, cuts, least, largest):
    def one(dim, shards_of):
        draws = jax.random.uniform(jax.random.fold_in(jax.random.fold_in(key, 6), dim), (shards_of,), jnp.float32, least / len(cuts), largest / len(cuts))
        return jnp.repeat(jnp.exp(draws), extent[dim] // shards_of).reshape((-1,) + (1,) * (len(extent) - dim - 1))

    level = one(*cuts[0])
    for cut in cuts[1:]:
        level = level * one(*cut)
    return level


def gaussian(own_key, dims, scale, reach, shards=(), dtype=jnp.bfloat16):
    array = jax.random.normal(own_key, dims, jnp.float32) * scale
    if len(shards) > 0:
        array = level_of(own_key, dims, shards, -0.22, 0.18) * array
    return jnp.clip(array, min=-reach, max=reach).astype(dtype)


def setup_inputs(seed: int = 0) -> dict:
    streams_of = jax.random.split(jax.random.key(seed), 17)
    return {
        "hidden": gaussian(streams_of[0], (SEQS, LEN, D), 1.0, 6.0, ((0, 4), (1, 8))),
        "cotangent": gaussian(streams_of[1], (SEQS, LEN, D), 1.0, 6.0, ((0, 4), (1, 8))),
        "norm_gain": jnp.clip(1.0 + 0.1 * jax.random.normal(streams_of[2], (D,), jnp.float32), 0.5, 1.5).astype(jnp.bfloat16),
        "w_z": gaussian(streams_of[3], (D, INNER), D ** -0.5, 0.15625, ((0, 8), (1, 4))),
        "w_x": gaussian(streams_of[4], (D, INNER), D ** -0.5, 0.15625, ((0, 8), (1, 4))),
        "w_bc": gaussian(streams_of[5], (D, 2 * NSTATE), D ** -0.5, 0.15625, ((0, 8),)),
        "w_dt": gaussian(streams_of[6], (D, HEADS), D ** -0.5, 0.15625, ((0, 8), (1, 4))),
        "conv_x": gaussian(streams_of[7], (KCONV, INNER), KCONV ** -0.5, 3.0, ((1, 4),)),
        "conv_x_bias": jnp.clip(jax.random.uniform(streams_of[8], (INNER,), jnp.float32, -0.5, 0.5) * level_of(streams_of[8], (INNER,), ((0, 4),), -0.4, 0.0), -0.5, 0.5).astype(jnp.bfloat16),
        "conv_bc": gaussian(streams_of[9], (KCONV, 2 * NSTATE), KCONV ** -0.5, 3.0),
        "conv_bc_bias": jnp.clip(jax.random.uniform(streams_of[10], (2 * NSTATE,), jnp.float32, -0.5, 0.5), -0.5, 0.5).astype(jnp.bfloat16),
        "dt_bias": jnp.clip(-7.0 + 5.0 * jax.random.uniform(streams_of[11], (HEADS,), jnp.float32) ** level_of(streams_of[11], (HEADS,), ((0, 4),), -0.2, 0.2), -7.0, -2.0),
        "a_log": jnp.clip(2.77 * jax.random.uniform(streams_of[12], (HEADS,), jnp.float32) ** level_of(streams_of[12], (HEADS,), ((0, 4),), -0.2, 0.2), 0.0, 2.77),
        "d_skip": jnp.clip(0.5 + 1.0 * jax.random.uniform(streams_of[13], (HEADS,), jnp.float32) ** level_of(streams_of[13], (HEADS,), ((0, 4),), -0.2, 0.2), 0.5, 1.5),
        "inner_gain": jnp.clip(1.0 + 0.1 * jax.random.normal(streams_of[14], (INNER,), jnp.float32), 0.5, 1.5).astype(jnp.bfloat16),
        "w_out": gaussian(streams_of[15], (INNER, D), INNER ** -0.5, 0.109375, ((0, 4), (1, 8))),
    }


EPS = 1e-05
exact_mode = lax.Precision.HIGHEST

@jax.custom_vjp
def low(v):
    return lax.optimization_barrier(v.astype(jnp.bfloat16)).astype(jnp.float32)

@jax.custom_vjp
def low_back(v):
    return v

def low_keep(v):
    return (low(v), None)

def low_pass(kept, grad):
    return (grad,)

def back_keep(v):
    return (v, None)

def back_low(kept, grad):
    return (low(grad),)
low.defvjp(low_keep, low_pass)
low_back.defvjp(back_keep, back_low)

def round_both(values):
    return low_back(low(values))

def matmul(left, right):
    return jnp.dot(left, right, precision=exact_mode)

def block_scan(carry_state, inputs):
    xs_blk, b_blk, c_blk, step_blk, decay_blk = inputs
    cumul = jnp.cumsum(decay_blk, axis=0)
    diff = cumul[:, None, :] - cumul[None, :, :]
    row_pos = lax.broadcasted_iota(jnp.int32, (BLOCK, BLOCK, 1), 0)
    col_pos = lax.broadcasted_iota(jnp.int32, (BLOCK, BLOCK, 1), 1)
    causal = row_pos >= col_pos
    decay = jnp.where(causal, jnp.exp(jnp.where(causal, diff, 0.0)), 0.0)
    scores = matmul(c_blk, b_blk.T)
    weights = scores[:, :, None] * decay * step_blk[None, :, :]
    intra = jnp.einsum('tsh,shp->thp', weights, xs_blk, precision=exact_mode)
    carried = jnp.exp(cumul)[:, :, None] * jnp.einsum('tn,hpn->thp', c_blk, carry_state, precision=exact_mode)
    tail = jnp.exp(cumul[-1][None, :] - cumul) * step_blk
    new_state = jnp.exp(cumul[-1])[:, None, None] * carry_state + jnp.einsum('sh,shp,sn->hpn', tail, xs_blk, b_blk, precision=exact_mode)
    return (new_state, intra + carried)

def layer(inputs, params):
    norm_gain, w_z, w_x, w_bc, w_dt, conv_x, conv_x_bias, conv_bc, conv_bc_bias, dt_bias, a_log, d_skip, inner_gain, w_out = params
    scale = lax.rsqrt(lax.optimization_barrier(jnp.mean(inputs * inputs, axis=-1, keepdims=True)) + EPS)
    normed = low(inputs * scale * norm_gain)
    gate_in = round_both(matmul(normed, w_z))
    mix_in = round_both(jnp.concatenate([matmul(normed, w_x), matmul(normed, w_bc)], axis=1))
    step_in = round_both(matmul(normed, w_dt))
    conv_weight = jnp.concatenate([conv_x, conv_bc], axis=1)
    conv_bias = jnp.concatenate([conv_x_bias, conv_bc_bias])
    padded = jnp.pad(mix_in, ((KCONV - 1, 0), (0, 0)))
    pre = conv_bias + jnp.zeros_like(mix_in)
    for offset in range(KCONV):
        pre = pre + conv_weight[offset] * padded[offset:offset + LEN]
    act = jax.nn.silu(pre)
    xs = round_both(act[:, :INNER]).reshape(LEN, HEADS, HEAD_DIM)
    b_state = round_both(act[:, INNER:INNER + NSTATE])
    c_state = round_both(act[:, INNER + NSTATE:])
    step = jax.nn.softplus(step_in + dt_bias)
    log_decay = -jnp.exp(a_log) * step
    block_count = LEN // BLOCK
    stacked = (xs.reshape(block_count, BLOCK, HEADS, HEAD_DIM), b_state.reshape(block_count, BLOCK, NSTATE), c_state.reshape(block_count, BLOCK, NSTATE), step.reshape(block_count, BLOCK, HEADS), log_decay.reshape(block_count, BLOCK, HEADS))
    start_state = jnp.zeros((HEADS, HEAD_DIM, NSTATE), jnp.float32)
    _, mixer_out = lax.scan(jax.checkpoint(block_scan), start_state, stacked)
    mixer_out = mixer_out.reshape(LEN, HEADS, HEAD_DIM) + d_skip[:, None] * xs
    gated = mixer_out.reshape(LEN, INNER) * jax.nn.silu(gate_in)
    inner_scale = lax.rsqrt(lax.optimization_barrier(jnp.mean(gated * gated, axis=-1, keepdims=True)) + EPS)
    mixed = low(gated * inner_scale * inner_gain)
    branch = low_back(matmul(mixed, w_out))
    return inputs + branch

def reference(hidden, cotangent, norm_gain, w_z, w_x, w_bc, w_dt, conv_x, conv_x_bias, conv_bc, conv_bc_bias, dt_bias, a_log, d_skip, inner_gain, w_out):
    params = tuple((value.astype(jnp.float32) for value in (norm_gain, w_z, w_x, w_bc, w_dt, conv_x, conv_x_bias, conv_bc, conv_bc_bias, dt_bias, a_log, d_skip, inner_gain, w_out)))

    def per_sequence(totals, pair):
        seq_input, seq_cot = pair
        result, pullback = jax.vjp(layer, seq_input.astype(jnp.float32), params)
        grad_input, grad_params = pullback(seq_cot.astype(jnp.float32))
        totals = jax.tree.map(lambda first, second: first + second, totals, grad_params)
        return (totals, (result.astype(jnp.bfloat16), grad_input))
    zero_grads = jax.tree.map(jnp.zeros_like, params)
    totals, (outputs, grad_hidden) = lax.scan(per_sequence, zero_grads, (hidden, cotangent))
    return (outputs, grad_hidden, totals[0], totals[1], totals[2], totals[3], totals[4], totals[5], totals[6], totals[7], totals[8], totals[9], totals[10], totals[11], totals[12], totals[13])
```

```python
import functools

import jax
import jax.numpy as jnp
from jax import lax
from jax.experimental import pallas as pl
from jax.experimental.pallas import tpu as pltpu
from jax.sharding import Mesh
from jax.sharding import PartitionSpec as P

CHUNK = 256
HALF = CHUNK // 2
LANES = 128
STRIP = 256
RIM = 16
EPS = 1e-05
F32 = jnp.float32
BF16 = jnp.bfloat16
VMEM_BYTES = 48 * 1024 * 1024


def dot(left, right):
    return lax.dot_general(left, right, (((1,), (0,)), ((), ())), preferred_element_type=F32)


def dot_nt(left, right):
    return lax.dot_general(left, right, (((1,), (1,)), ((), ())), preferred_element_type=F32)


def pieces(value, count):
    terms = []
    for _ in range(count):
        term = value.astype(BF16)
        terms.append(term)
        value = value - term.astype(F32)
    return terms


def spread_heads(value, spread):
    return sum(dot(term, spread) for term in pieces(value, 2))


def gather_heads(value, spread):
    return sum(dot_nt(term, spread) for term in pieces(value, 2))


def running_sum(value, mask):
    return sum(dot(mask, term) for term in pieces(value, 3))


def iota2(rows, cols, dim):
    return lax.broadcasted_iota(jnp.int32, (rows, cols), dim)


def turned(value):
    return jnp.transpose(value.astype(F32)).astype(BF16)


def strips(width):
    return [slice(at, at + STRIP) for at in range(0, width, STRIP)]


def conv_pre(ext, taps, cols):
    total = taps[4:5, cols] + taps[0:1, cols] * ext[pl.ds(RIM - 3, CHUNK), cols]
    for k in range(1, 4):
        total = total + taps[k : k + 1, cols] * ext[pl.ds(RIM - 3 + k, CHUNK), cols]
    return total


def softplus(value):
    return jnp.maximum(value, 0.0) + jnp.log1p(jnp.exp(-jnp.abs(value)))


def state_kernel(
    mix_ref, halo_ref, step_ref, taps_ref, heads_ref, spread_ref,
    xbc_ref, sum_ref, dt_ref, end_ref, total_ref, ext,
):
    inner = spread_ref.shape[1]
    place = pl.program_id(1)

    @pl.when(place == 0)
    def _():
        ext[0:RIM, :] = halo_ref[0].astype(F32)
        end_ref[...] = jnp.zeros_like(end_ref)
        total_ref[...] = jnp.zeros_like(total_ref)

    @pl.when(place > 0)
    def _():
        ext[0:RIM, :] = ext[CHUNK : CHUNK + RIM, :]

    dt = softplus(step_ref[0].astype(F32) + heads_ref[0:1, :])
    lower = (iota2(CHUNK, CHUNK, 0) >= iota2(CHUNK, CHUNK, 1)).astype(F32).astype(BF16)
    cumul = running_sum(dt * heads_ref[1:2, :], lower)
    sum_ref[0] = cumul
    dt_ref[0] = dt
    last = cumul[CHUNK - 1 : CHUNK, :]
    total_ref[0] += jnp.broadcast_to(last, total_ref.shape[1:])
    tail = jnp.exp(last - cumul) * dt
    decay = jnp.broadcast_to(jnp.exp(last), (8, LANES))
    b_turned = None
    for cols in reversed(strips(xbc_ref.shape[2])):
        ext[RIM:, cols] = mix_ref[0, :, cols].astype(F32)
        pre = conv_pre(ext, taps_ref, cols)
        act = (pre * jax.nn.sigmoid(pre)).astype(BF16)
        xbc_ref[0, :, cols] = act
        if cols.start >= inner:
            b_turned = turned(act[:, 0:LANES])
        else:
            held = spread_ref[:, cols]
            weighted = (act.astype(F32) * spread_heads(tail, held)).astype(BF16)
            kept = end_ref[0, :, cols] * spread_heads(decay, held)[0:1, :]
            end_ref[0, :, cols] = kept + dot(b_turned, weighted)


def scan_kernel(
    xbc_ref, sum_ref, dt_ref, start_ref, gate_ref, gm_ref, rows_ref, spread_ref,
    y_ref, mixed_ref, enter_ref, stat_ref, state,
):
    inner = spread_ref.shape[1]

    @pl.when(pl.program_id(1) == 0)
    def _():
        state[...] = start_ref[0]

    cumul = sum_ref[0]
    dt = dt_ref[0]
    across = jnp.transpose(cumul)
    last = cumul[CHUNK - 1 : CHUNK, :]
    tail = jnp.exp(last - cumul) * dt
    reach = jnp.exp(cumul)
    decay = jnp.broadcast_to(jnp.exp(last), (8, LANES))
    b_low = xbc_ref[0, :, inner : inner + LANES]
    c_low = xbc_ref[0, :, inner + LANES :]
    b_turned = turned(b_low)
    score = dot_nt(c_low, b_low)
    causal = iota2(HALF, HALF, 0) >= iota2(HALF, HALF, 1)
    first = iota2(1, LANES, 1) < LANES // 2
    squares = jnp.zeros((CHUNK, STRIP), F32)
    crossed = jnp.zeros((CHUNK, STRIP), F32)
    for cols in strips(inner):
        held = spread_ref[:, cols]
        x = xbc_ref[0, :, cols].astype(F32)
        u = x * spread_heads(dt, held)
        weighted = (x * spread_heads(tail, held)).astype(BF16)
        entering = state[:, cols].astype(BF16)
        enter_ref[0, 0, :, cols] = entering
        carried = dot(c_low, entering) * spread_heads(reach, held)
        state[:, cols] = state[:, cols] * spread_heads(decay, held)[0:1, :] + dot(b_turned, weighted)
        for pair in range(STRIP // LANES):
            lanes = slice(pair * LANES, (pair + 1) * LANES)
            top = carried[0:HALF, lanes]
            bottom = carried[HALF:, lanes]
            for side in range(2):
                head = (cols.start + pair * LANES) // (LANES // 2) + side
                mine = jnp.where(first if side == 0 else ~first, u[:, lanes], 0.0).astype(BF16)
                column = cumul[:, head : head + 1]
                row = across[head : head + 1, :]
                corner = jnp.where(causal, jnp.exp(column[0:HALF] - row[:, 0:HALF]), 0.0)
                top = top + dot((score[0:HALF, 0:HALF] * corner).astype(BF16), mine[0:HALF])
                left = jnp.exp(column[HALF:] - row[:, 0:HALF])
                right = jnp.where(causal, jnp.exp(column[HALF:] - row[:, HALF:]), 0.0)
                bottom = bottom + dot((score[HALF:, 0:HALF] * left).astype(BF16), mine[0:HALF])
                bottom = bottom + dot((score[HALF:, HALF:] * right).astype(BF16), mine[HALF:])
            into = slice(cols.start + pair * LANES, cols.start + (pair + 1) * LANES)
            y_ref[0, 0:HALF, into] = top
            y_ref[0, HALF:, into] = bottom
        y = y_ref[0, :, cols] + rows_ref[0:1, cols] * x
        gate = gate_ref[0, :, cols].astype(F32)
        gated = y * gate * jax.nn.sigmoid(gate)
        gained = gated * rows_ref[1:2, cols]
        mixed_ref[0, :, cols] = gained.astype(BF16)
        squares = squares + gated * gated
        crossed = crossed + gained * gm_ref[0, :, cols]
    ones = jnp.ones((8, STRIP), BF16)
    square_row = sum(dot_nt(ones, term) for term in pieces(squares, 3))
    cross_row = sum(dot_nt(ones, term) for term in pieces(crossed, 3))
    stat_ref[0] = jnp.where(iota2(8, CHUNK, 0) == 0, square_row, cross_row)


def gate_kernel(
    inner_full, y_ref, xbc_ref, gate_ref, gm_ref, stat_ref, sum_ref, rows_ref, spread_ref,
    gy_ref, gz_ref, mixed_ref, back_ref, gain_ref,
):
    inner = spread_ref.shape[1]

    @pl.when(pl.program_id(1) == 0)
    def _():
        back_ref[...] = jnp.zeros_like(back_ref)

    @pl.when((pl.program_id(0) == 0) & (pl.program_id(1) == 0))
    def _():
        gain_ref[...] = jnp.zeros_like(gain_ref)

    stats = jnp.transpose(stat_ref[0])
    scale = lax.rsqrt(stats[:, 0:1] / inner_full + EPS)
    bent = scale * scale * scale * (stats[:, 1:2] / inner_full)
    cumul = sum_ref[0]
    reach = jnp.exp(cumul)
    decay = jnp.broadcast_to(jnp.exp(cumul[CHUNK - 1 : CHUNK, :]), (8, LANES))
    c_turned = turned(xbc_ref[0, :, inner + LANES :])
    for cols in strips(inner):
        held = spread_ref[:, cols]
        x = xbc_ref[0, :, cols].astype(F32)
        y = y_ref[0, :, cols] + rows_ref[0:1, cols] * x
        gate = gate_ref[0, :, cols].astype(F32)
        sigmoid = jax.nn.sigmoid(gate)
        silu = gate * sigmoid
        gated = y * silu
        scaled = gated * scale
        gm = gm_ref[0, :, cols]
        gain = rows_ref[1:2, cols]
        gg = scale * gm * gain - gated * bent
        gy = (gg * silu).astype(BF16)
        gy_ref[0, :, cols] = gy
        gz_ref[0, :, cols] = (gg * y * sigmoid * (1.0 + gate * (1.0 - sigmoid))).astype(BF16)
        mixed_ref[0, :, cols] = (scaled * gain).astype(BF16)
        gain_ref[:, cols] += jnp.broadcast_to(jnp.sum(gm * scaled, axis=0, keepdims=True), (8, STRIP))
        reached = (gy.astype(F32) * spread_heads(reach, held)).astype(BF16)
        kept = back_ref[0, :, cols] * spread_heads(decay, held)[0:1, :]
        back_ref[0, :, cols] = kept + dot(c_turned, reached)


def adjoint_kernel(
    xbc_ref, sum_ref, dt_ref, gy_ref, y_ref, enter_ref, gin_ref, mix_ref, before_ref, halo_ref,
    step_ref, taps_ref, heads_ref, rows_ref, spread_ref,
    gmix_ref, rim_ref, gtaps_ref, gheads_ref, gskip_ref, back, ext, gpre, pulled,
):
    inner = spread_ref.shape[1]
    chunks = pl.num_programs(1)
    order = pl.program_id(1)

    @pl.when((pl.program_id(0) == 0) & (order == 0))
    def _():
        gtaps_ref[...] = jnp.zeros_like(gtaps_ref)
        gheads_ref[...] = jnp.zeros_like(gheads_ref)
        gskip_ref[...] = jnp.zeros_like(gskip_ref)

    @pl.when(order == 0)
    def _():
        back[...] = gin_ref[0]
        gpre[CHUNK:, :] = jnp.zeros((8, gpre.shape[1]), F32)

    @pl.when(order > 0)
    def _():
        gpre[CHUNK:, :] = gpre[0:8, :]

    @pl.when(order == chunks - 1)
    def _():
        ext[0:RIM, :] = halo_ref[0].astype(F32)

    @pl.when(order < chunks - 1)
    def _():
        ext[0:RIM, :] = before_ref[0].astype(F32)

    cumul = sum_ref[0]
    dt = dt_ref[0]
    across = jnp.transpose(cumul)
    last = cumul[CHUNK - 1 : CHUNK, :]
    fade = jnp.exp(last - cumul)
    reach = jnp.exp(cumul)
    decay = jnp.broadcast_to(jnp.exp(last), (8, LANES))
    b_low = xbc_ref[0, :, inner : inner + LANES]
    c_low = xbc_ref[0, :, inner + LANES :]
    c_turned = turned(c_low)
    score = dot_nt(b_low, c_low)
    causal = iota2(HALF, HALF, 0) <= iota2(HALF, HALF, 1)
    first = iota2(1, LANES, 1) < LANES // 2
    pulled[...] = jnp.zeros_like(pulled)
    gb = jnp.zeros((CHUNK, LANES), F32)
    gc = jnp.zeros((CHUNK, LANES), F32)
    between = jnp.zeros((CHUNK, LANES), F32)
    arrived = jnp.zeros((CHUNK, LANES), F32)
    direct = jnp.zeros((CHUNK, LANES), F32)
    joined = jnp.zeros((8, LANES), F32)

    def conv_part(cols, gact):
        ext[RIM:, cols] = mix_ref[0, :, cols].astype(F32)
        pre = conv_pre(ext, taps_ref, cols)
        sigmoid = jax.nn.sigmoid(pre)
        gp = gact.astype(BF16).astype(F32) * sigmoid * (1.0 + pre * (1.0 - sigmoid))
        gpre[0:CHUNK, cols] = gp
        rim_ref[0, :, cols] = gp[0:8, :]
        total = taps_ref[3:4, cols] * gp
        for k in range(3):
            total = total + taps_ref[k : k + 1, cols] * gpre[pl.ds(3 - k, CHUNK), cols]
            gtaps_ref[k : k + 1, cols] += jnp.sum(
                gp * ext[pl.ds(RIM - 3 + k, CHUNK), cols], axis=0, keepdims=True
            )
        gtaps_ref[3:4, cols] += jnp.sum(gp * ext[RIM:, cols], axis=0, keepdims=True)
        gtaps_ref[4:5, cols] += jnp.sum(gp, axis=0, keepdims=True)
        gmix_ref[0, :, cols] = total.astype(BF16)

    for cols in strips(inner):
        held = spread_ref[:, cols]
        x = xbc_ref[0, :, cols].astype(F32)
        dt_wide = spread_heads(dt, held)
        fade_wide = spread_heads(fade, held)
        u = x * dt_wide
        u_low = u.astype(BF16)
        weighted = (u * fade_wide).astype(BF16)
        gy_low = gy_ref[0, :, cols]
        gy = gy_low.astype(F32)
        reached = (gy * spread_heads(reach, held)).astype(BF16)
        later = back[:, cols]
        later_low = later.astype(BF16)
        entered = enter_ref[0, 0, :, cols]
        gb = gb + dot_nt(weighted, later_low)
        gc = gc + dot_nt(reached, entered)
        gu_carried = dot(b_low, later_low) * fade_wide
        sums = jnp.sum(later * entered.astype(F32), axis=0, keepdims=True)
        joined = joined + gather_heads(jnp.broadcast_to(sums, (8, STRIP)), held)
        back[:, cols] = later * spread_heads(decay, held)[0:1, :] + dot(c_turned, reached)
        parts = []
        for pair in range(STRIP // LANES):
            lanes = slice(pair * LANES, (pair + 1) * LANES)
            top = gu_carried[0:HALF, lanes]
            bottom = gu_carried[HALF:, lanes]
            gy_pair = gy_low[:, lanes]
            for side in range(2):
                head = (cols.start + pair * LANES) // (LANES // 2) + side
                keep = first if side == 0 else ~first
                gy_mine = jnp.where(keep, gy[:, lanes], 0.0).astype(BF16)
                u_mine = jnp.where(keep, u[:, lanes], 0.0).astype(BF16)
                column = cumul[:, head : head + 1]
                row = across[head : head + 1, :]
                corner = jnp.where(causal, jnp.exp(row[:, 0:HALF] - column[0:HALF]), 0.0)
                side_right = jnp.exp(row[:, HALF:] - column[0:HALF])
                low_right = jnp.where(causal, jnp.exp(row[:, HALF:] - column[HALF:]), 0.0)
                top = top + dot((score[0:HALF, 0:HALF] * corner).astype(BF16), gy_mine[0:HALF])
                top = top + dot((score[0:HALF, HALF:] * side_right).astype(BF16), gy_mine[HALF:])
                bottom = bottom + dot((score[HALF:, HALF:] * low_right).astype(BF16), gy_mine[HALF:])
                upper = dot_nt(u_mine[0:HALF], gy_pair)
                pulled[0:HALF, 0:HALF] += upper[:, 0:HALF] * corner
                pulled[0:HALF, HALF:] += upper[:, HALF:] * side_right
                pulled[HALF:, HALF:] += dot_nt(u_mine[HALF:], gy_pair[HALF:]) * low_right
            parts.append(jnp.concatenate([top, bottom], axis=0))
        gu = jnp.concatenate(parts, axis=1)
        u_kept = u_low.astype(F32)
        between = between + gather_heads(gy * y_ref[0, :, cols] - u_kept * gu, held)
        arrived = arrived + gather_heads(u_kept * gu_carried, held)
        direct = direct + gather_heads(x * gu, held)
        gskip_ref[:, cols] += jnp.broadcast_to(jnp.sum(gy * x, axis=0, keepdims=True), (8, STRIP))
        conv_part(cols, dt_wide * gu + rows_ref[0:1, cols] * gy)

    pulled_low = pulled[...].astype(BF16)
    gb = gb + dot(pulled_low, c_low)
    gc = gc + dot(jnp.transpose(pulled[...]).astype(BF16), b_low)
    conv_part(slice(inner, inner + 2 * LANES), jnp.concatenate([gb, gc], axis=1))

    upper = (iota2(CHUNK, CHUNK, 0) <= iota2(CHUNK, CHUNK, 1)).astype(F32).astype(BF16)
    whole = jnp.sum(arrived, axis=0, keepdims=True) + decay[0:1, :] * joined[0:1, :]
    glg = running_sum(between, upper) + whole
    rate = heads_ref[1:2, :]
    gdt = direct + rate * glg
    raw = step_ref[0].astype(F32) + heads_ref[0:1, :]
    gsi = gdt * jax.nn.sigmoid(raw) * heads_ref[2:3, :]
    gmix_ref[0, :, inner + 2 * LANES :] = gsi.astype(BF16)
    gheads_ref[0:1, :] += jnp.sum(gsi, axis=0, keepdims=True)
    gheads_ref[1:2, :] += jnp.sum(glg * dt * rate, axis=0, keepdims=True)


def tall(width, part, order=lambda i: i, column=0):
    return pl.BlockSpec((None, 1, CHUNK, width), lambda g, i: (part, g, order(i), column))


def flat(width, order=lambda i: i, column=0):
    return pl.BlockSpec((1, CHUNK, width), lambda g, i: (g, order(i), column))


def whole(*shape):
    return pl.BlockSpec((1,) + shape, lambda g, i: (g,) + (0,) * len(shape))


def fixed(shape):
    return pl.BlockSpec(shape, lambda g, i: (0,) * len(shape))


def shaped(shape, dtype=F32):
    return jax.ShapeDtypeStruct(shape, dtype)


def run(kernel, grid, ins, outs, scratch, flops, moved, into=None, after=()):
    into = {k: v for k, v in (into or {}).items() if v is not None}
    count = len(ins)
    extra = list(after) + list(into.values())

    def body(*refs):
        kernel(*refs[:count], *refs[count + len(extra) :])

    steps = grid[0] * grid[1]
    return pl.pallas_call(
        body,
        grid=grid,
        in_specs=[spec for _, spec in ins] + [pl.BlockSpec(memory_space=pl.ANY)] * len(extra),
        out_specs=[spec for _, spec in outs],
        out_shape=[shape for shape, _ in outs],
        scratch_shapes=scratch,
        input_output_aliases={count + len(after) + n: k for n, k in enumerate(into)},
        compiler_params=pltpu.CompilerParams(
            dimension_semantics=("arbitrary", "arbitrary"), vmem_limit_bytes=VMEM_BYTES
        ),
        cost_estimate=pl.CostEstimate(
            flops=steps * flops, bytes_accessed=steps * moved, transcendentals=0
        ),
    )(*[array for array, _ in ins], *extra)


def local_states(xw, halo, taps, heads, spread, after):
    groups, length, _ = xw.shape
    inner = spread.shape[1]
    width = inner + 2 * LANES
    return run(
        state_kernel,
        (groups, length // CHUNK),
        [
            (xw, flat(width)),
            (halo, whole(RIM, width)),
            (xw, flat(LANES, column=width // LANES)),
            (taps, fixed(taps.shape)),
            (heads, fixed(heads.shape)),
            (spread, fixed(spread.shape)),
        ],
        [
            (shaped((groups, length, width), BF16), flat(width)),
            (shaped((groups, length, LANES)), flat(LANES)),
            (shaped((groups, length, LANES)), flat(LANES)),
            (shaped((groups, LANES, inner)), whole(LANES, inner)),
            (shaped((groups, 8, LANES)), whole(8, LANES)),
        ],
        [pltpu.VMEM((RIM + CHUNK, width), F32)],
        1_500_000_000,
        2_000_000,
        None,
        after,
    )


def mixer(part, xbc, cumul, dt, start, gate, gm, rows, spread, gained, after):
    groups, length, width = xbc.shape
    inner = spread.shape[1]
    chunks = length // CHUNK
    return run(
        scan_kernel,
        (groups, chunks),
        [
            (xbc, flat(width)),
            (cumul, flat(LANES)),
            (dt, flat(LANES)),
            (start, whole(LANES, inner)),
            (gate, tall(inner, part)),
            (gm, tall(inner, part)),
            (rows, fixed(rows.shape)),
            (spread, fixed(spread.shape)),
        ],
        [
            (shaped((groups, length, inner)), flat(inner)),
            (shaped(gate.shape, BF16), tall(inner, part)),
            (
                shaped((groups, chunks, LANES, inner), BF16),
                pl.BlockSpec((1, 1, LANES, inner), lambda g, i: (g, i, 0, 0)),
            ),
            (shaped((groups, 8, length)), pl.BlockSpec((1, 8, CHUNK), lambda g, i: (g, 0, i))),
        ],
        [pltpu.VMEM((LANES, inner), F32)],
        2_500_000_000,
        4_000_000,
        {1: gained},
        after,
    )


def gate_back(part, inner_full, y, xbc, gate, gm, stats, cumul, rows, spread, gz, mixed, after):
    groups, length, width = xbc.shape
    inner = spread.shape[1]
    chunks = length // CHUNK
    back = lambda i: chunks - 1 - i
    return run(
        functools.partial(gate_kernel, float(inner_full)),
        (groups, chunks),
        [
            (y, flat(inner, back)),
            (xbc, flat(width, back)),
            (gate, tall(inner, part, back)),
            (gm, tall(inner, part, back)),
            (stats, pl.BlockSpec((1, 8, CHUNK), lambda g, i: (g, 0, back(i)))),
            (cumul, flat(LANES, back)),
            (rows, fixed(rows.shape)),
            (spread, fixed(spread.shape)),
        ],
        [
            (shaped((groups, length, inner), BF16), flat(inner, back)),
            (shaped(gate.shape, BF16), tall(inner, part, back)),
            (shaped(gate.shape, BF16), tall(inner, part, back)),
            (shaped((groups, LANES, inner)), whole(LANES, inner)),
            (shaped((8, inner)), fixed((8, inner))),
        ],
        [],
        1_500_000_000,
        4_500_000,
        {1: gz, 2: mixed},
        after,
    )


def adjoint(xbc, cumul, dt, gy, y, enter, gin, xw, halo, taps, heads, rows, spread, after):
    groups, length, width = xbc.shape
    inner = spread.shape[1]
    chunks = length // CHUNK
    back = lambda i: chunks - 1 - i
    per = CHUNK // RIM
    return run(
        adjoint_kernel,
        (groups, chunks),
        [
            (xbc, flat(width, back)),
            (cumul, flat(LANES, back)),
            (dt, flat(LANES, back)),
            (gy, flat(inner, back)),
            (y, flat(inner, back)),
            (enter, pl.BlockSpec((1, 1, LANES, inner), lambda g, i: (g, back(i), 0, 0))),
            (gin, whole(LANES, inner)),
            (xw, flat(width, back)),
            (
                xw,
                pl.BlockSpec(
                    (1, RIM, width), lambda g, i: (g, jnp.maximum(back(i) * per - 1, 0), 0)
                ),
            ),
            (halo, whole(RIM, width)),
            (xw, flat(LANES, back, width // LANES)),
            (taps, fixed(taps.shape)),
            (heads, fixed(heads.shape)),
            (rows, fixed(rows.shape)),
            (spread, fixed(spread.shape)),
        ],
        [
            (shaped((groups, length, width + LANES), BF16), flat(width + LANES, back)),
            (shaped((groups, 8, width)), whole(8, width)),
            (shaped((8, width)), fixed((8, width))),
            (shaped((8, LANES)), fixed((8, LANES))),
            (shaped((8, inner)), fixed((8, inner))),
        ],
        [
            pltpu.VMEM((LANES, inner), F32),
            pltpu.VMEM((RIM + CHUNK, width), F32),
            pltpu.VMEM((CHUNK + 8, width), F32),
            pltpu.VMEM((CHUNK, CHUNK), F32),
        ],
        8_000_000_000,
        6_000_000,
        None,
        after,
    )


def place_kernel(at_ref, first, first_y, second, second_x, full_ref):
    step = pl.program_id(0)
    for number, ref in enumerate((first, first_y, second, second_x)):

        @pl.when(step // 2 == number)
        def _(ref=ref):
            full_ref[0, 0, 0] = ref[0]


def place_row(number, step, at):
    x, core, y = at[0], at[1], at[2]
    later = number // 2
    side = number % 2
    row = x + jnp.where(later == 0, step, side)
    column = y + jnp.where(later == 0, side, step)
    return row % 2, jnp.where(later == 0, core, 1 - core), column % 2, 0, 0


def place(first, first_y, second, second_x):
    _, rows, columns = first.shape
    at = jnp.stack([lax.axis_index(name) for name in ("x", "core", "y")]).astype(jnp.int32)

    def piece(number):
        return pl.BlockSpec(
            (1, rows, columns), lambda i, at: (jnp.clip(i - 2 * number, 0, 1), 0, 0)
        )

    full = pl.pallas_call(
        place_kernel,
        grid_spec=pltpu.PrefetchScalarGridSpec(
            num_scalar_prefetch=1,
            grid=(8,),
            in_specs=[piece(number) for number in range(4)],
            out_specs=pl.BlockSpec(
                (1, 1, 1, rows, columns), lambda i, at: place_row(i // 2, i % 2, at)
            ),
        ),
        out_shape=shaped((2, 2, 2, rows, columns), first.dtype),
        compiler_params=pltpu.CompilerParams(
            dimension_semantics=("arbitrary",), vmem_limit_bytes=VMEM_BYTES
        ),
        cost_estimate=pl.CostEstimate(
            flops=0, bytes_accessed=32 * rows * columns, transcendentals=0
        ),
    )(at, first, first_y, second, second_x)
    return full.reshape(8 * rows, columns)


def swap(value, axis):
    return lax.ppermute(value, axis, [(0, 1), (1, 0)])


def sum_axis(value, axis):
    if lax.axis_size(axis) == 2:
        return value + swap(value, axis)
    return lax.psum(value, axis)


def cut(value, axis, dim):
    size = value.shape[dim] // 2
    at = lax.axis_index(axis)
    kept = lax.dynamic_slice_in_dim(value, at * size, size, dim)
    return kept, lax.dynamic_slice_in_dim(value, (1 - at) * size, size, dim)


def added(kept, got, dtype=BF16):
    return (kept.astype(F32) + got.astype(F32)).astype(dtype)


def ordered_pair(own, other):
    low = lax.axis_index("zq") == 0
    return jnp.where(low, jnp.concatenate([own, other]), jnp.concatenate([other, own]))


def hold(value, *before):
    return lax.optimization_barrier((value,) + before)[0]


def shift(value, by):
    blocks = lax.axis_size(("y", "zp"))
    pairs = [(i, i + by) for i in range(blocks) if 0 <= i + by < blocks]
    return lax.ppermute(value, ("y", "zp"), pairs)


def coarse(value):
    return lax.reduce_precision(value, 8, 7)


def weight(log, inner):
    heads = inner // (LANES // 2)
    return jnp.repeat(jnp.exp(log[:, :, 0:heads]), LANES // 2, axis=2)


def pack_states(ends, totals):
    groups, _, inner = ends.shape
    high = coarse(totals)
    middle = coarse(totals - high)
    low = coarse(totals - high - middle)
    logs = jnp.concatenate([high, middle, low, jnp.zeros((groups, RIM - 3, LANES), F32)], axis=1)
    logs = jnp.pad(logs, ((0, 0), (0, 0), (0, inner - LANES)))
    return jnp.concatenate([ends, logs], axis=1).astype(BF16)


def within_row(packed, ends, totals, way):
    columns = lax.axis_size("zp")
    groups, states, inner = ends.shape
    entering = jnp.zeros(ends.shape, F32)
    passed = jnp.zeros((groups, 1, LANES), F32)
    for by in range(1, columns):
        pairs = [(i, i + by * way) for i in range(columns) if 0 <= i + by * way < columns]
        got = lax.ppermute(packed, "zp", pairs).astype(F32)
        entering = entering + weight(passed, inner) * got[:, 0:states]
        passed = passed + jnp.sum(got[:, states : states + 3, 0:LANES], axis=1, keepdims=True)
    leaving = (ends + weight(totals, inner) * entering).astype(BF16)
    return entering, passed, leaving


def across_rows(entering, passed, leaving, ends, totals, way):
    rows, columns = lax.axis_size("y"), lax.axis_size("zp")
    inner = ends.shape[2]
    edge = columns - 1 if way == 1 else 0
    total = entering
    for step in range(rows - 1):
        if step > 0:
            leaving = (ends + weight(totals, inner) * total).astype(BF16)
        got = jnp.zeros(ends.shape, F32)
        for to in range(columns):
            pairs = [
                (row * columns + edge, (row + way) * columns + to)
                for row in range(rows)
                if 0 <= row + way < rows
            ]
            got = got + lax.ppermute(leaving, ("y", "zp"), pairs).astype(F32)
        total = entering + weight(passed, inner) * got
    return total


def all_pairs():
    return all(lax.axis_size(name) == 2 for name in ("x", "y", "zp"))


NEAR = [(0, 1), (3, 2), (1, 3), (2, 0)]
FAR = [(1, 2), (2, 1)]
HOME = [(to, source) for source, to in NEAR]


def fetched(piece, near, far):
    at_home = lax.axis_index("core") == lax.axis_index("zp")
    return jnp.where(at_home, piece, near), jnp.where(at_home, near, far)


def fetch(piece):
    return lax.ppermute(piece, ("core", "zp"), NEAR), lax.ppermute(piece, ("core", "zp"), FAR)


def gather_slice(piece):
    owners = lax.axis_size("zp")
    rows = lax.all_gather(piece, ("x", "core", "y"), axis=0, tiled=True)
    parts = lax.all_gather(rows, "zp")
    return lax.dynamic_slice_in_dim(parts, lax.axis_index("core") * (owners // 2), owners // 2, 0)


def reduce_slice(parts):
    owners = lax.axis_size("zp")
    full = jnp.zeros((owners,) + parts.shape[1:], parts.dtype)
    full = lax.dynamic_update_slice_in_dim(
        full, parts, lax.axis_index("core") * (owners // 2), axis=0
    )
    mine = lax.psum_scatter(full, "zp", scatter_dimension=0, tiled=True)[0]
    mine = lax.psum_scatter(mine, ("x", "core", "y"), scatter_dimension=0, tiled=True)
    return mine.astype(F32)


def cut_rows(full):
    rows, columns = full.shape[0] // 8, full.shape[1]
    full = full.reshape(2, 2, 2, rows, columns)
    core = lax.axis_index("core")
    same = cut(lax.dynamic_index_in_dim(full, core, 1, False), "x", 0)
    cross = cut(lax.dynamic_index_in_dim(full, 1 - core, 1, False), "y", 1)
    return same[0][0], cross[0][:, 0], same[1][0], cross[1][:, 0]


def cut_again(same, cross):
    same, cross = cut(same, "y", 0), cut(cross, "x", 0)
    return same[0][0], cross[0][0], same[1][0], cross[1][0]


def home_parts(same, cross):
    at_home = lax.axis_index("core") == lax.axis_index("zp")
    return jnp.where(at_home, cross, same), cross


def at_owner(near, far, same):
    at_home = lax.axis_index("core") == lax.axis_index("zp")
    return near.astype(F32) + jnp.where(at_home, same.astype(F32), far.astype(F32))


def own_of_slice(value):
    owners = lax.axis_size("zp")
    core, part = lax.axis_index("core"), lax.axis_index("zp")
    other = swap(value, "core")
    share = value.shape[-1] // (owners // 2)
    wanted = jnp.where(part // (owners // 2) == core, value, other)
    return lax.dynamic_slice_in_dim(wanted, (part % (owners // 2)) * share, share, value.ndim - 1)


def slice_of_own(value, after):
    owners = lax.axis_size("zp")
    core = lax.axis_index("core")
    if owners == 2:
        other = hold(swap(value, "zp"), after)
        return jnp.where(core == lax.axis_index("zp"), value, other)[None]
    parts = lax.all_gather(value, "zp")
    return lax.dynamic_slice_in_dim(parts, core * (owners // 2), owners // 2, 0)


def per_device(
    hidden,
    cotangent,
    norm_gain,
    w_z,
    w_x,
    w_bc,
    w_dt,
    conv_x,
    conv_x_bias,
    conv_bc,
    conv_bc_bias,
    dt_bias,
    a_log,
    d_skip,
    inner_gain,
    w_out,
):
    micro, own_len, model = hidden.shape
    owners = lax.axis_size("zp")
    share = w_x.shape[1]
    own_heads = w_dt.shape[1]
    inner_full = share * 2 * owners
    states2 = w_bc.shape[1]
    halves = owners // 2
    inner = share * halves
    heads = own_heads * halves
    head_width = inner // heads
    width = inner + states2

    def matmul(left, right, contract, dtype=F32):
        return lax.dot_general(
            left, right, (contract, ((), ())), preferred_element_type=F32
        ).astype(dtype)

    def spliced(parts, sizes):
        if halves == 1:
            return parts[0]
        columns, at = [], 0
        for size, copies in sizes:
            columns += [parts[k][:, at : at + size] for k in range(halves if copies else 1)]
            at += size
        return jnp.concatenate(columns, axis=1)

    parts = range(micro)

    own = hidden.astype(F32)
    gain_in = norm_gain.astype(F32)
    r0 = lax.rsqrt(jnp.mean(own * own, axis=-1, keepdims=True) + EPS)
    filler = LANES // halves - own_heads
    own_first = jnp.concatenate(
        [w_x, w_bc, w_dt, jnp.zeros((w_dt.shape[0], filler), BF16)], axis=1
    )
    own_second = jnp.concatenate([w_z, jnp.transpose(w_out)], axis=1)
    normed_own = (own * r0 * gain_in).astype(BF16)
    fast = all_pairs()
    if fast:
        got = fetch(own_first)
    normed_got = [swap(normed_own[part], "zq") for part in parts]
    if fast:
        same, cross = fetched(own_first, *got)
        first, second = [jnp.stack([same, swap(same, "x")]), jnp.stack([cross, swap(cross, "y")])]
        own_second = hold(own_second, same, cross)
        got = fetch(own_second)
        rest = swap(first, "y"), swap(second, "x")
    near = [ordered_pair(normed_own[0], hold(normed_got[0], *((first, second) if fast else ())))]
    far = [swap(near[0], "core")]
    if fast:
        same, cross = fetched(own_second, *hold(got, near[0]))
        moved = swap(same, "x"), swap(cross, "y")
        w_first = place(first, rest[0], second, rest[1])
        same, cross, *moved = hold((same, cross, *moved), w_first)
        first, second = jnp.stack([same, moved[0]]), jnp.stack([cross, moved[1]])
        got_second = first, swap(first, "y"), second, swap(second, "x")
    else:
        w_first = spliced(
            gather_slice(own_first), ((share, 1), (states2, 0), (own_heads, 1), (filler, 1))
        )
    for part in parts[1:]:
        near.append(ordered_pair(normed_own[part], hold(normed_got[part], near[part - 1])))
        far.append(swap(near[part], "core"))
    normed = jnp.stack([jnp.stack(pair) for pair in zip(near, far)])
    cot_own = hold(cotangent, near[-1])
    cot_got = swap(cot_own, "zq")

    per_head = jnp.concatenate([dt_bias, a_log, d_skip])
    per_head = jnp.pad(per_head, (0, share - 3 * own_heads))
    small = jnp.concatenate([conv_x, conv_x_bias[None], inner_gain[None]], axis=0).astype(F32)
    small = jnp.concatenate([small, per_head[None], jnp.zeros((1, share), F32)])
    small = slice_of_own(small, w_first)
    channel_rows = jnp.concatenate([small[k, 0:6] for k in range(halves)], axis=1)
    head_rows = jnp.concatenate(
        [small[k, 6, 0 : 3 * own_heads].reshape(3, own_heads) for k in range(halves)], axis=1
    )
    conv_shared = jnp.concatenate([conv_bc, conv_bc_bias[None]], axis=0).astype(F32)
    taps = jnp.pad(jnp.concatenate([channel_rows[0:5], conv_shared], axis=1), ((0, 3), (0, 0)))
    head_in = jnp.stack([head_rows[0], -jnp.exp(head_rows[1]), jnp.ones((heads,), F32)])
    head_in = jnp.pad(head_in, ((0, 5), (0, LANES - heads)))
    rows = jnp.stack([jnp.repeat(head_rows[2], head_width), channel_rows[5]])
    rows = jnp.pad(rows, ((0, 6), (0, 0)))
    spread = (
        lax.broadcasted_iota(jnp.int32, (LANES, inner), 1) // head_width
        == lax.broadcasted_iota(jnp.int32, (LANES, inner), 0)
    ).astype(BF16)

    scans = []
    for part in parts:
        xw = matmul(normed[part], w_first, ((2,), (0,)), BF16)
        scans.append((xw, shift(xw[:, -RIM:, 0:width], 1)))
    local, packed = [], []
    for part in parts:
        local.append(local_states(*scans[part], taps, head_in, spread, packed[-1:]))
        packed.append(pack_states(local[part][3], local[part][4][:, 0:1]))
        if part == 0:
            cot_got = hold(cot_got, packed[0])
            cot_near = jnp.stack(
                [ordered_pair(cotangent[k], cot_got[k]) for k in parts]
            )
            cot_far = swap(cot_near, "core")
    if fast:
        got_second = hold(got_second, packed[-1])
        w_second = place(*got_second)
    else:
        w_second = spliced(
            gather_slice(hold(own_second, packed[-1])), ((share, 1), (share, 1))
        )
    w_gate, w_down = w_second[:, 0:inner], w_second[:, inner:]
    gate = matmul(normed, w_gate, ((3,), (0,)), BF16)
    totals = [local[part][4][:, 0:1] for part in parts]
    rowwise = [within_row(packed[part], local[part][3], totals[part], 1) for part in parts]
    w_down, _, cot_far = hold((w_down, cot_near, cot_far), gate, rowwise[0][2])
    cot = jnp.stack([cot_near, cot_far], axis=1)
    gm = matmul(cot, w_down, ((3,), (0,)))
    gained, mixes, stats = None, [], []
    for part in parts:
        xbc, cumul, dt = local[part][0:3]
        start = across_rows(*rowwise[part], local[part][3], totals[part], 1)
        y, gained, enter, stat = mixer(
            part, xbc, cumul, dt, start, gate, gm, rows, spread, gained,
            [r[2] for r in rowwise[part + 1 :]],
        )
        mixes.append((y, enter))
        stat = stat + jnp.flip(swap(stat, "core"), 0)
        stats.append(sum_axis(stat, "zq"))
    branch = matmul(gained, w_down, ((3,), (1,)), BF16)
    gz = mixed = None
    gates, packed = [], []
    for part in parts:
        xbc, cumul = local[part][0:2]
        gy, gz, mixed, back_end, g_gain = gate_back(
            part, inner_full, mixes[part][0], xbc, gate, gm, stats[part], cumul, rows, spread,
            gz, mixed, [branch] + packed[-1:],
        )
        gates.append((gy, back_end, g_gain))
        packed.append(pack_states(back_end, totals[part]))

    tokens = ((0, 1, 2), (0, 1, 2))
    branch = added(branch[:, 0], swap(branch[:, 1], "core"))
    branch_kept, branch_sent = cut(branch, "zq", 1)
    mixed = hold(mixed, *packed)
    g_down = matmul(cot, mixed, tokens, BF16)
    g_gate = matmul(normed, hold(gz, g_down), tokens, BF16)
    rowwise = [within_row(packed[part], gates[part][1], totals[part], -1) for part in parts]
    gz = hold(gz, g_gate, rowwise[0][2])
    g_normed_gate = matmul(gz, w_gate, ((3,), (1,)))
    gins = [across_rows(*rowwise[part], gates[part][1], totals[part], -1) for part in parts]
    wait_for = [branch_sent, g_normed_gate, rowwise[-1][2]]
    if fast:
        second = cut_rows(hold(jnp.concatenate([g_gate, g_down], axis=1), gins[0]))
        moved = swap(second[2], "x"), swap(second[3], "y")
        wait_for += second[2:]
    branch_got = swap(branch_sent, "zq")

    g_first, heads_out, norm_sums = 0.0, [], []
    for part in parts:
        xbc, cumul, dt = local[part][0:3]
        gmix, rim, *sums = adjoint(
            xbc, cumul, dt, gates[part][0], mixes[part][0], mixes[part][1], gins[part],
            *scans[part], taps, head_in, rows, spread, wait_for,
        )
        heads_out.append(sums)
        ahead = shift(rim, -1)
        if fast and part == 0:
            moved = hold(moved, gmix)
            second = cut_again(added(second[0], moved[0]), added(second[1], moved[1]))
            moved = swap(second[2], "y"), swap(second[3], "x")
        if part == micro - 1:
            branch_got = hold(branch_got, gmix)
            branch_own = added(branch_kept, branch_got, F32)
        fix = jnp.stack(
            [sum(taps[k, :] * ahead[:, r - k] for k in range(r + 1)) for r in range(3)], axis=1
        )
        length = gmix.shape[1]
        last = gmix[:, length - RIM :].astype(F32)
        last = last + jnp.pad(fix, ((0, 0), (RIM - 3, 0), (0, LANES)))
        gmix = lax.dynamic_update_slice_in_dim(gmix, last.astype(BF16), length - RIM, 1)

        def for_weights(gmix, g_first):
            return g_first + matmul(normed[part], gmix, ((0, 1), (0, 1)))

        def for_tokens(gmix):
            total = g_normed_gate[part] + matmul(gmix, w_first, ((2,), (1,)))
            return total.astype(BF16)

        if part < micro - 1:
            total = for_tokens(gmix)
            other = swap(total[1], "core")
            g_first = for_weights(hold(gmix, total), g_first)
            total, other, _ = hold((total[0], other), g_first) + (None,)
            norm_sums.append(cut(added(total, other), "zq", 0))
            wait_for = [g_first, norm_sums[-1][1]]
            if fast:
                moved = hold(moved, g_first)
                same, cross = added(second[0], moved[0]), added(second[1], moved[1])
                sent = home_parts(same, cross)
                wait_for += sent
                got = (
                    lax.ppermute(sent[0], ("core", "zp"), HOME),
                    lax.ppermute(sent[1], ("core", "zp"), FAR),
                )
        else:
            g_first = for_weights(gmix, g_first).astype(BF16)
            if fast:
                first = cut_rows(g_first)
                moved_first = swap(first[2], "x"), swap(first[3], "y")
                gmix = hold(gmix, *first[2:])
            total = for_tokens(gmix)
            norm_sums.append(cut(added(total[0], swap(total[1], "core")), "zq", 0))

    if fast:
        g_second = at_owner(*hold(got, g_first), same)
        first = cut_again(added(first[0], moved_first[0]), added(first[1], moved_first[1]))
        moved = swap(first[2], "y"), swap(first[3], "x")
        same, cross = added(first[0], moved[0]), added(first[1], moved[1])
        sent = home_parts(same, cross)
        g_first = at_owner(
            lax.ppermute(sent[0], ("core", "zp"), HOME),
            lax.ppermute(sent[1], ("core", "zp"), FAR),
            same,
        )
    else:
        g_second = reduce_slice(
            jnp.stack(
                [
                    jnp.concatenate(pair, axis=1)
                    for pair in zip(
                        jnp.split(g_gate, halves, axis=1), jnp.split(g_down, halves, axis=1)
                    )
                ]
            )
        )
        g_first = reduce_slice(
            jnp.concatenate(
                [
                    jnp.stack(jnp.split(g_first[:, 0:inner], halves, axis=1)),
                    jnp.concatenate(
                        [
                            g_first[None, :, inner:width],
                            jnp.zeros((halves - 1, model, states2), BF16),
                        ]
                    ),
                    jnp.stack(jnp.split(g_first[:, width : width + heads], halves, axis=1)),
                ],
                axis=2,
            )
        )
    g_bc = g_first[:, share : share + states2]
    g_bc = sum_axis(sum_axis(g_bc, "zp"), "zq")

    own_squares, g_hidden, g_norm_gain = [], [], 0.0
    for part in parts:
        own_squares.append(
            lax.dynamic_slice_in_dim(stats[part][0, 0], lax.axis_index("zq") * own_len, own_len, 0)
        )
        kept, sent = norm_sums[part]
        x, r, g = own[part], r0[part], added(kept, swap(sent, "zq"), F32)
        q0 = g * gain_in
        g_norm_gain = g_norm_gain + jnp.sum(g * x * r, axis=0)
        g_hidden.append(
            cotangent[part].astype(F32) + r * q0
            - x * (r * r * r) * jnp.mean(q0 * x, axis=-1, keepdims=True)
        )
    r1 = lax.rsqrt(jnp.stack(own_squares) / inner_full + EPS)[..., None]
    outputs = (own + r1 * branch_own).astype(BF16)

    g_taps, g_heads, g_skip = (sum(b[k] for b in heads_out) for k in range(3))
    g_gain = sum(g[2] for g in gates)
    skip_heads = jnp.sum(g_skip[0].reshape(heads, head_width), axis=1)
    small = jnp.concatenate(
        [g_taps[0:5, 0:inner].reshape(-1), g_gain[0], g_heads[0, 0:heads], g_heads[1, 0:heads], skip_heads]
    )
    size = small.shape[0]
    packed = jnp.concatenate([small, g_taps[0:5, inner:width].reshape(-1)])
    packed = hold(packed, norm_sums[-1][1])
    for axis in ("x", "y", "zp"):
        packed = sum_axis(packed, axis)
    small = packed[:size]
    bc_rows = sum_axis(sum_axis(packed[size:], "core"), "zq").reshape(5, states2)
    channel = own_of_slice(small[0 : 6 * inner].reshape(6, inner))
    per_head = own_of_slice(small[6 * inner :].reshape(3, heads))
    for axis in ("core", "zq", "x", "y", "zp"):
        g_norm_gain = sum_axis(g_norm_gain, axis)
    return (
        outputs,
        jnp.stack(g_hidden),
        g_norm_gain,
        g_second[:, 0:share],
        g_first[:, 0:share],
        g_bc,
        g_first[:, share + states2 : share + states2 + own_heads],
        channel[0:4],
        channel[4],
        bc_rows[0:4],
        bc_rows[4],
        per_head[0],
        per_head[1],
        per_head[2],
        channel[5],
        jnp.transpose(g_second[:, share : 2 * share]),
    )


def solution(mesh):
    dp, seq, tensor = (mesh.shape[name] for name in ("dp", "seq", "tensor"))
    fine = Mesh(
        mesh.devices.reshape(dp // 2, 2, seq, tensor // 2, 2), ("x", "core", "y", "zp", "zq")
    )
    data, tens = ("x", "core", "y"), ("zp", "zq")
    tokens = P(("x", "core"), ("y", "zp", "zq"), None)
    params = (
        P(),
        P(data, tens),
        P(data, tens),
        P(data, None),
        P(data, tens),
        P(None, tens),
        P(tens),
        P(),
        P(),
        P(tens),
        P(tens),
        P(tens),
        P(tens),
        P(tens, data),
    )
    return jax.shard_map(
        per_device,
        mesh=fine,
        in_specs=(tokens, tokens) + params,
        out_specs=(tokens, tokens) + params,
        check_vma=False,
    )
```

```python
import functools

import jax
import jax.numpy as jnp
from jax import lax
from jax.experimental import pallas as pl
from jax.experimental.pallas import tpu as pltpu
from jax.sharding import Mesh
from jax.sharding import PartitionSpec as P

CHUNK = 256
HALF = CHUNK // 2
LANES = 128
STRIP = 256
ROWS = 64
RIM = 16
EPS = 1e-05
F32 = jnp.float32
BF16 = jnp.bfloat16
VMEM_BYTES = 48 * 1024 * 1024


def dot(left, right):
    return lax.dot_general(left, right, (((1,), (0,)), ((), ())), preferred_element_type=F32)


def dot_nt(left, right):
    return lax.dot_general(left, right, (((1,), (1,)), ((), ())), preferred_element_type=F32)


def pieces(value, count):
    terms = []
    for _ in range(count):
        term = value.astype(BF16)
        terms.append(term)
        value = value - term.astype(F32)
    return terms


def doubled(value):
    return jnp.concatenate(pieces(value, 2), axis=1)


def spread_heads(pair, spread):
    return dot(pair, spread)


def gather_heads(value, spread, count=2):
    return sum(dot_nt(term, spread[0:LANES, :]) for term in pieces(value, count))


def running_sum(value, mask):
    return sum(dot(mask, term) for term in pieces(value, 3))


def iota2(rows, cols, dim):
    return lax.broadcasted_iota(jnp.int32, (rows, cols), dim)


def turned(value):
    return jnp.transpose(value.astype(F32)).astype(BF16)


def strips(width):
    return [slice(at, at + STRIP) for at in range(0, width, STRIP)]


def row_blocks():
    return [slice(at, at + ROWS) for at in range(0, CHUNK, ROWS)]


def conv_pre(ext, taps, rows, cols):
    total = taps[4:5, cols] + taps[0:1, cols] * ext[pl.ds(RIM - 3 + rows.start, ROWS), cols]
    for k in range(1, 4):
        total = total + taps[k : k + 1, cols] * ext[pl.ds(RIM - 3 + k + rows.start, ROWS), cols]
    return total


def softplus(value):
    return jnp.maximum(value, 0.0) + jnp.log1p(jnp.exp(-jnp.abs(value)))


def write_packed(packed_ref, end, total):
    packed_ref[0, 0:LANES, :] = end.astype(BF16)
    packed_ref[0, LANES:, :] = jnp.zeros((RIM, end.shape[1]), BF16)
    row = iota2(RIM, LANES, 0)
    logs = jnp.zeros((RIM, LANES), F32)
    for k, term in enumerate(pieces(total, 3)):
        logs = jnp.where(row == k, term.astype(F32), logs)
    packed_ref[0, LANES:, 0:LANES] = logs.astype(BF16)


def widened(log, spread):
    return spread_heads(doubled(jnp.broadcast_to(jnp.exp(log), (8, LANES))), spread)[0:1, :]


def entering_state(packed_ref, first_ref, second_ref, spread_ref):
    passed = jnp.sum(packed_ref[0, LANES:, 0:LANES].astype(F32), axis=0, keepdims=True)
    from_row = first_ref[0].astype(F32) + second_ref[0].astype(F32)
    return packed_ref[0, 0:LANES, :].astype(F32) + widened(passed, spread_ref[...]) * from_row


def leave_kernel(end_ref, total_ref, packed_ref, spread_ref, leaving_ref):
    kept = packed_ref[0, 0:LANES, :].astype(F32) * widened(total_ref[0, 0:1, :], spread_ref[...])
    leaving_ref[0] = (end_ref[0] + kept).astype(BF16)


def state_kernel(
    mix_ref, halo_ref, step_ref, taps_ref, heads_ref, spread_ref,
    xbc_ref, sum_ref, dt_ref, end_ref, total_ref, packed_ref, ext, weighted,
):
    inner = spread_ref.shape[1]
    place = pl.program_id(1)

    @pl.when(place == 0)
    def _():
        ext[0:RIM, :] = halo_ref[0].astype(F32)
        end_ref[...] = jnp.zeros_like(end_ref)
        total_ref[...] = jnp.zeros_like(total_ref)

    @pl.when(place > 0)
    def _():
        ext[0:RIM, :] = ext[CHUNK : CHUNK + RIM, :]

    dt = softplus(step_ref[0].astype(F32) + heads_ref[0:1, :])
    lower = (iota2(CHUNK, CHUNK, 0) >= iota2(CHUNK, CHUNK, 1)).astype(F32).astype(BF16)
    cumul = running_sum(dt * heads_ref[1:2, :], lower)
    sum_ref[0] = cumul
    dt_ref[0] = dt
    last = cumul[CHUNK - 1 : CHUNK, :]
    total_ref[0] += jnp.broadcast_to(last, total_ref.shape[1:])
    tail = doubled(jnp.exp(last - cumul) * dt)
    decay = doubled(jnp.broadcast_to(jnp.exp(last), (8, LANES)))
    b_turned = None
    for cols in reversed(strips(xbc_ref.shape[2])):
        held = spread_ref[:, cols] if cols.start < inner else None
        for rows in row_blocks():
            ext[RIM + rows.start : RIM + rows.stop, cols] = mix_ref[0, rows, cols].astype(F32)
            pre = conv_pre(ext, taps_ref, rows, cols)
            act = (pre * jax.nn.sigmoid(pre)).astype(BF16)
            xbc_ref[0, rows, cols] = act
            if held is not None:
                weighted[rows, :] = (act.astype(F32) * spread_heads(tail[rows], held)).astype(BF16)
        if held is None:
            b_turned = turned(xbc_ref[0, :, inner : inner + LANES])
        else:
            kept = end_ref[0, :, cols] * spread_heads(decay, held)[0:1, :]
            end_ref[0, :, cols] = kept + dot(b_turned, weighted[...])

    @pl.when(place == pl.num_programs(1) - 1)
    def _():
        write_packed(packed_ref, end_ref[0], total_ref[0, 0:1, :])


def scan_kernel(
    xbc_ref, sum_ref, dt_ref, packed_ref, first_ref, second_ref, gate_ref, gm_ref, rows_ref, spread_ref,
    y_ref, mixed_ref, enter_ref, stat_ref, state, stepped, weighted,
):
    inner = spread_ref.shape[1]

    @pl.when(pl.program_id(1) == 0)
    def _():
        state[...] = entering_state(packed_ref, first_ref, second_ref, spread_ref)

    cumul = sum_ref[0]
    dt = dt_ref[0]
    across = jnp.transpose(cumul)
    last = cumul[CHUNK - 1 : CHUNK, :]
    tail = doubled(jnp.exp(last - cumul) * dt)
    reach = doubled(jnp.exp(cumul))
    decay = doubled(jnp.broadcast_to(jnp.exp(last), (8, LANES)))
    dt = doubled(dt)
    b_low = xbc_ref[0, :, inner : inner + LANES]
    c_low = xbc_ref[0, :, inner + LANES :]
    b_turned = turned(b_low)
    score = dot_nt(c_low, b_low)
    causal = iota2(HALF, HALF, 0) >= iota2(HALF, HALF, 1)
    first = iota2(1, LANES, 1) < LANES // 2
    squares = [jnp.zeros((ROWS, STRIP), F32) for _ in row_blocks()]
    crossed = [jnp.zeros((ROWS, STRIP), F32) for _ in row_blocks()]
    for cols in strips(inner):
        held = spread_ref[:, cols]
        entering = state[:, cols].astype(BF16)
        enter_ref[0, 0, :, cols] = entering
        for rows in row_blocks():
            x = xbc_ref[0, rows, cols].astype(F32)
            stepped[rows, :] = x * spread_heads(dt[rows], held)
            weighted[rows, :] = (x * spread_heads(tail[rows], held)).astype(BF16)
            y_ref[0, rows, cols] = dot(c_low[rows], entering) * spread_heads(reach[rows], held)
        kept = state[:, cols] * spread_heads(decay, held)[0:1, :]
        state[:, cols] = kept + dot(b_turned, weighted[...])
        for pair in range(STRIP // LANES):
            lanes = slice(pair * LANES, (pair + 1) * LANES)
            into = slice(cols.start + pair * LANES, cols.start + (pair + 1) * LANES)
            top = y_ref[0, 0:HALF, into]
            bottom = y_ref[0, HALF:, into]
            u = stepped[:, lanes]
            for side in range(2):
                head = (cols.start + pair * LANES) // (LANES // 2) + side
                mine = jnp.where(first if side == 0 else ~first, u, 0.0).astype(BF16)
                column = cumul[:, head : head + 1]
                row = across[head : head + 1, :]
                corner = jnp.where(causal, jnp.exp(column[0:HALF] - row[:, 0:HALF]), 0.0)
                top = top + dot((score[0:HALF, 0:HALF] * corner).astype(BF16), mine[0:HALF])
                left = jnp.exp(column[HALF:] - row[:, 0:HALF])
                right = jnp.where(causal, jnp.exp(column[HALF:] - row[:, HALF:]), 0.0)
                below = jnp.concatenate([left, right], axis=1)
                bottom = bottom + dot((score[HALF:, :] * below).astype(BF16), mine)
            y_ref[0, 0:HALF, into] = top
            y_ref[0, HALF:, into] = bottom
        for k, rows in enumerate(row_blocks()):
            y = y_ref[0, rows, cols] + rows_ref[0:1, cols] * xbc_ref[0, rows, cols].astype(F32)
            gate = gate_ref[0, rows, cols].astype(F32)
            gated = y * gate * jax.nn.sigmoid(gate)
            gained = gated * rows_ref[1:2, cols]
            mixed_ref[0, rows, cols] = gained.astype(BF16)
            squares[k] = squares[k] + gated * gated
            crossed[k] = crossed[k] + gained * gm_ref[0, rows, cols]
    squares = jnp.concatenate(squares, axis=0)
    crossed = jnp.concatenate(crossed, axis=0)
    ones = jnp.ones((8, STRIP), BF16)
    square_row = sum(dot_nt(ones, term) for term in pieces(squares, 3))
    cross_row = sum(dot_nt(ones, term) for term in pieces(crossed, 3))
    stat_ref[0] = jnp.where(iota2(8, CHUNK, 0) == 0, square_row, cross_row)


def gate_kernel(
    inner_full, y_ref, xbc_ref, gate_ref, gm_ref, stat_ref, sum_ref, total_ref, rows_ref, spread_ref,
    gy_ref, gz_ref, mixed_ref, back_ref, gain_ref, packed_ref, reached,
):
    inner = spread_ref.shape[1]

    @pl.when(pl.program_id(1) == 0)
    def _():
        back_ref[...] = jnp.zeros_like(back_ref)

    @pl.when((pl.program_id(0) == 0) & (pl.program_id(1) == 0))
    def _():
        gain_ref[...] = jnp.zeros_like(gain_ref)

    stats = jnp.transpose(stat_ref[0])
    scale = lax.rsqrt(stats[:, 0:1] / inner_full + EPS)
    bent = scale * scale * scale * (stats[:, 1:2] / inner_full)
    cumul = sum_ref[0]
    reach = doubled(jnp.exp(cumul))
    decay = doubled(jnp.broadcast_to(jnp.exp(cumul[CHUNK - 1 : CHUNK, :]), (8, LANES)))
    c_turned = turned(xbc_ref[0, :, inner + LANES :])
    for cols in strips(inner):
        held = spread_ref[:, cols]
        gain = rows_ref[1:2, cols]
        gain_sum = jnp.zeros((1, STRIP), F32)
        for rows in row_blocks():
            x = xbc_ref[0, rows, cols].astype(F32)
            y = y_ref[0, rows, cols] + rows_ref[0:1, cols] * x
            gate = gate_ref[0, rows, cols].astype(F32)
            sigmoid = jax.nn.sigmoid(gate)
            silu = gate * sigmoid
            gated = y * silu
            scaled = gated * scale[rows]
            gm = gm_ref[0, rows, cols]
            gg = scale[rows] * gm * gain - gated * bent[rows]
            gy = (gg * silu).astype(BF16)
            gy_ref[0, rows, cols] = gy
            gz_ref[0, rows, cols] = (gg * y * sigmoid * (1.0 + gate * (1.0 - sigmoid))).astype(BF16)
            mixed_ref[0, rows, cols] = (scaled * gain).astype(BF16)
            gain_sum = gain_sum + jnp.sum(gm * scaled, axis=0, keepdims=True)
            reached[rows, :] = (gy.astype(F32) * spread_heads(reach[rows], held)).astype(BF16)
        gain_ref[:, cols] += jnp.broadcast_to(gain_sum, (8, STRIP))
        kept = back_ref[0, :, cols] * spread_heads(decay, held)[0:1, :]
        back_ref[0, :, cols] = kept + dot(c_turned, reached[...])

    @pl.when(pl.program_id(1) == pl.num_programs(1) - 1)
    def _():
        write_packed(packed_ref, back_ref[0], total_ref[0, 0:1, :])


def adjoint_kernel(
    xbc_ref, sum_ref, dt_ref, gy_ref, y_ref, enter_ref, packed_ref, first_ref, second_ref, mix_ref, before_ref, halo_ref,
    step_ref, taps_ref, heads_ref, rows_ref, spread_ref,
    gmix_ref, rim_ref, gtaps_ref, gheads_ref, gskip_ref, back, ext, gpre, pulled,
):
    inner = spread_ref.shape[1]
    chunks = pl.num_programs(1)
    order = pl.program_id(1)

    @pl.when((pl.program_id(0) == 0) & (order == 0))
    def _():
        gtaps_ref[...] = jnp.zeros_like(gtaps_ref)
        gheads_ref[...] = jnp.zeros_like(gheads_ref)
        gskip_ref[...] = jnp.zeros_like(gskip_ref)

    @pl.when(order == 0)
    def _():
        back[...] = entering_state(packed_ref, first_ref, second_ref, spread_ref)
        gpre[CHUNK:, :] = jnp.zeros((8, gpre.shape[1]), F32)

    @pl.when(order > 0)
    def _():
        gpre[CHUNK:, :] = gpre[0:8, :]

    @pl.when(order == chunks - 1)
    def _():
        ext[0:RIM, :] = halo_ref[0].astype(F32)

    @pl.when(order < chunks - 1)
    def _():
        ext[0:RIM, :] = before_ref[0].astype(F32)

    cumul = sum_ref[0]
    dt = dt_ref[0]
    across = jnp.transpose(cumul)
    last = cumul[CHUNK - 1 : CHUNK, :]
    fade_pair = doubled(jnp.exp(last - cumul))
    reach_pair = doubled(jnp.exp(cumul))
    dt_pair = doubled(dt)
    decay = jnp.broadcast_to(jnp.exp(last), (8, LANES))
    decay_pair = doubled(decay)
    b_low = xbc_ref[0, :, inner : inner + LANES]
    c_low = xbc_ref[0, :, inner + LANES :]
    c_turned = turned(c_low)
    score = dot_nt(b_low, c_low)
    causal = iota2(HALF, HALF, 0) <= iota2(HALF, HALF, 1)
    first = iota2(1, LANES, 1) < LANES // 2
    pulled[...] = jnp.zeros_like(pulled)
    gb = jnp.zeros((CHUNK, LANES), F32)
    gc = jnp.zeros((CHUNK, LANES), F32)
    between = jnp.zeros((CHUNK, LANES), F32)
    arrived = jnp.zeros((CHUNK, LANES), F32)
    direct = jnp.zeros((CHUNK, LANES), F32)
    joined = jnp.zeros((8, LANES), F32)

    def conv_part(cols, gact):
        sums = [jnp.zeros((1, STRIP), F32) for _ in range(5)]
        for rows in row_blocks():
            ext[RIM + rows.start : RIM + rows.stop, cols] = mix_ref[0, rows, cols].astype(F32)
        for rows in reversed(row_blocks()):
            pre = conv_pre(ext, taps_ref, rows, cols)
            sigmoid = jax.nn.sigmoid(pre)
            gp = gact[rows].astype(BF16).astype(F32) * sigmoid * (1.0 + pre * (1.0 - sigmoid))
            gpre[rows, cols] = gp
            total = taps_ref[3:4, cols] * gp
            for k in range(3):
                total = total + taps_ref[k : k + 1, cols] * gpre[pl.ds(3 - k + rows.start, ROWS), cols]
            for k in range(4):
                moved = ext[pl.ds(RIM - 3 + k + rows.start, ROWS), cols]
                sums[k] = sums[k] + jnp.sum(gp * moved, axis=0, keepdims=True)
            sums[4] = sums[4] + jnp.sum(gp, axis=0, keepdims=True)
            gmix_ref[0, rows, cols] = total.astype(BF16)
        rim_ref[0, :, cols] = gpre[0:8, cols]
        for k in range(5):
            gtaps_ref[k : k + 1, cols] += sums[k]

    for cols in strips(inner):
        held = spread_ref[:, cols]
        x = xbc_ref[0, :, cols].astype(F32)
        dt_wide = spread_heads(dt_pair, held)
        fade_wide = spread_heads(fade_pair, held)
        u = x * dt_wide
        u_low = u.astype(BF16)
        weighted = (u * fade_wide).astype(BF16)
        gy_low = gy_ref[0, :, cols]
        gy = gy_low.astype(F32)
        reached = (gy * spread_heads(reach_pair, held)).astype(BF16)
        later = back[:, cols]
        later_low = later.astype(BF16)
        entered = enter_ref[0, 0, :, cols]
        gb = gb + dot_nt(weighted, later_low)
        gc = gc + dot_nt(reached, entered)
        gu_carried = dot(b_low, later_low) * fade_wide
        sums = jnp.sum(later * entered.astype(F32), axis=0, keepdims=True)
        joined = joined + gather_heads(jnp.broadcast_to(sums, (8, STRIP)), held)
        back[:, cols] = later * spread_heads(decay_pair, held)[0:1, :] + dot(c_turned, reached)
        parts = []
        for pair in range(STRIP // LANES):
            lanes = slice(pair * LANES, (pair + 1) * LANES)
            top = gu_carried[0:HALF, lanes]
            bottom = gu_carried[HALF:, lanes]
            gy_pair = gy_low[:, lanes]
            for side in range(2):
                head = (cols.start + pair * LANES) // (LANES // 2) + side
                keep = first if side == 0 else ~first
                gy_mine = jnp.where(keep, gy[:, lanes], 0.0).astype(BF16)
                u_mine = jnp.where(keep, u[:, lanes], 0.0).astype(BF16)
                column = cumul[:, head : head + 1]
                row = across[head : head + 1, :]
                corner = jnp.where(causal, jnp.exp(row[:, 0:HALF] - column[0:HALF]), 0.0)
                side_right = jnp.exp(row[:, HALF:] - column[0:HALF])
                low_right = jnp.where(causal, jnp.exp(row[:, HALF:] - column[HALF:]), 0.0)
                above = jnp.concatenate([corner, side_right], axis=1)
                top = top + dot((score[0:HALF, :] * above).astype(BF16), gy_mine)
                bottom = bottom + dot((score[HALF:, HALF:] * low_right).astype(BF16), gy_mine[HALF:])
                pulled[0:HALF, :] += dot_nt(u_mine[0:HALF], gy_pair) * above
                pulled[HALF:, HALF:] += dot_nt(u_mine[HALF:], gy_pair[HALF:]) * low_right
            parts.append(jnp.concatenate([top, bottom], axis=0))
        gu = jnp.concatenate(parts, axis=1)
        u_kept = u_low.astype(F32)
        between = between + gather_heads(gy * y_ref[0, :, cols] - u_kept * gu, held)
        arrived = arrived + gather_heads(u_kept * gu_carried, held)
        direct = direct + gather_heads(x * gu, held)
        gskip_ref[:, cols] += jnp.broadcast_to(jnp.sum(gy * x, axis=0, keepdims=True), (8, STRIP))
        conv_part(cols, dt_wide * gu + rows_ref[0:1, cols] * gy)

    pulled_low = pulled[...].astype(BF16)
    gb = gb + dot(pulled_low, c_low)
    gc = gc + dot(jnp.transpose(pulled[...]).astype(BF16), b_low)
    conv_part(slice(inner, inner + 2 * LANES), jnp.concatenate([gb, gc], axis=1))

    upper = (iota2(CHUNK, CHUNK, 0) <= iota2(CHUNK, CHUNK, 1)).astype(F32).astype(BF16)
    whole = jnp.sum(arrived, axis=0, keepdims=True) + decay[0:1, :] * joined[0:1, :]
    glg = running_sum(between, upper) + whole
    rate = heads_ref[1:2, :]
    gdt = direct + rate * glg
    raw = step_ref[0].astype(F32) + heads_ref[0:1, :]
    gsi = gdt * jax.nn.sigmoid(raw) * heads_ref[2:3, :]
    gmix_ref[0, :, inner + 2 * LANES :] = gsi.astype(BF16)
    gheads_ref[0:1, :] += jnp.sum(gsi, axis=0, keepdims=True)
    gheads_ref[1:2, :] += jnp.sum(glg * dt * rate, axis=0, keepdims=True)


def flat(width, order=lambda i: i, column=0):
    return pl.BlockSpec((1, CHUNK, width), lambda g, i: (g, order(i), column))


def whole(*shape):
    return pl.BlockSpec((1,) + shape, lambda g, i: (g,) + (0,) * len(shape))


def fixed(shape):
    return pl.BlockSpec(shape, lambda g, i: (0,) * len(shape))


def shaped(shape, dtype=F32):
    return jax.ShapeDtypeStruct(shape, dtype)


def run(kernel, grid, ins, outs, scratch, flops, moved, after=()):
    count = len(ins)
    extra = list(after)

    def body(*refs):
        kernel(*refs[:count], *refs[count + len(extra) :])

    steps = grid[0] * grid[1]
    return pl.pallas_call(
        body,
        grid=grid,
        in_specs=[spec for _, spec in ins] + [pl.BlockSpec(memory_space=pl.ANY)] * len(extra),
        out_specs=[spec for _, spec in outs],
        out_shape=[shape for shape, _ in outs],
        scratch_shapes=scratch,
        compiler_params=pltpu.CompilerParams(
            dimension_semantics=("arbitrary", "arbitrary"), vmem_limit_bytes=VMEM_BYTES
        ),
        cost_estimate=pl.CostEstimate(
            flops=steps * flops, bytes_accessed=steps * moved, transcendentals=0
        ),
    )(*[array for array, _ in ins], *extra)


def local_states(xw, halo, taps, heads, spread, after):
    groups, length, _ = xw.shape
    inner = spread.shape[1]
    width = inner + 2 * LANES
    return run(
        state_kernel,
        (groups, length // CHUNK),
        [
            (xw, flat(width)),
            (halo, whole(RIM, width)),
            (xw, flat(LANES, column=width // LANES)),
            (taps, fixed(taps.shape)),
            (heads, fixed(heads.shape)),
            (spread, fixed(spread.shape)),
        ],
        [
            (shaped((groups, length, width), BF16), flat(width)),
            (shaped((groups, length, LANES)), flat(LANES)),
            (shaped((groups, length, LANES)), flat(LANES)),
            (shaped((groups, LANES, inner)), whole(LANES, inner)),
            (shaped((groups, 8, LANES)), whole(8, LANES)),
            (shaped((groups, LANES + RIM, inner), BF16), whole(LANES + RIM, inner)),
        ],
        [pltpu.VMEM((RIM + CHUNK, width), F32), pltpu.VMEM((CHUNK, STRIP), BF16)],
        1_500_000_000,
        2_000_000,
        after,
    )


def mixer(xbc, cumul, dt, start, gate, gm, rows, spread, after):
    groups, length, width = xbc.shape
    inner = spread.shape[1]
    chunks = length // CHUNK
    return run(
        scan_kernel,
        (groups, chunks),
        [
            (xbc, flat(width)),
            (cumul, flat(LANES)),
            (dt, flat(LANES)),
            (start[0], whole(LANES + RIM, inner)),
            (start[1], whole(LANES, inner)),
            (start[2], whole(LANES, inner)),
            (gate, flat(inner)),
            (gm, flat(inner)),
            (rows, fixed(rows.shape)),
            (spread, fixed(spread.shape)),
        ],
        [
            (shaped((groups, length, inner)), flat(inner)),
            (shaped(gate.shape, BF16), flat(inner)),
            (
                shaped((groups, chunks, LANES, inner), BF16),
                pl.BlockSpec((1, 1, LANES, inner), lambda g, i: (g, i, 0, 0)),
            ),
            (shaped((groups, 8, length)), pl.BlockSpec((1, 8, CHUNK), lambda g, i: (g, 0, i))),
        ],
        [
            pltpu.VMEM((LANES, inner), F32),
            pltpu.VMEM((CHUNK, STRIP), F32),
            pltpu.VMEM((CHUNK, STRIP), BF16),
        ],
        2_500_000_000,
        4_000_000,
        after,
    )


def gate_back(inner_full, y, xbc, gate, gm, stats, cumul, total, rows, spread, after):
    groups, length, width = xbc.shape
    inner = spread.shape[1]
    chunks = length // CHUNK
    back = lambda i: chunks - 1 - i
    return run(
        functools.partial(gate_kernel, float(inner_full)),
        (groups, chunks),
        [
            (y, flat(inner, back)),
            (xbc, flat(width, back)),
            (gate, flat(inner, back)),
            (gm, flat(inner, back)),
            (stats, pl.BlockSpec((1, 8, CHUNK), lambda g, i: (g, 0, back(i)))),
            (cumul, flat(LANES, back)),
            (total, whole(8, LANES)),
            (rows, fixed(rows.shape)),
            (spread, fixed(spread.shape)),
        ],
        [
            (shaped((groups, length, inner), BF16), flat(inner, back)),
            (shaped(gate.shape, BF16), flat(inner, back)),
            (shaped(gate.shape, BF16), flat(inner, back)),
            (shaped((groups, LANES, inner)), whole(LANES, inner)),
            (shaped((8, inner)), fixed((8, inner))),
            (shaped((groups, LANES + RIM, inner), BF16), whole(LANES + RIM, inner)),
        ],
        [pltpu.VMEM((CHUNK, STRIP), BF16)],
        1_500_000_000,
        4_500_000,
        after,
    )


def adjoint(xbc, cumul, dt, gy, y, enter, gin, xw, halo, taps, heads, rows, spread, after):
    groups, length, width = xbc.shape
    inner = spread.shape[1]
    chunks = length // CHUNK
    back = lambda i: chunks - 1 - i
    per = CHUNK // RIM
    return run(
        adjoint_kernel,
        (groups, chunks),
        [
            (xbc, flat(width, back)),
            (cumul, flat(LANES, back)),
            (dt, flat(LANES, back)),
            (gy, flat(inner, back)),
            (y, flat(inner, back)),
            (enter, pl.BlockSpec((1, 1, LANES, inner), lambda g, i: (g, back(i), 0, 0))),
            (gin[0], whole(LANES + RIM, inner)),
            (gin[1], whole(LANES, inner)),
            (gin[2], whole(LANES, inner)),
            (xw, flat(width, back)),
            (
                xw,
                pl.BlockSpec(
                    (1, RIM, width), lambda g, i: (g, jnp.maximum(back(i) * per - 1, 0), 0)
                ),
            ),
            (halo, whole(RIM, width)),
            (xw, flat(LANES, back, width // LANES)),
            (taps, fixed(taps.shape)),
            (heads, fixed(heads.shape)),
            (rows, fixed(rows.shape)),
            (spread, fixed(spread.shape)),
        ],
        [
            (shaped((groups, length, width + LANES), BF16), flat(width + LANES, back)),
            (shaped((groups, 8, width)), whole(8, width)),
            (shaped((8, width)), fixed((8, width))),
            (shaped((8, LANES)), fixed((8, LANES))),
            (shaped((8, inner)), fixed((8, inner))),
        ],
        [
            pltpu.VMEM((LANES, inner), F32),
            pltpu.VMEM((RIM + CHUNK, width), F32),
            pltpu.VMEM((CHUNK + 8, width), F32),
            pltpu.VMEM((CHUNK, CHUNK), F32),
        ],
        8_000_000_000,
        6_000_000,
        after,
    )


def leave(ends, totals, packed, spread):
    groups, states, inner = ends.shape

    def one(*shape):
        return pl.BlockSpec((1,) + shape, lambda g: (g,) + (0,) * len(shape))

    return pl.pallas_call(
        leave_kernel,
        grid=(groups,),
        in_specs=[
            one(states, inner), one(8, LANES), one(states + RIM, inner),
            pl.BlockSpec(spread.shape, lambda g: (0, 0)),
        ],
        out_specs=one(states, inner),
        out_shape=shaped(ends.shape, BF16),
        compiler_params=pltpu.CompilerParams(
            dimension_semantics=("arbitrary",), vmem_limit_bytes=VMEM_BYTES
        ),
        cost_estimate=pl.CostEstimate(
            flops=0, bytes_accessed=8 * groups * states * inner, transcendentals=0
        ),
    )(ends, totals, packed, spread)


def place_kernel(at_ref, first, first_y, second, second_x, full_ref):
    step = pl.program_id(0)
    for number, ref in enumerate((first, first_y, second, second_x)):

        @pl.when(step // 2 == number)
        def _(ref=ref):
            full_ref[0, 0, 0] = ref[0]


def place_row(number, step, at):
    x, core, y = at[0], at[1], at[2]
    later = number // 2
    side = number % 2
    row = x + jnp.where(later == 0, step, side)
    column = y + jnp.where(later == 0, side, step)
    return row % 2, jnp.where(later == 0, core, 1 - core), column % 2, 0, 0


def place(first, first_y, second, second_x):
    _, rows, columns = first.shape
    at = jnp.stack([lax.axis_index(name) for name in ("x", "core", "y")]).astype(jnp.int32)

    def piece(number):
        return pl.BlockSpec(
            (1, rows, columns), lambda i, at: (jnp.clip(i - 2 * number, 0, 1), 0, 0)
        )

    full = pl.pallas_call(
        place_kernel,
        grid_spec=pltpu.PrefetchScalarGridSpec(
            num_scalar_prefetch=1,
            grid=(8,),
            in_specs=[piece(number) for number in range(4)],
            out_specs=pl.BlockSpec(
                (1, 1, 1, rows, columns), lambda i, at: place_row(i // 2, i % 2, at)
            ),
        ),
        out_shape=shaped((2, 2, 2, rows, columns), first.dtype),
        compiler_params=pltpu.CompilerParams(
            dimension_semantics=("arbitrary",), vmem_limit_bytes=VMEM_BYTES
        ),
        cost_estimate=pl.CostEstimate(
            flops=0, bytes_accessed=rows * columns, transcendentals=0
        ),
    )(at, first, first_y, second, second_x)
    return full.reshape(8 * rows, columns)


def join_kernel(at_ref, own, got, far_own, far_got, full_ref):
    half_is_own = pl.program_id(1) == at_ref[0]
    for core, (mine, other) in enumerate(((own, got), (far_own, far_got))):
        for ref, wanted in ((mine, half_is_own), (other, ~half_is_own)):

            @pl.when(wanted & (pl.program_id(0) == core))
            def _(ref=ref):
                full_ref[0] = ref[...]


def joined(own, got, far_own, far_got, part=0):
    _, rows, columns = own.shape
    at = lax.axis_index("zq").astype(jnp.int32)[None]
    piece = pl.BlockSpec((None, rows, columns), lambda c, h, at: (part, 0, 0))
    return pl.pallas_call(
        join_kernel,
        grid_spec=pltpu.PrefetchScalarGridSpec(
            num_scalar_prefetch=1,
            grid=(2, 2),
            in_specs=[piece] * 4,
            out_specs=pl.BlockSpec((1, rows, columns), lambda c, h, at: (c, h, 0)),
        ),
        out_shape=shaped((2, 2 * rows, columns), own.dtype),
        compiler_params=pltpu.CompilerParams(
            dimension_semantics=("arbitrary", "arbitrary"), vmem_limit_bytes=VMEM_BYTES
        ),
        cost_estimate=pl.CostEstimate(
            flops=0, bytes_accessed=16 * rows * columns, transcendentals=0
        ),
    )(at, own, got, far_own, far_got)


def swap(value, axis):
    return lax.ppermute(value, axis, [(0, 1), (1, 0)])


def sum_axis(value, axis):
    if lax.axis_size(axis) == 2:
        return value + swap(value, axis)
    return lax.psum(value, axis)


def cut(value, axis, dim):
    size = value.shape[dim] // 2
    at = lax.axis_index(axis)
    kept = lax.dynamic_slice_in_dim(value, at * size, size, dim)
    return kept, lax.dynamic_slice_in_dim(value, (1 - at) * size, size, dim)


def added(kept, got, dtype=BF16):
    return (kept.astype(F32) + got.astype(F32)).astype(dtype)


def hold(value, *before):
    return lax.optimization_barrier((value,) + before)[0]


def shift(value, by):
    blocks = lax.axis_size(("y", "zp"))
    pairs = [(i, i + by) for i in range(blocks) if 0 <= i + by < blocks]
    return lax.ppermute(value, ("y", "zp"), pairs)


def row_hop(packed, way, *before):
    return hold(lax.ppermute(packed, "zp", [(0, 1)] if way == 1 else [(1, 0)]), *before)


def column_hops(leaving, way, *before):
    source = 1 if way == 1 else 2
    pairs = [[(source, source + way * (1 + to))] for to in range(2)]
    return [hold(lax.ppermute(leaving, ("y", "zp"), pair), *before) for pair in pairs]


def chained(packed, way):
    blocks = lax.axis_size(("y", "zp"))
    groups, _, inner = packed.shape
    heads = inner // (LANES // 2)
    entering = jnp.zeros((groups, LANES, inner), F32)
    passed = jnp.zeros((groups, 1, LANES), F32)
    for by in range(1, blocks):
        got = shift(packed, by * way).astype(F32)
        weight = jnp.repeat(jnp.exp(passed[:, :, 0:heads]), LANES // 2, axis=2)
        entering = entering + weight * got[:, 0:LANES]
        passed = passed + jnp.sum(got[:, LANES:, 0:LANES], axis=1, keepdims=True)
    none = jnp.zeros(entering.shape, BF16)
    return jnp.pad(entering.astype(BF16), ((0, 0), (0, RIM), (0, 0))), none, none


def all_pairs():
    return all(lax.axis_size(name) == 2 for name in ("x", "y", "zp"))


NEAR = [(0, 1), (3, 2), (1, 3), (2, 0)]
FAR = [(1, 2), (2, 1)]
HOME = [(to, source) for source, to in NEAR]


def fetched(piece, near, far):
    at_home = lax.axis_index("core") == lax.axis_index("zp")
    return jnp.where(at_home, piece, near), jnp.where(at_home, near, far)


def fetch(piece):
    return lax.ppermute(piece, ("core", "zp"), NEAR), lax.ppermute(piece, ("core", "zp"), FAR)


def gather_slice(piece):
    owners = lax.axis_size("zp")
    rows = lax.all_gather(piece, ("x", "core", "y"), axis=0, tiled=True)
    parts = lax.all_gather(rows, "zp")
    return lax.dynamic_slice_in_dim(parts, lax.axis_index("core") * (owners // 2), owners // 2, 0)


def reduce_slice(parts):
    owners = lax.axis_size("zp")
    full = jnp.zeros((owners,) + parts.shape[1:], parts.dtype)
    full = lax.dynamic_update_slice_in_dim(
        full, parts, lax.axis_index("core") * (owners // 2), axis=0
    )
    mine = lax.psum_scatter(full, "zp", scatter_dimension=0, tiled=True)[0]
    mine = lax.psum_scatter(mine, ("x", "core", "y"), scatter_dimension=0, tiled=True)
    return mine.astype(F32)


def cut_rows(fulls):
    core = lax.axis_index("core")
    same, cross = [], []
    for full in fulls:
        rows, columns = full.shape[0] // 8, full.shape[1]
        full = full.reshape(2, 2, 2, rows, columns)
        same.append(cut(lax.dynamic_index_in_dim(full, core, 1, False), "x", 0))
        cross.append(cut(lax.dynamic_index_in_dim(full, 1 - core, 1, False), "y", 1))
    return (
        [kept[0] for kept, _ in same],
        [kept[:, 0] for kept, _ in cross],
        jnp.stack([sent[0] for _, sent in same]),
        jnp.stack([sent[:, 0] for _, sent in cross]),
    )


def cut_again(sames, crosses):
    same = [cut(value, "y", 0) for value in sames]
    cross = [cut(value, "x", 0) for value in crosses]
    return (
        [kept[0] for kept, _ in same],
        [kept[0] for kept, _ in cross],
        jnp.stack([sent[0] for _, sent in same]),
        jnp.stack([sent[0] for _, sent in cross]),
    )


def both(kept, got):
    return [
        [added(mine, other[k]) for k, mine in enumerate(values)]
        for values, other in zip(kept[0:2], got)
    ]


def home_parts(sames, crosses):
    at_home = lax.axis_index("core") == lax.axis_index("zp")
    cross = jnp.stack(crosses)
    return jnp.where(at_home, cross, jnp.stack(sames)), cross


def at_owner(near, far, sames):
    at_home = lax.axis_index("core") == lax.axis_index("zp")
    return [
        near[k].astype(F32) + jnp.where(at_home, same.astype(F32), far[k].astype(F32))
        for k, same in enumerate(sames)
    ]


def go_home(sent):
    return (
        lax.ppermute(sent[0], ("core", "zp"), HOME),
        lax.ppermute(sent[1], ("core", "zp"), FAR),
    )


def own_of_slice(value):
    owners = lax.axis_size("zp")
    core, part = lax.axis_index("core"), lax.axis_index("zp")
    other = swap(value, "core")
    share = value.shape[-1] // (owners // 2)
    wanted = jnp.where(part // (owners // 2) == core, value, other)
    return lax.dynamic_slice_in_dim(wanted, (part % (owners // 2)) * share, share, value.ndim - 1)


def slice_of_own(value, after):
    owners = lax.axis_size("zp")
    core = lax.axis_index("core")
    if owners == 2:
        other = hold(swap(value, "zp"), after)
        return jnp.where(core == lax.axis_index("zp"), value, other)[None]
    parts = lax.all_gather(value, "zp")
    return lax.dynamic_slice_in_dim(parts, core * (owners // 2), owners // 2, 0)


def per_device(
    hidden,
    cotangent,
    norm_gain,
    w_z,
    w_x,
    w_bc,
    w_dt,
    conv_x,
    conv_x_bias,
    conv_bc,
    conv_bc_bias,
    dt_bias,
    a_log,
    d_skip,
    inner_gain,
    w_out,
):
    micro, own_len, model = hidden.shape
    owners = lax.axis_size("zp")
    share = w_x.shape[1]
    own_heads = w_dt.shape[1]
    inner_full = share * 2 * owners
    states2 = w_bc.shape[1]
    halves = owners // 2
    inner = share * halves
    heads = own_heads * halves
    head_width = inner // heads
    width = inner + states2

    def matmul(left, right, contract, dtype=F32):
        return lax.dot_general(
            left, right, (contract, ((), ())), preferred_element_type=F32
        ).astype(dtype)

    def spliced(parts, sizes):
        if halves == 1:
            return parts[0]
        columns, at = [], 0
        for size, copies in sizes:
            columns += [parts[k][:, at : at + size] for k in range(halves if copies else 1)]
            at += size
        return jnp.concatenate(columns, axis=1)

    parts = range(micro)

    own = hidden.astype(F32)
    gain_in = norm_gain.astype(F32)
    r0 = lax.rsqrt(jnp.mean(own * own, axis=-1, keepdims=True) + EPS)
    filler = LANES // halves - own_heads
    own_first = jnp.concatenate(
        [w_x, w_bc, w_dt, jnp.zeros((w_dt.shape[0], filler), BF16)], axis=1
    )
    own_second = jnp.concatenate([w_z, jnp.transpose(w_out)], axis=1)
    normed_own = [(own[part : part + 1] * r0[part : part + 1] * gain_in).astype(BF16) for part in parts]
    fast = all_pairs()

    if fast:
        got = fetch(own_first)
        start = swap(normed_own[0], "zq")
        same, cross = fetched(own_first, *got)
        first = jnp.stack([same, swap(same, "x")])
        second = jnp.stack([cross, swap(cross, "y")])
        rest = swap(first, "y"), swap(second, "x")
        own_second, after_first = hold((own_second, normed_own[1:]), first, second)
        got = fetch(own_second)
        started = [start] + [swap(value, "zq") for value in after_first]
        w_first = place(first, rest[0], second, rest[1])
        later = rest
        got = hold(got, w_first)
        same, cross = fetched(own_second, *got)
        moved = swap(same, "x"), swap(cross, "y")
    else:
        started = [swap(value, "zq") for value in normed_own]
        later = ()
        w_first = spliced(
            gather_slice(own_first), ((share, 1), (states2, 0), (own_heads, 1), (filler, 1))
        )
    per_head = jnp.concatenate([dt_bias, a_log, d_skip])
    per_head = jnp.pad(per_head, (0, share - 3 * own_heads))
    small = jnp.concatenate([conv_x, conv_x_bias[None], inner_gain[None]], axis=0).astype(F32)
    small = jnp.concatenate([small, per_head[None], jnp.zeros((1, share), F32)])
    small = slice_of_own(hold(small, w_first), w_first)
    channel_rows = jnp.concatenate([small[k, 0:6] for k in range(halves)], axis=1)
    head_rows = jnp.concatenate(
        [small[k, 6, 0 : 3 * own_heads].reshape(3, own_heads) for k in range(halves)], axis=1
    )
    conv_shared = jnp.concatenate([conv_bc, conv_bc_bias[None]], axis=0).astype(F32)
    taps = jnp.pad(jnp.concatenate([channel_rows[0:5], conv_shared], axis=1), ((0, 3), (0, 0)))
    head_in = jnp.stack([head_rows[0], -jnp.exp(head_rows[1]), jnp.ones((heads,), F32)])
    head_in = jnp.pad(head_in, ((0, 5), (0, LANES - heads)))
    rows = jnp.stack([jnp.repeat(head_rows[2], head_width), channel_rows[5]])
    rows = jnp.pad(rows, ((0, 6), (0, 0)))
    spread = (
        lax.broadcasted_iota(jnp.int32, (LANES, inner), 1) // head_width
        == lax.broadcasted_iota(jnp.int32, (LANES, inner), 0)
    ).astype(BF16)
    spread = jnp.concatenate([spread, spread])

    normed, scans = [], []
    for part in parts:
        value, got = normed_own[part], hold(started[part], *later)
        normed.append(joined(value, got, swap(value, "core"), swap(got, "core")))
        xw = matmul(normed[part], w_first, ((2,), (0,)), BF16)
        scans.append((xw, shift(xw[:, -RIM:, 0:width], 1)))
        later = (xw,)
    if fast:
        moved = hold(moved, scans[0][0])
        first, second = jnp.stack([same, moved[0]]), jnp.stack([cross, moved[1]])
        got_second = first, swap(first, "y"), second, swap(second, "x")
    local = []
    for part in parts:
        before = [k[5] for k in local[-1:]]
        local.append(local_states(*scans[part], taps, head_in, spread, before))
        if part == 0:
            cot_own = hold(cotangent, local[0][5], scans[-1][1])
            cot_own = [cot_own[k : k + 1] for k in parts]
            cot_got = [swap(value, "zq") for value in cot_own]
    totals = [local[part][4] for part in parts]
    packed = [local[part][5] for part in parts]
    if fast:
        w_second = place(*hold(got_second, packed[-1]))
    else:
        w_second = spliced(
            gather_slice(hold(own_second, packed[-1])), ((share, 1), (share, 1))
        )
    w_gate, w_down = w_second[:, 0:inner], w_second[:, inner:]
    def hop(part, packed, ends, way, *before):
        if not fast:
            return packed, packed
        got = row_hop(packed, way, *before)
        return got, leave(ends, totals[part], got, spread)

    def entering(found, way, *before):
        if not fast:
            return chained(found[0], way)
        return found[0], *column_hops(found[1], way, *before)

    found = [hop(0, packed[0], local[0][3], 1, w_second)]
    gate = [
        matmul(hold(normed[part], found[0][1]), w_gate, ((2,), (0,)), BF16) for part in parts
    ]
    cot_far = (
        swap(hold(cotangent, local[0][5]), "core"),
        [swap(hold(cot_got[k], gate[k]), "core") for k in parts],
    )

    def whole_cot(part, *before):
        far = hold((cot_far[0], cot_far[1][part]), *before)
        return joined(cot_own[part], cot_got[part], far[0][part : part + 1], far[1])

    cot = [whole_cot(0, gate[-1])]

    w_down_held = hold(w_down, found[0][1])
    gm = [matmul(cot[0], w_down_held, ((2,), (0,)))]
    mixes, stats, branches, gates = [], [], [], []
    g_gate = g_down = 0.0
    tokens = ((0, 1), (0, 1))
    for part in parts:
        xbc, cumul, dt = local[part][0:3]
        before = (gm[0],) if part == 0 else (gates[part - 1][5], gm[part])
        start = entering(found[part], 1, *before)
        y, gained, enter, stat = mixer(xbc, cumul, dt, start, gate[part], gm[part], rows, spread, before)
        mixes.append((y, enter))
        other = swap(stat, "core")
        if part + 1 < micro:
            following = hold(packed[part + 1], found[part][1])
            found.append(hop(part + 1, following, local[part + 1][3], 1, y))
            cot.append(whole_cot(part + 1, found[-1][1]))
            gm.append(matmul(cot[-1], w_down, ((2,), (0,))))
            other = hold(other, cot[-1])
        else:
            g_gate = matmul(normed[0], hold(gates[0][1], y), tokens)
            other = hold(other, g_gate)
        stat = stat + jnp.flip(other, 0)
        other = swap(stat, "zq")
        branch = matmul(hold(gained, stat, gm[-1]), w_down, ((2,), (1,)), BF16)
        stats.append(stat + hold(other, branch))
        branches.append((branch, swap(branch[1], "core")))
        gates.append(
            gate_back(
                inner_full, y, xbc, gate[part], gm[part], stats[part], cumul, totals[part],
                rows, spread, [branch],
            )
        )
    back_packed = [g[5] for g in gates]

    found = [hop(0, back_packed[0], gates[0][3], -1, back_packed[-1])]
    for part in parts:
        g_down = g_down + matmul(cot[part], hold(gates[part][2], found[0][1]), tokens)
        if part == 0:
            branch_cut = [
                cut(added(branch[0], hold(got, g_down)), "zq", 0) for branch, got in branches
            ]
            branch_sent = jnp.stack([sent for _, sent in branch_cut])
            branch_got = swap(branch_sent, "zq")
        else:
            g_gate = g_gate + matmul(normed[part], hold(gates[part][1], g_down), tokens)
    g_gate, g_down = g_gate.astype(BF16), g_down.astype(BF16)
    g_normed_gate = [matmul(hold(gates[0][1], g_gate), w_gate, ((2,), (1,)))]
    gin = entering(found[0], -1, g_normed_gate[0])
    for part in parts[1:]:
        following = hold(back_packed[part], found[part - 1][1])
        found.append(hop(part, following, gates[part][3], -1, g_normed_gate[0]))
        g_normed_gate.append(
            matmul(hold(gates[part][1], found[part][1]), w_gate, ((2,), (1,)))
        )
    wait_for = [g_normed_gate[-1], branch_sent]
    if fast:
        second = cut_rows(hold([g_gate, g_down], *gin))
        moved = swap(second[2], "x"), swap(second[3], "y")
        wait_for += second[2:]

    g_first, heads_out, g_hidden, g_norm_gain = 0.0, [], [], 0.0

    def token_grad(part, kept, got):
        x, r, g = own[part], r0[part], added(kept, got, F32)
        q0 = g * gain_in
        grad = (
            cotangent[part].astype(F32) + r * q0
            - x * (r * r * r) * jnp.mean(q0 * x, axis=-1, keepdims=True)
        )
        return grad, jnp.sum(g * x * r, axis=0)

    def whole_output(*before):
        outputs = []
        for part in parts:
            square = lax.dynamic_slice_in_dim(
                stats[part][0, 0], lax.axis_index("zq") * own_len, own_len, 0
            )
            r1 = lax.rsqrt(square / inner_full + EPS)[:, None]
            got = hold(branch_got, *before)[part]
            outputs.append((own[part] + r1 * added(branch_cut[part][0], got, F32)).astype(BF16))
        return jnp.stack(outputs)

    for part in parts:
        xbc, cumul, dt = local[part][0:3]
        gmix, rim, *sums = adjoint(
            xbc, cumul, dt, gates[part][0], mixes[part][0], mixes[part][1], gin,
            *scans[part], taps, head_in, rows, spread, wait_for,
        )
        if part == micro - 1 and fast and micro > 1:
            (gmix, rim, *sums), norm_cut, got_home = hold(
                ((gmix, rim, *sums), norm_cut, got_home)
            )
        if part < micro - 1:
            gin = entering(found[part + 1], -1)
            gmix, rim, *sums = hold(
                (gmix, rim, *sums), *gin, branch_got, *(moved if fast else ())
            )
        heads_out.append(sums)
        ahead = shift(rim, -1)
        last_part = part == micro - 1
        if last_part:
            if micro > 1:
                kept, got = norm_cut
                grad, gain = token_grad(part - 1, kept, hold(got, gmix))
                g_hidden.append(grad)
                g_norm_gain = g_norm_gain + gain
                ahead = hold(ahead, grad)
        else:
            if fast:
                moved = hold(moved, gmix)
                second = cut_again(*both(second, moved))
                moved = swap(second[2], "y"), swap(second[3], "x")
        fix = jnp.stack(
            [sum(taps[k, :] * ahead[:, r - k] for k in range(r + 1)) for r in range(3)], axis=1
        )
        length = gmix.shape[1]
        last = gmix[:, length - RIM :].astype(F32)
        last = last + jnp.pad(fix, ((0, 0), (RIM - 3, 0), (0, LANES)))
        gmix = lax.dynamic_update_slice_in_dim(gmix, last.astype(BF16), length - RIM, 1)

        def for_weights(gmix):
            return g_first + matmul(normed[part], gmix, tokens)

        def for_tokens(gmix):
            total = g_normed_gate[part] + matmul(gmix, w_first, ((2,), (1,)))
            return total.astype(BF16)

        if last_part:
            g_first = for_weights(gmix).astype(BF16)
            if fast:
                first = cut_rows([g_first])
                moved_first = swap(first[2], "x"), swap(first[3], "y")
            total = for_tokens(hold(gmix, g_first, *(first[2:] if fast else ())))
            other = swap(total[1], "core")
        else:
            total = for_tokens(gmix)
            other = swap(total[1], "core")
            g_first = for_weights(hold(gmix, total))
            kept, sent = cut(added(total[0], hold(other, g_first)), "zq", 0)
            norm_cut = kept, swap(sent, "zq")
            if part == micro - 2:
                outputs = whole_output(g_first, sent)
            gin = hold(gin, outputs)
            wait_for = [sent, outputs]
            if fast and part == micro - 2:
                moved = hold(moved, g_first)
                pair = both(second, moved)
                home = home_parts(*pair)
                wait_for += home
                got_home = go_home(home)

    kept, sent = cut(added(total[0], other), "zq", 0)
    got_norm = swap(sent, "zq")
    if fast:
        g_gate, g_down = at_owner(*got_home, pair[0])
        first = cut_again(*both(first, hold(moved_first, g_gate, g_down)))
        moved = swap(first[2], "y"), swap(first[3], "x")
        got_norm = hold(got_norm, *first[2:])
        pair = both(first, hold(moved, got_norm))
        home = home_parts(*pair)
        got_home = go_home(home)
        grad, gain = token_grad(micro - 1, kept, hold(got_norm, *home))
        g_first = at_owner(*hold(got_home, grad), pair[0])[0]
    else:
        g_gate, g_down = [
            reduce_slice(jnp.stack(jnp.split(value, halves, axis=1))) for value in (g_gate.astype(BF16), g_down.astype(BF16))
        ]
        grad, gain = token_grad(micro - 1, kept, got_norm)
        g_first = reduce_slice(
            jnp.concatenate(
                [
                    jnp.stack(jnp.split(g_first[:, 0:inner], halves, axis=1)),
                    jnp.concatenate(
                        [
                            g_first[None, :, inner:width],
                            jnp.zeros((halves - 1, model, states2), BF16),
                        ]
                    ),
                    jnp.stack(jnp.split(g_first[:, width : width + heads], halves, axis=1)),
                ],
                axis=2,
            )
        )
    g_hidden = jnp.stack(g_hidden + [grad])
    g_norm_gain = g_norm_gain + gain
    g_bc = g_first[:, share : share + states2]
    g_bc = sum_axis(sum_axis(g_bc, "zp"), "zq")

    g_taps, g_heads, g_skip = (sum(b[k] for b in heads_out) for k in range(3))
    g_gain = sum(g[4] for g in gates)
    skip_heads = jnp.sum(g_skip[0].reshape(heads, head_width), axis=1)
    small = jnp.concatenate(
        [g_taps[0:5, 0:inner].reshape(-1), g_gain[0], g_heads[0, 0:heads], g_heads[1, 0:heads], skip_heads]
    )
    size = small.shape[0]
    packed = jnp.concatenate([small, g_taps[0:5, inner:width].reshape(-1), g_norm_gain])
    for axis in ("x", "y", "zp"):
        packed = sum_axis(packed, axis)
    small = packed[:size]
    shared = sum_axis(sum_axis(packed[size:], "core"), "zq")
    bc_rows = shared[0 : 5 * states2].reshape(5, states2)
    channel = own_of_slice(small[0 : 6 * inner].reshape(6, inner))
    per_head = own_of_slice(small[6 * inner :].reshape(3, heads))
    return (
        outputs,
        g_hidden,
        shared[5 * states2 :],
        g_gate,
        g_first[:, 0:share],
        g_bc,
        g_first[:, share + states2 : share + states2 + own_heads],
        channel[0:4],
        channel[4],
        bc_rows[0:4],
        bc_rows[4],
        per_head[0],
        per_head[1],
        per_head[2],
        channel[5],
        jnp.transpose(g_down),
    )


def solution(mesh):
    dp, seq, tensor = (mesh.shape[name] for name in ("dp", "seq", "tensor"))
    fine = Mesh(
        mesh.devices.reshape(dp // 2, 2, seq, tensor // 2, 2), ("x", "core", "y", "zp", "zq")
    )
    data, tens = ("x", "core", "y"), ("zp", "zq")
    tokens = P(("x", "core"), ("y", "zp", "zq"), None)
    params = (
        P(),
        P(data, tens),
        P(data, tens),
        P(data, None),
        P(data, tens),
        P(None, tens),
        P(tens),
        P(),
        P(),
        P(tens),
        P(tens),
        P(tens),
        P(tens),
        P(tens, data),
    )
    return jax.shard_map(
        per_device,
        mesh=fine,
        in_specs=(tokens, tokens) + params,
        out_specs=(tokens, tokens) + params,
        check_vma=False,
    )
```

```python
import functools

import jax
import jax.numpy as jnp
from jax import lax
from jax.experimental import pallas as pl
from jax.experimental.pallas import tpu as pltpu
from jax.sharding import Mesh
from jax.sharding import PartitionSpec as P

CHUNK = 256
HALF = CHUNK // 2
LANES = 128
STRIP = 256
RIM = 16
EPS = 1e-05
F32 = jnp.float32
BF16 = jnp.bfloat16
VMEM_BYTES = 48 * 1024 * 1024


def dot(left, right):
    return lax.dot_general(left, right, (((1,), (0,)), ((), ())), preferred_element_type=F32)


def dot_nt(left, right):
    return lax.dot_general(left, right, (((1,), (1,)), ((), ())), preferred_element_type=F32)


def pieces(value, count):
    terms = []
    for _ in range(count):
        term = value.astype(BF16)
        terms.append(term)
        value = value - term.astype(F32)
    return terms


def spread_heads(value, spread):
    return sum(dot(term, spread) for term in pieces(value, 2))


def gather_heads(value, spread):
    return sum(dot_nt(term, spread) for term in pieces(value, 2))


def running_sum(value, mask):
    return sum(dot(mask, term) for term in pieces(value, 3))


def iota2(rows, cols, dim):
    return lax.broadcasted_iota(jnp.int32, (rows, cols), dim)


def turned(value):
    return jnp.transpose(value.astype(F32)).astype(BF16)


def strips(width):
    return [slice(at, at + STRIP) for at in range(0, width, STRIP)]


def conv_pre(ext, taps, cols):
    total = taps[4:5, cols] + taps[0:1, cols] * ext[pl.ds(RIM - 3, CHUNK), cols]
    for k in range(1, 4):
        total = total + taps[k : k + 1, cols] * ext[pl.ds(RIM - 3 + k, CHUNK), cols]
    return total


def softplus(value):
    return jnp.maximum(value, 0.0) + jnp.log1p(jnp.exp(-jnp.abs(value)))


def write_packed(packed_ref, end, total):
    packed_ref[0, 0:LANES, :] = end.astype(BF16)
    packed_ref[0, LANES:, :] = jnp.zeros((RIM, end.shape[1]), BF16)
    row = iota2(RIM, LANES, 0)
    logs = jnp.zeros((RIM, LANES), F32)
    for k, term in enumerate(pieces(total, 3)):
        logs = jnp.where(row == k, term.astype(F32), logs)
    packed_ref[0, LANES:, 0:LANES] = logs.astype(BF16)


def widened(log, spread):
    return spread_heads(jnp.broadcast_to(jnp.exp(log), (8, LANES)), spread)[0:1, :]


def entering_state(packed_ref, first_ref, second_ref, spread_ref):
    passed = jnp.sum(packed_ref[0, LANES:, 0:LANES].astype(F32), axis=0, keepdims=True)
    from_row = first_ref[0].astype(F32) + second_ref[0].astype(F32)
    return packed_ref[0, 0:LANES, :].astype(F32) + widened(passed, spread_ref[...]) * from_row


def leave_kernel(end_ref, total_ref, packed_ref, spread_ref, leaving_ref):
    kept = packed_ref[0, 0:LANES, :].astype(F32) * widened(total_ref[0, 0:1, :], spread_ref[...])
    leaving_ref[0] = (end_ref[0] + kept).astype(BF16)


def state_kernel(
    mix_ref, halo_ref, step_ref, taps_ref, heads_ref, spread_ref,
    xbc_ref, sum_ref, dt_ref, end_ref, total_ref, packed_ref, ext,
):
    inner = spread_ref.shape[1]
    place = pl.program_id(1)

    @pl.when(place == 0)
    def _():
        ext[0:RIM, :] = halo_ref[0].astype(F32)
        end_ref[...] = jnp.zeros_like(end_ref)
        total_ref[...] = jnp.zeros_like(total_ref)

    @pl.when(place > 0)
    def _():
        ext[0:RIM, :] = ext[CHUNK : CHUNK + RIM, :]

    dt = softplus(step_ref[0].astype(F32) + heads_ref[0:1, :])
    lower = (iota2(CHUNK, CHUNK, 0) >= iota2(CHUNK, CHUNK, 1)).astype(F32).astype(BF16)
    cumul = running_sum(dt * heads_ref[1:2, :], lower)
    sum_ref[0] = cumul
    dt_ref[0] = dt
    last = cumul[CHUNK - 1 : CHUNK, :]
    total_ref[0] += jnp.broadcast_to(last, total_ref.shape[1:])
    tail = jnp.exp(last - cumul) * dt
    decay = jnp.broadcast_to(jnp.exp(last), (8, LANES))
    b_turned = None
    for cols in reversed(strips(xbc_ref.shape[2])):
        ext[RIM:, cols] = mix_ref[0, :, cols].astype(F32)
        pre = conv_pre(ext, taps_ref, cols)
        act = (pre * jax.nn.sigmoid(pre)).astype(BF16)
        xbc_ref[0, :, cols] = act
        if cols.start >= inner:
            b_turned = turned(act[:, 0:LANES])
        else:
            held = spread_ref[:, cols]
            weighted = (act.astype(F32) * spread_heads(tail, held)).astype(BF16)
            kept = end_ref[0, :, cols] * spread_heads(decay, held)[0:1, :]
            end_ref[0, :, cols] = kept + dot(b_turned, weighted)

    @pl.when(place == pl.num_programs(1) - 1)
    def _():
        write_packed(packed_ref, end_ref[0], total_ref[0, 0:1, :])


def scan_kernel(
    xbc_ref, sum_ref, dt_ref, packed_ref, first_ref, second_ref, gate_ref, gm_ref, rows_ref, spread_ref,
    y_ref, mixed_ref, enter_ref, stat_ref, state,
):
    inner = spread_ref.shape[1]

    @pl.when(pl.program_id(1) == 0)
    def _():
        state[...] = entering_state(packed_ref, first_ref, second_ref, spread_ref)

    cumul = sum_ref[0]
    dt = dt_ref[0]
    across = jnp.transpose(cumul)
    last = cumul[CHUNK - 1 : CHUNK, :]
    tail = jnp.exp(last - cumul) * dt
    reach = jnp.exp(cumul)
    decay = jnp.broadcast_to(jnp.exp(last), (8, LANES))
    b_low = xbc_ref[0, :, inner : inner + LANES]
    c_low = xbc_ref[0, :, inner + LANES :]
    b_turned = turned(b_low)
    score = dot_nt(c_low, b_low)
    causal = iota2(HALF, HALF, 0) >= iota2(HALF, HALF, 1)
    first = iota2(1, LANES, 1) < LANES // 2
    squares = jnp.zeros((CHUNK, STRIP), F32)
    crossed = jnp.zeros((CHUNK, STRIP), F32)
    for cols in strips(inner):
        held = spread_ref[:, cols]
        x = xbc_ref[0, :, cols].astype(F32)
        u = x * spread_heads(dt, held)
        weighted = (x * spread_heads(tail, held)).astype(BF16)
        entering = state[:, cols].astype(BF16)
        enter_ref[0, 0, :, cols] = entering
        carried = dot(c_low, entering) * spread_heads(reach, held)
        state[:, cols] = state[:, cols] * spread_heads(decay, held)[0:1, :] + dot(b_turned, weighted)
        for pair in range(STRIP // LANES):
            lanes = slice(pair * LANES, (pair + 1) * LANES)
            top = carried[0:HALF, lanes]
            bottom = carried[HALF:, lanes]
            for side in range(2):
                head = (cols.start + pair * LANES) // (LANES // 2) + side
                mine = jnp.where(first if side == 0 else ~first, u[:, lanes], 0.0).astype(BF16)
                column = cumul[:, head : head + 1]
                row = across[head : head + 1, :]
                corner = jnp.where(causal, jnp.exp(column[0:HALF] - row[:, 0:HALF]), 0.0)
                top = top + dot((score[0:HALF, 0:HALF] * corner).astype(BF16), mine[0:HALF])
                left = jnp.exp(column[HALF:] - row[:, 0:HALF])
                right = jnp.where(causal, jnp.exp(column[HALF:] - row[:, HALF:]), 0.0)
                bottom = bottom + dot((score[HALF:, 0:HALF] * left).astype(BF16), mine[0:HALF])
                bottom = bottom + dot((score[HALF:, HALF:] * right).astype(BF16), mine[HALF:])
            into = slice(cols.start + pair * LANES, cols.start + (pair + 1) * LANES)
            y_ref[0, 0:HALF, into] = top
            y_ref[0, HALF:, into] = bottom
        y = y_ref[0, :, cols] + rows_ref[0:1, cols] * x
        gate = gate_ref[0, :, cols].astype(F32)
        gated = y * gate * jax.nn.sigmoid(gate)
        gained = gated * rows_ref[1:2, cols]
        mixed_ref[0, :, cols] = gained.astype(BF16)
        squares = squares + gated * gated
        crossed = crossed + gained * gm_ref[0, :, cols]
    ones = jnp.ones((8, STRIP), BF16)
    square_row = sum(dot_nt(ones, term) for term in pieces(squares, 3))
    cross_row = sum(dot_nt(ones, term) for term in pieces(crossed, 3))
    stat_ref[0] = jnp.where(iota2(8, CHUNK, 0) == 0, square_row, cross_row)


def gate_kernel(
    inner_full, y_ref, xbc_ref, gate_ref, gm_ref, stat_ref, sum_ref, total_ref, rows_ref, spread_ref,
    gy_ref, gz_ref, mixed_ref, back_ref, gain_ref, packed_ref,
):
    inner = spread_ref.shape[1]

    @pl.when(pl.program_id(1) == 0)
    def _():
        back_ref[...] = jnp.zeros_like(back_ref)

    @pl.when((pl.program_id(0) == 0) & (pl.program_id(1) == 0))
    def _():
        gain_ref[...] = jnp.zeros_like(gain_ref)

    stats = jnp.transpose(stat_ref[0])
    scale = lax.rsqrt(stats[:, 0:1] / inner_full + EPS)
    bent = scale * scale * scale * (stats[:, 1:2] / inner_full)
    cumul = sum_ref[0]
    reach = jnp.exp(cumul)
    decay = jnp.broadcast_to(jnp.exp(cumul[CHUNK - 1 : CHUNK, :]), (8, LANES))
    c_turned = turned(xbc_ref[0, :, inner + LANES :])
    for cols in strips(inner):
        held = spread_ref[:, cols]
        x = xbc_ref[0, :, cols].astype(F32)
        y = y_ref[0, :, cols] + rows_ref[0:1, cols] * x
        gate = gate_ref[0, :, cols].astype(F32)
        sigmoid = jax.nn.sigmoid(gate)
        silu = gate * sigmoid
        gated = y * silu
        scaled = gated * scale
        gm = gm_ref[0, :, cols]
        gain = rows_ref[1:2, cols]
        gg = scale * gm * gain - gated * bent
        gy = (gg * silu).astype(BF16)
        gy_ref[0, :, cols] = gy
        gz_ref[0, :, cols] = (gg * y * sigmoid * (1.0 + gate * (1.0 - sigmoid))).astype(BF16)
        mixed_ref[0, :, cols] = (scaled * gain).astype(BF16)
        gain_ref[:, cols] += jnp.broadcast_to(jnp.sum(gm * scaled, axis=0, keepdims=True), (8, STRIP))
        reached = (gy.astype(F32) * spread_heads(reach, held)).astype(BF16)
        kept = back_ref[0, :, cols] * spread_heads(decay, held)[0:1, :]
        back_ref[0, :, cols] = kept + dot(c_turned, reached)

    @pl.when(pl.program_id(1) == pl.num_programs(1) - 1)
    def _():
        write_packed(packed_ref, back_ref[0], total_ref[0, 0:1, :])


def adjoint_kernel(
    xbc_ref, sum_ref, dt_ref, gy_ref, y_ref, enter_ref, packed_ref, first_ref, second_ref, mix_ref, before_ref, halo_ref,
    step_ref, taps_ref, heads_ref, rows_ref, spread_ref,
    gmix_ref, rim_ref, gtaps_ref, gheads_ref, gskip_ref, back, ext, gpre, pulled,
):
    inner = spread_ref.shape[1]
    chunks = pl.num_programs(1)
    order = pl.program_id(1)

    @pl.when((pl.program_id(0) == 0) & (order == 0))
    def _():
        gtaps_ref[...] = jnp.zeros_like(gtaps_ref)
        gheads_ref[...] = jnp.zeros_like(gheads_ref)
        gskip_ref[...] = jnp.zeros_like(gskip_ref)

    @pl.when(order == 0)
    def _():
        back[...] = entering_state(packed_ref, first_ref, second_ref, spread_ref)
        gpre[CHUNK:, :] = jnp.zeros((8, gpre.shape[1]), F32)

    @pl.when(order > 0)
    def _():
        gpre[CHUNK:, :] = gpre[0:8, :]

    @pl.when(order == chunks - 1)
    def _():
        ext[0:RIM, :] = halo_ref[0].astype(F32)

    @pl.when(order < chunks - 1)
    def _():
        ext[0:RIM, :] = before_ref[0].astype(F32)

    cumul = sum_ref[0]
    dt = dt_ref[0]
    across = jnp.transpose(cumul)
    last = cumul[CHUNK - 1 : CHUNK, :]
    fade = jnp.exp(last - cumul)
    reach = jnp.exp(cumul)
    decay = jnp.broadcast_to(jnp.exp(last), (8, LANES))
    b_low = xbc_ref[0, :, inner : inner + LANES]
    c_low = xbc_ref[0, :, inner + LANES :]
    c_turned = turned(c_low)
    score = dot_nt(b_low, c_low)
    causal = iota2(HALF, HALF, 0) <= iota2(HALF, HALF, 1)
    first = iota2(1, LANES, 1) < LANES // 2
    pulled[...] = jnp.zeros_like(pulled)
    gb = jnp.zeros((CHUNK, LANES), F32)
    gc = jnp.zeros((CHUNK, LANES), F32)
    between = jnp.zeros((CHUNK, LANES), F32)
    arrived = jnp.zeros((CHUNK, LANES), F32)
    direct = jnp.zeros((CHUNK, LANES), F32)
    joined = jnp.zeros((8, LANES), F32)

    def conv_part(cols, gact):
        ext[RIM:, cols] = mix_ref[0, :, cols].astype(F32)
        pre = conv_pre(ext, taps_ref, cols)
        sigmoid = jax.nn.sigmoid(pre)
        gp = gact.astype(BF16).astype(F32) * sigmoid * (1.0 + pre * (1.0 - sigmoid))
        gpre[0:CHUNK, cols] = gp
        rim_ref[0, :, cols] = gp[0:8, :]
        total = taps_ref[3:4, cols] * gp
        for k in range(3):
            total = total + taps_ref[k : k + 1, cols] * gpre[pl.ds(3 - k, CHUNK), cols]
            gtaps_ref[k : k + 1, cols] += jnp.sum(
                gp * ext[pl.ds(RIM - 3 + k, CHUNK), cols], axis=0, keepdims=True
            )
        gtaps_ref[3:4, cols] += jnp.sum(gp * ext[RIM:, cols], axis=0, keepdims=True)
        gtaps_ref[4:5, cols] += jnp.sum(gp, axis=0, keepdims=True)
        gmix_ref[0, :, cols] = total.astype(BF16)

    for cols in strips(inner):
        held = spread_ref[:, cols]
        x = xbc_ref[0, :, cols].astype(F32)
        dt_wide = spread_heads(dt, held)
        fade_wide = spread_heads(fade, held)
        u = x * dt_wide
        u_low = u.astype(BF16)
        weighted = (u * fade_wide).astype(BF16)
        gy_low = gy_ref[0, :, cols]
        gy = gy_low.astype(F32)
        reached = (gy * spread_heads(reach, held)).astype(BF16)
        later = back[:, cols]
        later_low = later.astype(BF16)
        entered = enter_ref[0, 0, :, cols]
        gb = gb + dot_nt(weighted, later_low)
        gc = gc + dot_nt(reached, entered)
        gu_carried = dot(b_low, later_low) * fade_wide
        sums = jnp.sum(later * entered.astype(F32), axis=0, keepdims=True)
        joined = joined + gather_heads(jnp.broadcast_to(sums, (8, STRIP)), held)
        back[:, cols] = later * spread_heads(decay, held)[0:1, :] + dot(c_turned, reached)
        parts = []
        for pair in range(STRIP // LANES):
            lanes = slice(pair * LANES, (pair + 1) * LANES)
            top = gu_carried[0:HALF, lanes]
            bottom = gu_carried[HALF:, lanes]
            gy_pair = gy_low[:, lanes]
            for side in range(2):
                head = (cols.start + pair * LANES) // (LANES // 2) + side
                keep = first if side == 0 else ~first
                gy_mine = jnp.where(keep, gy[:, lanes], 0.0).astype(BF16)
                u_mine = jnp.where(keep, u[:, lanes], 0.0).astype(BF16)
                column = cumul[:, head : head + 1]
                row = across[head : head + 1, :]
                corner = jnp.where(causal, jnp.exp(row[:, 0:HALF] - column[0:HALF]), 0.0)
                side_right = jnp.exp(row[:, HALF:] - column[0:HALF])
                low_right = jnp.where(causal, jnp.exp(row[:, HALF:] - column[HALF:]), 0.0)
                top = top + dot((score[0:HALF, 0:HALF] * corner).astype(BF16), gy_mine[0:HALF])
                top = top + dot((score[0:HALF, HALF:] * side_right).astype(BF16), gy_mine[HALF:])
                bottom = bottom + dot((score[HALF:, HALF:] * low_right).astype(BF16), gy_mine[HALF:])
                upper = dot_nt(u_mine[0:HALF], gy_pair)
                pulled[0:HALF, 0:HALF] += upper[:, 0:HALF] * corner
                pulled[0:HALF, HALF:] += upper[:, HALF:] * side_right
                pulled[HALF:, HALF:] += dot_nt(u_mine[HALF:], gy_pair[HALF:]) * low_right
            parts.append(jnp.concatenate([top, bottom], axis=0))
        gu = jnp.concatenate(parts, axis=1)
        u_kept = u_low.astype(F32)
        between = between + gather_heads(gy * y_ref[0, :, cols] - u_kept * gu, held)
        arrived = arrived + gather_heads(u_kept * gu_carried, held)
        direct = direct + gather_heads(x * gu, held)
        gskip_ref[:, cols] += jnp.broadcast_to(jnp.sum(gy * x, axis=0, keepdims=True), (8, STRIP))
        conv_part(cols, dt_wide * gu + rows_ref[0:1, cols] * gy)

    pulled_low = pulled[...].astype(BF16)
    gb = gb + dot(pulled_low, c_low)
    gc = gc + dot(jnp.transpose(pulled[...]).astype(BF16), b_low)
    conv_part(slice(inner, inner + 2 * LANES), jnp.concatenate([gb, gc], axis=1))

    upper = (iota2(CHUNK, CHUNK, 0) <= iota2(CHUNK, CHUNK, 1)).astype(F32).astype(BF16)
    whole = jnp.sum(arrived, axis=0, keepdims=True) + decay[0:1, :] * joined[0:1, :]
    glg = running_sum(between, upper) + whole
    rate = heads_ref[1:2, :]
    gdt = direct + rate * glg
    raw = step_ref[0].astype(F32) + heads_ref[0:1, :]
    gsi = gdt * jax.nn.sigmoid(raw) * heads_ref[2:3, :]
    gmix_ref[0, :, inner + 2 * LANES :] = gsi.astype(BF16)
    gheads_ref[0:1, :] += jnp.sum(gsi, axis=0, keepdims=True)
    gheads_ref[1:2, :] += jnp.sum(glg * dt * rate, axis=0, keepdims=True)


def flat(width, order=lambda i: i, column=0):
    return pl.BlockSpec((1, CHUNK, width), lambda g, i: (g, order(i), column))


def whole(*shape):
    return pl.BlockSpec((1,) + shape, lambda g, i: (g,) + (0,) * len(shape))


def fixed(shape):
    return pl.BlockSpec(shape, lambda g, i: (0,) * len(shape))


def shaped(shape, dtype=F32):
    return jax.ShapeDtypeStruct(shape, dtype)


def run(kernel, grid, ins, outs, scratch, flops, moved, after=()):
    count = len(ins)
    extra = list(after)

    def body(*refs):
        kernel(*refs[:count], *refs[count + len(extra) :])

    steps = grid[0] * grid[1]
    return pl.pallas_call(
        body,
        grid=grid,
        in_specs=[spec for _, spec in ins] + [pl.BlockSpec(memory_space=pl.ANY)] * len(extra),
        out_specs=[spec for _, spec in outs],
        out_shape=[shape for shape, _ in outs],
        scratch_shapes=scratch,
        compiler_params=pltpu.CompilerParams(
            dimension_semantics=("arbitrary", "arbitrary"), vmem_limit_bytes=VMEM_BYTES
        ),
        cost_estimate=pl.CostEstimate(
            flops=steps * flops, bytes_accessed=steps * moved, transcendentals=0
        ),
    )(*[array for array, _ in ins], *extra)


def local_states(xw, halo, taps, heads, spread, after):
    groups, length, _ = xw.shape
    inner = spread.shape[1]
    width = inner + 2 * LANES
    return run(
        state_kernel,
        (groups, length // CHUNK),
        [
            (xw, flat(width)),
            (halo, whole(RIM, width)),
            (xw, flat(LANES, column=width // LANES)),
            (taps, fixed(taps.shape)),
            (heads, fixed(heads.shape)),
            (spread, fixed(spread.shape)),
        ],
        [
            (shaped((groups, length, width), BF16), flat(width)),
            (shaped((groups, length, LANES)), flat(LANES)),
            (shaped((groups, length, LANES)), flat(LANES)),
            (shaped((groups, LANES, inner)), whole(LANES, inner)),
            (shaped((groups, 8, LANES)), whole(8, LANES)),
            (shaped((groups, LANES + RIM, inner), BF16), whole(LANES + RIM, inner)),
        ],
        [pltpu.VMEM((RIM + CHUNK, width), F32)],
        1_500_000_000,
        2_000_000,
        after,
    )


def mixer(xbc, cumul, dt, start, gate, gm, rows, spread, after):
    groups, length, width = xbc.shape
    inner = spread.shape[1]
    chunks = length // CHUNK
    return run(
        scan_kernel,
        (groups, chunks),
        [
            (xbc, flat(width)),
            (cumul, flat(LANES)),
            (dt, flat(LANES)),
            (start[0], whole(LANES + RIM, inner)),
            (start[1], whole(LANES, inner)),
            (start[2], whole(LANES, inner)),
            (gate, flat(inner)),
            (gm, flat(inner)),
            (rows, fixed(rows.shape)),
            (spread, fixed(spread.shape)),
        ],
        [
            (shaped((groups, length, inner)), flat(inner)),
            (shaped(gate.shape, BF16), flat(inner)),
            (
                shaped((groups, chunks, LANES, inner), BF16),
                pl.BlockSpec((1, 1, LANES, inner), lambda g, i: (g, i, 0, 0)),
            ),
            (shaped((groups, 8, length)), pl.BlockSpec((1, 8, CHUNK), lambda g, i: (g, 0, i))),
        ],
        [pltpu.VMEM((LANES, inner), F32)],
        2_500_000_000,
        4_000_000,
        after,
    )


def gate_back(inner_full, y, xbc, gate, gm, stats, cumul, total, rows, spread, after):
    groups, length, width = xbc.shape
    inner = spread.shape[1]
    chunks = length // CHUNK
    back = lambda i: chunks - 1 - i
    return run(
        functools.partial(gate_kernel, float(inner_full)),
        (groups, chunks),
        [
            (y, flat(inner, back)),
            (xbc, flat(width, back)),
            (gate, flat(inner, back)),
            (gm, flat(inner, back)),
            (stats, pl.BlockSpec((1, 8, CHUNK), lambda g, i: (g, 0, back(i)))),
            (cumul, flat(LANES, back)),
            (total, whole(8, LANES)),
            (rows, fixed(rows.shape)),
            (spread, fixed(spread.shape)),
        ],
        [
            (shaped((groups, length, inner), BF16), flat(inner, back)),
            (shaped(gate.shape, BF16), flat(inner, back)),
            (shaped(gate.shape, BF16), flat(inner, back)),
            (shaped((groups, LANES, inner)), whole(LANES, inner)),
            (shaped((8, inner)), fixed((8, inner))),
            (shaped((groups, LANES + RIM, inner), BF16), whole(LANES + RIM, inner)),
        ],
        [],
        1_500_000_000,
        4_500_000,
        after,
    )


def adjoint(xbc, cumul, dt, gy, y, enter, gin, xw, halo, taps, heads, rows, spread, after):
    groups, length, width = xbc.shape
    inner = spread.shape[1]
    chunks = length // CHUNK
    back = lambda i: chunks - 1 - i
    per = CHUNK // RIM
    return run(
        adjoint_kernel,
        (groups, chunks),
        [
            (xbc, flat(width, back)),
            (cumul, flat(LANES, back)),
            (dt, flat(LANES, back)),
            (gy, flat(inner, back)),
            (y, flat(inner, back)),
            (enter, pl.BlockSpec((1, 1, LANES, inner), lambda g, i: (g, back(i), 0, 0))),
            (gin[0], whole(LANES + RIM, inner)),
            (gin[1], whole(LANES, inner)),
            (gin[2], whole(LANES, inner)),
            (xw, flat(width, back)),
            (
                xw,
                pl.BlockSpec(
                    (1, RIM, width), lambda g, i: (g, jnp.maximum(back(i) * per - 1, 0), 0)
                ),
            ),
            (halo, whole(RIM, width)),
            (xw, flat(LANES, back, width // LANES)),
            (taps, fixed(taps.shape)),
            (heads, fixed(heads.shape)),
            (rows, fixed(rows.shape)),
            (spread, fixed(spread.shape)),
        ],
        [
            (shaped((groups, length, width + LANES), BF16), flat(width + LANES, back)),
            (shaped((groups, 8, width)), whole(8, width)),
            (shaped((8, width)), fixed((8, width))),
            (shaped((8, LANES)), fixed((8, LANES))),
            (shaped((8, inner)), fixed((8, inner))),
        ],
        [
            pltpu.VMEM((LANES, inner), F32),
            pltpu.VMEM((RIM + CHUNK, width), F32),
            pltpu.VMEM((CHUNK + 8, width), F32),
            pltpu.VMEM((CHUNK, CHUNK), F32),
        ],
        8_000_000_000,
        6_000_000,
        after,
    )


def leave(ends, totals, packed, spread):
    groups, states, inner = ends.shape

    def one(*shape):
        return pl.BlockSpec((1,) + shape, lambda g: (g,) + (0,) * len(shape))

    return pl.pallas_call(
        leave_kernel,
        grid=(groups,),
        in_specs=[
            one(states, inner), one(8, LANES), one(states + RIM, inner),
            pl.BlockSpec(spread.shape, lambda g: (0, 0)),
        ],
        out_specs=one(states, inner),
        out_shape=shaped(ends.shape, BF16),
        compiler_params=pltpu.CompilerParams(
            dimension_semantics=("arbitrary",), vmem_limit_bytes=VMEM_BYTES
        ),
        cost_estimate=pl.CostEstimate(
            flops=0, bytes_accessed=8 * groups * states * inner, transcendentals=0
        ),
    )(ends, totals, packed, spread)


def place_kernel(at_ref, first, first_y, second, second_x, full_ref):
    step = pl.program_id(0)
    for number, ref in enumerate((first, first_y, second, second_x)):

        @pl.when(step // 2 == number)
        def _(ref=ref):
            full_ref[0, 0, 0] = ref[0]


def place_row(number, step, at):
    x, core, y = at[0], at[1], at[2]
    later = number // 2
    side = number % 2
    row = x + jnp.where(later == 0, step, side)
    column = y + jnp.where(later == 0, side, step)
    return row % 2, jnp.where(later == 0, core, 1 - core), column % 2, 0, 0


def place(first, first_y, second, second_x):
    _, rows, columns = first.shape
    at = jnp.stack([lax.axis_index(name) for name in ("x", "core", "y")]).astype(jnp.int32)

    def piece(number):
        return pl.BlockSpec(
            (1, rows, columns), lambda i, at: (jnp.clip(i - 2 * number, 0, 1), 0, 0)
        )

    full = pl.pallas_call(
        place_kernel,
        grid_spec=pltpu.PrefetchScalarGridSpec(
            num_scalar_prefetch=1,
            grid=(8,),
            in_specs=[piece(number) for number in range(4)],
            out_specs=pl.BlockSpec(
                (1, 1, 1, rows, columns), lambda i, at: place_row(i // 2, i % 2, at)
            ),
        ),
        out_shape=shaped((2, 2, 2, rows, columns), first.dtype),
        compiler_params=pltpu.CompilerParams(
            dimension_semantics=("arbitrary",), vmem_limit_bytes=VMEM_BYTES
        ),
        cost_estimate=pl.CostEstimate(
            flops=0, bytes_accessed=rows * columns, transcendentals=0
        ),
    )(at, first, first_y, second, second_x)
    return full.reshape(8 * rows, columns)


def join_kernel(at_ref, own, got, far_own, far_got, full_ref):
    half_is_own = pl.program_id(1) == at_ref[0]
    for core, (mine, other) in enumerate(((own, got), (far_own, far_got))):
        for ref, wanted in ((mine, half_is_own), (other, ~half_is_own)):

            @pl.when(wanted & (pl.program_id(0) == core))
            def _(ref=ref):
                full_ref[0] = ref[...]


def joined(own, got, far_own, far_got, part=0):
    _, rows, columns = own.shape
    at = lax.axis_index("zq").astype(jnp.int32)[None]
    piece = pl.BlockSpec((None, rows, columns), lambda c, h, at: (part, 0, 0))
    return pl.pallas_call(
        join_kernel,
        grid_spec=pltpu.PrefetchScalarGridSpec(
            num_scalar_prefetch=1,
            grid=(2, 2),
            in_specs=[piece] * 4,
            out_specs=pl.BlockSpec((1, rows, columns), lambda c, h, at: (c, h, 0)),
        ),
        out_shape=shaped((2, 2 * rows, columns), own.dtype),
        compiler_params=pltpu.CompilerParams(
            dimension_semantics=("arbitrary", "arbitrary"), vmem_limit_bytes=VMEM_BYTES
        ),
        cost_estimate=pl.CostEstimate(
            flops=0, bytes_accessed=16 * rows * columns, transcendentals=0
        ),
    )(at, own, got, far_own, far_got)


def swap(value, axis):
    return lax.ppermute(value, axis, [(0, 1), (1, 0)])


def sum_axis(value, axis):
    if lax.axis_size(axis) == 2:
        return value + swap(value, axis)
    return lax.psum(value, axis)


def cut(value, axis, dim):
    size = value.shape[dim] // 2
    at = lax.axis_index(axis)
    kept = lax.dynamic_slice_in_dim(value, at * size, size, dim)
    return kept, lax.dynamic_slice_in_dim(value, (1 - at) * size, size, dim)


def added(kept, got, dtype=BF16):
    return (kept.astype(F32) + got.astype(F32)).astype(dtype)


def hold(value, *before):
    if not before:
        return value
    return lax.optimization_barrier((value,) + before)[0]


def shift(value, by):
    blocks = lax.axis_size(("y", "zp"))
    pairs = [(i, i + by) for i in range(blocks) if 0 <= i + by < blocks]
    return lax.ppermute(value, ("y", "zp"), pairs)


def row_hop(packed, way, *before):
    return hold(lax.ppermute(packed, "zp", [(0, 1)] if way == 1 else [(1, 0)]), *before)


def column_hops(leaving, way, *before):
    source = 1 if way == 1 else 2
    pairs = [[(source, source + way * (1 + to))] for to in range(2)]
    return [hold(lax.ppermute(leaving, ("y", "zp"), pair), *before) for pair in pairs]


def chained(packed, way):
    blocks = lax.axis_size(("y", "zp"))
    groups, _, inner = packed.shape
    heads = inner // (LANES // 2)
    entering = jnp.zeros((groups, LANES, inner), F32)
    passed = jnp.zeros((groups, 1, LANES), F32)
    for by in range(1, blocks):
        got = shift(packed, by * way).astype(F32)
        weight = jnp.repeat(jnp.exp(passed[:, :, 0:heads]), LANES // 2, axis=2)
        entering = entering + weight * got[:, 0:LANES]
        passed = passed + jnp.sum(got[:, LANES:, 0:LANES], axis=1, keepdims=True)
    none = jnp.zeros(entering.shape, BF16)
    return jnp.pad(entering.astype(BF16), ((0, 0), (0, RIM), (0, 0))), none, none


def all_pairs():
    return all(lax.axis_size(name) == 2 for name in ("x", "y", "zp"))


NEAR = [(0, 1), (3, 2), (1, 3), (2, 0)]
FAR = [(1, 2), (2, 1)]
HOME = [(to, source) for source, to in NEAR]


def fetched(piece, near, far):
    at_home = lax.axis_index("core") == lax.axis_index("zp")
    return jnp.where(at_home, piece, near), jnp.where(at_home, near, far)


def fetch(piece):
    return lax.ppermute(piece, ("core", "zp"), NEAR), lax.ppermute(piece, ("core", "zp"), FAR)


def gather_slice(piece):
    owners = lax.axis_size("zp")
    rows = lax.all_gather(piece, ("x", "core", "y"), axis=0, tiled=True)
    parts = lax.all_gather(rows, "zp")
    return lax.dynamic_slice_in_dim(parts, lax.axis_index("core") * (owners // 2), owners // 2, 0)


def reduce_slice(parts):
    owners = lax.axis_size("zp")
    full = jnp.zeros((owners,) + parts.shape[1:], parts.dtype)
    full = lax.dynamic_update_slice_in_dim(
        full, parts, lax.axis_index("core") * (owners // 2), axis=0
    )
    mine = lax.psum_scatter(full, "zp", scatter_dimension=0, tiled=True)[0]
    mine = lax.psum_scatter(mine, ("x", "core", "y"), scatter_dimension=0, tiled=True)
    return mine.astype(F32)


def cut_rows(fulls):
    core = lax.axis_index("core")
    same, cross = [], []
    for full in fulls:
        rows, columns = full.shape[0] // 8, full.shape[1]
        full = full.reshape(2, 2, 2, rows, columns)
        same.append(cut(lax.dynamic_index_in_dim(full, core, 1, False), "x", 0))
        cross.append(cut(lax.dynamic_index_in_dim(full, 1 - core, 1, False), "y", 1))
    return (
        [kept[0] for kept, _ in same],
        [kept[:, 0] for kept, _ in cross],
        jnp.stack([sent[0] for _, sent in same]),
        jnp.stack([sent[:, 0] for _, sent in cross]),
    )


def cut_again(sames, crosses):
    same = [cut(value, "y", 0) for value in sames]
    cross = [cut(value, "x", 0) for value in crosses]
    return (
        [kept[0] for kept, _ in same],
        [kept[0] for kept, _ in cross],
        jnp.stack([sent[0] for _, sent in same]),
        jnp.stack([sent[0] for _, sent in cross]),
    )


def both(kept, got):
    return [
        [added(mine, other[k]) for k, mine in enumerate(values)]
        for values, other in zip(kept[0:2], got)
    ]


def home_parts(sames, crosses):
    at_home = lax.axis_index("core") == lax.axis_index("zp")
    cross = jnp.stack(crosses)
    return jnp.where(at_home, cross, jnp.stack(sames)), cross


def at_owner(near, far, sames):
    at_home = lax.axis_index("core") == lax.axis_index("zp")
    return [
        near[k].astype(F32) + jnp.where(at_home, same.astype(F32), far[k].astype(F32))
        for k, same in enumerate(sames)
    ]


def go_home(sent):
    return (
        lax.ppermute(sent[0], ("core", "zp"), HOME),
        lax.ppermute(sent[1], ("core", "zp"), FAR),
    )


def own_of_slice(value):
    owners = lax.axis_size("zp")
    core, part = lax.axis_index("core"), lax.axis_index("zp")
    other = swap(value, "core")
    share = value.shape[-1] // (owners // 2)
    wanted = jnp.where(part // (owners // 2) == core, value, other)
    return lax.dynamic_slice_in_dim(wanted, (part % (owners // 2)) * share, share, value.ndim - 1)


def slice_of_own(value, after):
    owners = lax.axis_size("zp")
    core = lax.axis_index("core")
    if owners == 2:
        other = hold(swap(value, "zp"), after)
        return jnp.where(core == lax.axis_index("zp"), value, other)[None]
    parts = lax.all_gather(value, "zp")
    return lax.dynamic_slice_in_dim(parts, core * (owners // 2), owners // 2, 0)


def per_device(
    hidden,
    cotangent,
    norm_gain,
    w_z,
    w_x,
    w_bc,
    w_dt,
    conv_x,
    conv_x_bias,
    conv_bc,
    conv_bc_bias,
    dt_bias,
    a_log,
    d_skip,
    inner_gain,
    w_out,
):
    micro, own_len, model = hidden.shape
    owners = lax.axis_size("zp")
    share = w_x.shape[1]
    own_heads = w_dt.shape[1]
    inner_full = share * 2 * owners
    states2 = w_bc.shape[1]
    halves = owners // 2
    inner = share * halves
    heads = own_heads * halves
    head_width = inner // heads
    width = inner + states2

    def matmul(left, right, contract, dtype=F32):
        return lax.dot_general(
            left, right, (contract, ((), ())), preferred_element_type=F32
        ).astype(dtype)

    def spliced(parts, sizes):
        if halves == 1:
            return parts[0]
        columns, at = [], 0
        for size, copies in sizes:
            columns += [parts[k][:, at : at + size] for k in range(halves if copies else 1)]
            at += size
        return jnp.concatenate(columns, axis=1)

    parts = range(micro)

    own = hidden.astype(F32)
    gain_in = norm_gain.astype(F32)
    r0 = lax.rsqrt(jnp.mean(own * own, axis=-1, keepdims=True) + EPS)
    filler = LANES // halves - own_heads
    own_first = jnp.concatenate(
        [w_x, w_bc, w_dt, jnp.zeros((w_dt.shape[0], filler), BF16)], axis=1
    )
    own_second = jnp.concatenate([w_z, jnp.transpose(w_out)], axis=1)
    normed_own = [(own[part : part + 1] * r0[part : part + 1] * gain_in).astype(BF16) for part in parts]
    fast = all_pairs()

    def tokens_of(value, *before):
        got = hold(swap(value, "zq"), *before)
        return value, got, swap(value, "core"), swap(got, "core")

    if fast:
        got = fetch(own_first)
    fours = [tokens_of(normed_own[0])]
    if fast:
        same, cross = fetched(own_first, *got)
        moved = hold((swap(same, "x"), swap(cross, "y")), fours[0][1])
        first, second = jnp.stack([same, moved[0]]), jnp.stack([cross, moved[1]])
        own_second = hold(own_second, fours[0][1], *moved)
        got = fetch(own_second)
        rest = swap(first, "y"), swap(second, "x")
        later = first, second
    else:
        later = (fours[0][1],)
    for part in parts[1:]:
        fours.append(tokens_of(hold(normed_own[part], fours[0][1]), *later))
        later = (fours[-1][1],)
    if fast:
        w_first = place(first, rest[0], second, rest[1])
        got = hold(got, w_first)
        same, cross = fetched(own_second, *got)
        moved = swap(same, "x"), swap(cross, "y")
    else:
        w_first = spliced(
            gather_slice(own_first), ((share, 1), (states2, 0), (own_heads, 1), (filler, 1))
        )
    normed = [joined(*four) for four in fours]
    per_head = jnp.concatenate([dt_bias, a_log, d_skip])
    per_head = jnp.pad(per_head, (0, share - 3 * own_heads))
    small = jnp.concatenate([conv_x, conv_x_bias[None], inner_gain[None]], axis=0).astype(F32)
    small = jnp.concatenate([small, per_head[None], jnp.zeros((1, share), F32)])
    small = slice_of_own(small, w_first)
    channel_rows = jnp.concatenate([small[k, 0:6] for k in range(halves)], axis=1)
    head_rows = jnp.concatenate(
        [small[k, 6, 0 : 3 * own_heads].reshape(3, own_heads) for k in range(halves)], axis=1
    )
    conv_shared = jnp.concatenate([conv_bc, conv_bc_bias[None]], axis=0).astype(F32)
    taps = jnp.pad(jnp.concatenate([channel_rows[0:5], conv_shared], axis=1), ((0, 3), (0, 0)))
    head_in = jnp.stack([head_rows[0], -jnp.exp(head_rows[1]), jnp.ones((heads,), F32)])
    head_in = jnp.pad(head_in, ((0, 5), (0, LANES - heads)))
    rows = jnp.stack([jnp.repeat(head_rows[2], head_width), channel_rows[5]])
    rows = jnp.pad(rows, ((0, 6), (0, 0)))
    spread = (
        lax.broadcasted_iota(jnp.int32, (LANES, inner), 1) // head_width
        == lax.broadcasted_iota(jnp.int32, (LANES, inner), 0)
    ).astype(BF16)

    scans = []
    for part in parts:
        xw = matmul(normed[part], w_first, ((2,), (0,)), BF16)
        scans.append((xw, shift(xw[:, -RIM:, 0:width], 1)))
        if part == 0:
            normed[-1] = hold(normed[-1], xw)
    if fast:
        moved = hold(moved, scans[0][0])
        first, second = jnp.stack([same, moved[0]]), jnp.stack([cross, moved[1]])
        got_second = first, swap(first, "y"), second, swap(second, "x")
    local = []
    for part in parts:
        before = [k[5] for k in local[-1:]]
        local.append(local_states(*scans[part], taps, head_in, spread, before))
        if part == 0:
            cot_own = hold(cotangent, local[0][5], scans[-1][1])
            cot_own = [cot_own[k : k + 1] for k in parts]
            cot_got = [swap(value, "zq") for value in cot_own]
    totals = [local[part][4] for part in parts]
    packed = [local[part][5] for part in parts]
    if fast:
        w_second = place(*hold(got_second, packed[-1]))
    else:
        w_second = spliced(
            gather_slice(hold(own_second, packed[-1])), ((share, 1), (share, 1))
        )
    w_gate, w_down = w_second[:, 0:inner], w_second[:, inner:]
    def hop(part, packed, ends, way, *before):
        if not fast:
            return packed, packed
        got = row_hop(packed, way, *before)
        return got, leave(ends, totals[part], got, spread)

    def entering(found, way, *before):
        if not fast:
            return chained(found[0], way)
        return found[0], *column_hops(found[1], way, *before)

    found = [hop(0, packed[0], local[0][3], 1, w_second)]
    gate = [
        matmul(hold(normed[part], found[0][1]), w_gate, ((2,), (0,)), BF16) for part in parts
    ]
    cot_far = (
        swap(hold(cotangent, local[0][5]), "core"),
        [swap(hold(cot_got[k], gate[k]), "core") for k in parts],
    )

    def whole_cot(part, *before):
        far = hold((cot_far[0], cot_far[1][part]), *before)
        return joined(cot_own[part], cot_got[part], far[0][part : part + 1], far[1])

    cot = [whole_cot(0, gate[-1])]

    w_down_held = hold(w_down, found[0][1])
    gm = [matmul(cot[0], w_down_held, ((2,), (0,)))]
    mixes, stats, branches, gates = [], [], [], []
    g_gate = g_down = 0.0
    tokens = ((0, 1), (0, 1))
    for part in parts:
        xbc, cumul, dt = local[part][0:3]
        before = (gm[0],) if part == 0 else (gates[part - 1][5], gm[part])
        start = entering(found[part], 1, *before)
        y, gained, enter, stat = mixer(xbc, cumul, dt, start, gate[part], gm[part], rows, spread, before)
        mixes.append((y, enter))
        other = swap(stat, "core")
        if part + 1 < micro:
            following = hold(packed[part + 1], found[part][1])
            found.append(hop(part + 1, following, local[part + 1][3], 1, y))
            cot.append(whole_cot(part + 1, found[-1][1]))
            gm.append(matmul(cot[-1], w_down, ((2,), (0,))))
            other = hold(other, cot[-1])
        else:
            g_gate = matmul(normed[0], hold(gates[0][1], y), tokens)
            other = hold(other, g_gate)
        stat = stat + jnp.flip(other, 0)
        other = swap(stat, "zq")
        branch = matmul(hold(gained, stat, gm[-1]), w_down, ((2,), (1,)), BF16)
        stats.append(stat + hold(other, branch))
        branches.append((branch, swap(branch[1], "core")))
        gates.append(
            gate_back(
                inner_full, y, xbc, gate[part], gm[part], stats[part], cumul, totals[part],
                rows, spread, [branch],
            )
        )
    back_packed = [g[5] for g in gates]

    found = [hop(0, back_packed[0], gates[0][3], -1, back_packed[-1])]
    for part in parts:
        g_down = g_down + matmul(cot[part], hold(gates[part][2], found[0][1]), tokens)
        if part == 0:
            branch_cut = [
                cut(added(branch[0], hold(got, g_down)), "zq", 0) for branch, got in branches
            ]
            branch_sent = jnp.stack([sent for _, sent in branch_cut])
            branch_got = swap(branch_sent, "zq")
        else:
            g_gate = g_gate + matmul(normed[part], hold(gates[part][1], g_down), tokens)
    g_gate, g_down = g_gate.astype(BF16), g_down.astype(BF16)
    g_normed_gate = [matmul(hold(gates[0][1], g_gate), w_gate, ((2,), (1,)))]
    gin = entering(found[0], -1, g_normed_gate[0])
    for part in parts[1:]:
        following = hold(back_packed[part], found[part - 1][1])
        found.append(hop(part, following, gates[part][3], -1, g_normed_gate[0]))
    wait_for = [found[-1][1], branch_sent]
    if fast:
        second = cut_rows(hold([g_gate, g_down], *gin))
        moved = swap(second[2], "x"), swap(second[3], "y")
        wait_for += second[2:]

    g_first, heads_out, g_hidden, g_norm_gain = 0.0, [], [], 0.0

    def token_grad(part, kept, got):
        x, r, g = own[part], r0[part], added(kept, got, F32)
        q0 = g * gain_in
        grad = (
            cotangent[part].astype(F32) + r * q0
            - x * (r * r * r) * jnp.mean(q0 * x, axis=-1, keepdims=True)
        )
        return grad, jnp.sum(g * x * r, axis=0)

    def whole_output(*before):
        outputs = []
        for part in parts:
            square = lax.dynamic_slice_in_dim(
                stats[part][0, 0], lax.axis_index("zq") * own_len, own_len, 0
            )
            r1 = lax.rsqrt(square / inner_full + EPS)[:, None]
            got = hold(branch_got, *before)[part]
            outputs.append((own[part] + r1 * added(branch_cut[part][0], got, F32)).astype(BF16))
        return jnp.stack(outputs)

    for part in parts:
        xbc, cumul, dt = local[part][0:3]
        gmix, rim, *sums = adjoint(
            xbc, cumul, dt, gates[part][0], mixes[part][0], mixes[part][1], gin,
            *scans[part], taps, head_in, rows, spread, wait_for,
        )
        if part == micro - 1 and fast and micro > 1:
            got_home = hold(got_home, gmix)
            g_gate, g_down = at_owner(*got_home, pair[0])
            rim = hold(rim, g_gate, g_down)
        if part < micro - 1:
            gin = entering(found[part + 1], -1)
            gmix, rim, *sums = hold(
                (gmix, rim, *sums), *gin, branch_got, *(moved if fast else ())
            )
        heads_out.append(sums)
        ahead = shift(rim, -1)
        last_part = part == micro - 1
        if last_part:
            if micro > 1:
                kept, got = norm_cut
                grad, gain = token_grad(part - 1, kept, hold(got, gmix))
                g_hidden.append(grad)
                g_norm_gain = g_norm_gain + gain
                ahead = hold(ahead, grad)
        else:
            if fast:
                moved = hold(moved, gmix)
                second = cut_again(*both(second, moved))
                moved = swap(second[2], "y"), swap(second[3], "x")
        fix = jnp.stack(
            [sum(taps[k, :] * ahead[:, r - k] for k in range(r + 1)) for r in range(3)], axis=1
        )
        length = gmix.shape[1]
        last = gmix[:, length - RIM :].astype(F32)
        last = last + jnp.pad(fix, ((0, 0), (RIM - 3, 0), (0, LANES)))
        gmix = lax.dynamic_update_slice_in_dim(gmix, last.astype(BF16), length - RIM, 1)

        def for_weights(gmix):
            return g_first + matmul(normed[part], gmix, tokens)

        def for_tokens(gmix):
            total = g_normed_gate[part] + matmul(gmix, w_first, ((2,), (1,)))
            return total.astype(BF16)

        total = for_tokens(gmix)
        other = swap(total[1], "core")
        g_first = for_weights(hold(gmix, total))
        if last_part:
            g_first = g_first.astype(BF16)
            if fast:
                first = cut_rows([g_first])
                moved_first = swap(first[2], "x"), swap(first[3], "y")
        else:
            g_normed_gate.append(
                matmul(hold(gates[part + 1][1], g_first), w_gate, ((2,), (1,)))
            )
            kept, sent = cut(added(total[0], hold(other, g_first)), "zq", 0)
            norm_cut = kept, swap(sent, "zq")
            if part == micro - 2:
                outputs = whole_output(g_normed_gate[-1], sent)
            gin = hold(gin, outputs)
            wait_for = [sent, outputs]
            if fast and part == micro - 2:
                moved = hold(moved, g_normed_gate[-1])
                pair = both(second, moved)
                home = home_parts(*pair)
                wait_for += home
                got_home = go_home(home)

    kept, sent = cut(added(total[0], hold(other, g_first, *(first[2:] if fast else ()))), "zq", 0)
    got_norm = swap(sent, "zq")
    if fast:
        first = cut_again(*both(first, hold(moved_first, sent)))
        moved = swap(first[2], "y"), swap(first[3], "x")
        got_norm = hold(got_norm, *first[2:])
        pair = both(first, hold(moved, got_norm))
        home = home_parts(*pair)
        got_home = go_home(home)
        grad, gain = token_grad(micro - 1, kept, hold(got_norm, *home))
        g_first = at_owner(*hold(got_home, grad), pair[0])[0]
    else:
        g_gate, g_down = [
            reduce_slice(jnp.stack(jnp.split(value, halves, axis=1))) for value in (g_gate.astype(BF16), g_down.astype(BF16))
        ]
        grad, gain = token_grad(micro - 1, kept, got_norm)
        g_first = reduce_slice(
            jnp.concatenate(
                [
                    jnp.stack(jnp.split(g_first[:, 0:inner], halves, axis=1)),
                    jnp.concatenate(
                        [
                            g_first[None, :, inner:width],
                            jnp.zeros((halves - 1, model, states2), BF16),
                        ]
                    ),
                    jnp.stack(jnp.split(g_first[:, width : width + heads], halves, axis=1)),
                ],
                axis=2,
            )
        )
    g_hidden = jnp.stack(g_hidden + [grad])
    g_norm_gain = g_norm_gain + gain
    g_bc = g_first[:, share : share + states2]
    if fast:
        across = lax.ppermute(g_bc, ("zp", "zq"), [(0, 3), (3, 0), (1, 2), (2, 1)])
        g_bc = (g_bc + swap(g_bc, "zq")) + (swap(g_bc, "zp") + across)
    else:
        g_bc = sum_axis(sum_axis(g_bc, "zp"), "zq")

    g_taps, g_heads, g_skip = (sum(b[k] for b in heads_out) for k in range(3))
    g_gain = sum(g[4] for g in gates)
    skip_heads = jnp.sum(g_skip[0].reshape(heads, head_width), axis=1)
    small = jnp.concatenate(
        [g_taps[0:5, 0:inner].reshape(-1), g_gain[0], g_heads[0, 0:heads], g_heads[1, 0:heads], skip_heads]
    )
    size = small.shape[0]
    packed = jnp.concatenate([small, g_taps[0:5, inner:width].reshape(-1), g_norm_gain])
    packed = sum_axis(sum_axis(packed, "x"), "y")
    packed = sum_axis(hold(packed, g_first), "zp")
    small = packed[:size]
    shared = sum_axis(sum_axis(packed[size:], "core"), "zq")
    bc_rows = shared[0 : 5 * states2].reshape(5, states2)
    channel = own_of_slice(small[0 : 6 * inner].reshape(6, inner))
    per_head = own_of_slice(small[6 * inner :].reshape(3, heads))
    return (
        outputs,
        g_hidden,
        shared[5 * states2 :],
        g_gate,
        g_first[:, 0:share],
        g_bc,
        g_first[:, share + states2 : share + states2 + own_heads],
        channel[0:4],
        channel[4],
        bc_rows[0:4],
        bc_rows[4],
        per_head[0],
        per_head[1],
        per_head[2],
        channel[5],
        jnp.transpose(g_down),
    )


def solution(mesh):
    dp, seq, tensor = (mesh.shape[name] for name in ("dp", "seq", "tensor"))
    fine = Mesh(
        mesh.devices.reshape(dp // 2, 2, seq, tensor // 2, 2), ("x", "core", "y", "zp", "zq")
    )
    data, tens = ("x", "core", "y"), ("zp", "zq")
    tokens = P(("x", "core"), ("y", "zp", "zq"), None)
    params = (
        P(),
        P(data, tens),
        P(data, tens),
        P(data, None),
        P(data, tens),
        P(None, tens),
        P(tens),
        P(),
        P(),
        P(tens),
        P(tens),
        P(tens),
        P(tens),
        P(tens, data),
    )
    return jax.shard_map(
        per_device,
        mesh=fine,
        in_specs=(tokens, tokens) + params,
        out_specs=(tokens, tokens) + params,
        check_vma=False,
    )
```

```python
import functools

import jax
import jax.numpy as jnp
from jax import lax
from jax.experimental import pallas as pl
from jax.experimental.pallas import tpu as pltpu
from jax.sharding import Mesh
from jax.sharding import PartitionSpec as P

CHUNK = 256
HALF = CHUNK // 2
LANES = 128
STRIP = 256
RIM = 16
EPS = 1e-05
F32 = jnp.float32
BF16 = jnp.bfloat16
VMEM_BYTES = 48 * 1024 * 1024


def dot(left, right):
    return lax.dot_general(left, right, (((1,), (0,)), ((), ())), preferred_element_type=F32)


def dot_nt(left, right):
    return lax.dot_general(left, right, (((1,), (1,)), ((), ())), preferred_element_type=F32)


def pieces(value, count):
    terms = []
    for _ in range(count):
        term = value.astype(BF16)
        terms.append(term)
        value = value - term.astype(F32)
    return terms


def spread_heads(value, spread):
    return sum(dot(term, spread) for term in pieces(value, 2))


def gather_heads(value, collect):
    return sum(dot(term, collect) for term in pieces(value, 2))


def lane_sums(value):
    folded = sum(value[:, at : at + LANES] for at in range(0, value.shape[1], LANES))
    return jnp.sum(jnp.transpose(folded), axis=0, keepdims=True)


def running_sum(value, mask):
    return sum(dot(mask, term) for term in pieces(value, 3))


def iota2(rows, cols, dim):
    return lax.broadcasted_iota(jnp.int32, (rows, cols), dim)


def turned(value):
    return jnp.transpose(value.astype(F32)).astype(BF16)


def strips(width):
    return [slice(at, at + STRIP) for at in range(0, width, STRIP)]


def conv_pre(ext, taps, cols):
    total = taps[4:5, cols] + taps[0:1, cols] * ext[pl.ds(RIM - 3, CHUNK), cols]
    for k in range(1, 4):
        total = total + taps[k : k + 1, cols] * ext[pl.ds(RIM - 3 + k, CHUNK), cols]
    return total


def softplus(value):
    return jnp.maximum(value, 0.0) + jnp.log1p(jnp.exp(-jnp.abs(value)))


def write_packed(packed_ref, end, total):
    packed_ref[0, 0:LANES, :] = end.astype(BF16)
    packed_ref[0, LANES:, :] = jnp.zeros((RIM, end.shape[1]), BF16)
    row = iota2(RIM, LANES, 0)
    logs = jnp.zeros((RIM, LANES), F32)
    for k, term in enumerate(pieces(total, 3)):
        logs = jnp.where(row == k, term.astype(F32), logs)
    packed_ref[0, LANES:, 0:LANES] = logs.astype(BF16)


def widened(log, spread):
    return spread_heads(jnp.broadcast_to(jnp.exp(log), (8, LANES)), spread)[0:1, :]


def entering_state(packed_ref, first_ref, second_ref, spread_ref):
    passed = jnp.sum(packed_ref[0, LANES:, 0:LANES].astype(F32), axis=0, keepdims=True)
    from_row = first_ref[0].astype(F32) + second_ref[0].astype(F32)
    return packed_ref[0, 0:LANES, :].astype(F32) + widened(passed, spread_ref[...]) * from_row


def leave_kernel(end_ref, total_ref, packed_ref, spread_ref, leaving_ref):
    kept = packed_ref[0, 0:LANES, :].astype(F32) * widened(total_ref[0, 0:1, :], spread_ref[...])
    leaving_ref[0] = (end_ref[0] + kept).astype(BF16)


def state_kernel(
    mix_ref, halo_ref, step_ref, taps_ref, heads_ref, spread_ref,
    xbc_ref, sum_ref, dt_ref, end_ref, total_ref, packed_ref, ext,
):
    inner = spread_ref.shape[1]
    place = pl.program_id(1)

    @pl.when(place == 0)
    def _():
        ext[0:RIM, :] = halo_ref[0].astype(F32)
        end_ref[...] = jnp.zeros_like(end_ref)
        total_ref[...] = jnp.zeros_like(total_ref)

    @pl.when(place > 0)
    def _():
        ext[0:RIM, :] = ext[CHUNK : CHUNK + RIM, :]

    dt = softplus(step_ref[0].astype(F32) + heads_ref[0:1, :])
    lower = (iota2(CHUNK, CHUNK, 0) >= iota2(CHUNK, CHUNK, 1)).astype(F32).astype(BF16)
    cumul = running_sum(dt * heads_ref[1:2, :], lower)
    sum_ref[0] = cumul
    dt_ref[0] = dt
    last = cumul[CHUNK - 1 : CHUNK, :]
    total_ref[0] += jnp.broadcast_to(last, total_ref.shape[1:])
    tail = jnp.exp(last - cumul) * dt
    decay = jnp.broadcast_to(jnp.exp(last), (8, LANES))
    b_turned = None
    for cols in reversed(strips(xbc_ref.shape[2])):
        ext[RIM:, cols] = mix_ref[0, :, cols].astype(F32)
        pre = conv_pre(ext, taps_ref, cols)
        act = (pre * jax.nn.sigmoid(pre)).astype(BF16)
        xbc_ref[0, :, cols] = act
        if cols.start >= inner:
            b_turned = turned(act[:, 0:LANES])
        else:
            held = spread_ref[:, cols]
            weighted = (act.astype(F32) * spread_heads(tail, held)).astype(BF16)
            kept = end_ref[0, :, cols] * spread_heads(decay, held)[0:1, :]
            end_ref[0, :, cols] = kept + dot(b_turned, weighted)

    @pl.when(place == pl.num_programs(1) - 1)
    def _():
        write_packed(packed_ref, end_ref[0], total_ref[0, 0:1, :])


def scan_kernel(
    xbc_ref, sum_ref, dt_ref, packed_ref, first_ref, second_ref, gate_ref, gm_ref, rows_ref, spread_ref,
    y_ref, mixed_ref, enter_ref, stat_ref, state,
):
    inner = spread_ref.shape[1]

    @pl.when(pl.program_id(1) == 0)
    def _():
        state[...] = entering_state(packed_ref, first_ref, second_ref, spread_ref)

    cumul = sum_ref[0]
    dt = dt_ref[0]
    across = jnp.transpose(cumul)
    last = cumul[CHUNK - 1 : CHUNK, :]
    tail = jnp.exp(last - cumul) * dt
    reach = jnp.exp(cumul)
    decay = jnp.broadcast_to(jnp.exp(last), (8, LANES))
    b_low = xbc_ref[0, :, inner : inner + LANES]
    c_low = xbc_ref[0, :, inner + LANES :]
    b_turned = turned(b_low)
    score = dot(c_low, b_turned)
    causal = iota2(HALF, HALF, 0) >= iota2(HALF, HALF, 1)
    first = iota2(1, LANES, 1) < LANES // 2
    squares = jnp.zeros((CHUNK, STRIP), F32)
    crossed = jnp.zeros((CHUNK, STRIP), F32)
    for cols in strips(inner):
        held = spread_ref[:, cols]
        x = xbc_ref[0, :, cols].astype(F32)
        u = x * spread_heads(dt, held)
        weighted = (x * spread_heads(tail, held)).astype(BF16)
        entering = state[:, cols].astype(BF16)
        enter_ref[0, 0, :, cols] = entering
        carried = dot(c_low, entering) * spread_heads(reach, held)
        state[:, cols] = state[:, cols] * spread_heads(decay, held)[0:1, :] + dot(b_turned, weighted)
        for pair in range(STRIP // LANES):
            lanes = slice(pair * LANES, (pair + 1) * LANES)
            top = carried[0:HALF, lanes]
            bottom = carried[HALF:, lanes]
            for side in range(2):
                head = (cols.start + pair * LANES) // (LANES // 2) + side
                mine = jnp.where(first if side == 0 else ~first, u[:, lanes], 0.0).astype(BF16)
                column = cumul[:, head : head + 1]
                row = across[head : head + 1, :]
                corner = jnp.where(causal, jnp.exp(column[0:HALF] - row[:, 0:HALF]), 0.0)
                top = top + dot((score[0:HALF, 0:HALF] * corner).astype(BF16), mine[0:HALF])
                left = jnp.exp(column[HALF:] - row[:, 0:HALF])
                right = jnp.where(causal, jnp.exp(column[HALF:] - row[:, HALF:]), 0.0)
                bottom = bottom + dot((score[HALF:, 0:HALF] * left).astype(BF16), mine[0:HALF])
                bottom = bottom + dot((score[HALF:, HALF:] * right).astype(BF16), mine[HALF:])
            into = slice(cols.start + pair * LANES, cols.start + (pair + 1) * LANES)
            y_ref[0, 0:HALF, into] = top
            y_ref[0, HALF:, into] = bottom
        y = y_ref[0, :, cols] + rows_ref[0:1, cols] * x
        gate = gate_ref[0, :, cols].astype(F32)
        gated = y * gate * jax.nn.sigmoid(gate)
        gained = gated * rows_ref[1:2, cols]
        mixed_ref[0, :, cols] = gained.astype(BF16)
        squares = squares + gated * gated
        crossed = crossed + gained * gm_ref[0, :, cols]
    stat_ref[0] = jnp.where(iota2(8, CHUNK, 0) == 0, lane_sums(squares), lane_sums(crossed))


def gate_kernel(
    inner_full, y_ref, xbc_ref, gate_ref, gm_ref, stat_ref, sum_ref, total_ref, rows_ref, spread_ref,
    gy_ref, gz_ref, mixed_ref, back_ref, gain_ref, packed_ref,
):
    inner = spread_ref.shape[1]

    @pl.when(pl.program_id(1) == 0)
    def _():
        back_ref[...] = jnp.zeros_like(back_ref)

    @pl.when((pl.program_id(0) == 0) & (pl.program_id(1) == 0))
    def _():
        gain_ref[...] = jnp.zeros_like(gain_ref)

    stats = jnp.transpose(stat_ref[0])
    scale = lax.rsqrt(stats[:, 0:1] / inner_full + EPS)
    bent = scale * scale * scale * (stats[:, 1:2] / inner_full)
    cumul = sum_ref[0]
    reach = jnp.exp(cumul)
    decay = jnp.broadcast_to(jnp.exp(cumul[CHUNK - 1 : CHUNK, :]), (8, LANES))
    c_turned = turned(xbc_ref[0, :, inner + LANES :])
    for cols in strips(inner):
        held = spread_ref[:, cols]
        x = xbc_ref[0, :, cols].astype(F32)
        y = y_ref[0, :, cols] + rows_ref[0:1, cols] * x
        gate = gate_ref[0, :, cols].astype(F32)
        sigmoid = jax.nn.sigmoid(gate)
        silu = gate * sigmoid
        gated = y * silu
        scaled = gated * scale
        gm = gm_ref[0, :, cols]
        gain = rows_ref[1:2, cols]
        gg = scale * gm * gain - gated * bent
        gy = (gg * silu).astype(BF16)
        gy_ref[0, :, cols] = gy
        gz_ref[0, :, cols] = (gg * y * sigmoid * (1.0 + gate * (1.0 - sigmoid))).astype(BF16)
        mixed_ref[0, :, cols] = (scaled * gain).astype(BF16)
        gain_ref[:, cols] += jnp.broadcast_to(jnp.sum(gm * scaled, axis=0, keepdims=True), (8, STRIP))
        reached = (gy.astype(F32) * spread_heads(reach, held)).astype(BF16)
        kept = back_ref[0, :, cols] * spread_heads(decay, held)[0:1, :]
        back_ref[0, :, cols] = kept + dot(c_turned, reached)

    @pl.when(pl.program_id(1) == pl.num_programs(1) - 1)
    def _():
        write_packed(packed_ref, back_ref[0], total_ref[0, 0:1, :])


def adjoint_kernel(
    xbc_ref, sum_ref, dt_ref, gy_ref, y_ref, enter_ref, packed_ref, first_ref, second_ref, mix_ref, before_ref, halo_ref,
    step_ref, taps_ref, heads_ref, rows_ref, spread_ref, collect_ref,
    gmix_ref, rim_ref, gtaps_ref, gheads_ref, gskip_ref, back, ext, gpre, pulled,
):
    inner = spread_ref.shape[1]
    chunks = pl.num_programs(1)
    order = pl.program_id(1)

    @pl.when((pl.program_id(0) == 0) & (order == 0))
    def _():
        gtaps_ref[...] = jnp.zeros_like(gtaps_ref)
        gheads_ref[...] = jnp.zeros_like(gheads_ref)
        gskip_ref[...] = jnp.zeros_like(gskip_ref)

    @pl.when(order == 0)
    def _():
        back[...] = entering_state(packed_ref, first_ref, second_ref, spread_ref)
        gpre[CHUNK:, :] = jnp.zeros((8, gpre.shape[1]), F32)

    @pl.when(order > 0)
    def _():
        gpre[CHUNK:, :] = gpre[0:8, :]

    @pl.when(order == chunks - 1)
    def _():
        ext[0:RIM, :] = halo_ref[0].astype(F32)

    @pl.when(order < chunks - 1)
    def _():
        ext[0:RIM, :] = before_ref[0].astype(F32)

    cumul = sum_ref[0]
    dt = dt_ref[0]
    across = jnp.transpose(cumul)
    last = cumul[CHUNK - 1 : CHUNK, :]
    fade = jnp.exp(last - cumul)
    reach = jnp.exp(cumul)
    decay = jnp.broadcast_to(jnp.exp(last), (8, LANES))
    b_low = xbc_ref[0, :, inner : inner + LANES]
    c_low = xbc_ref[0, :, inner + LANES :]
    c_turned = turned(c_low)
    score = dot(b_low, c_turned)
    causal = iota2(HALF, HALF, 0) <= iota2(HALF, HALF, 1)
    first = iota2(1, LANES, 1) < LANES // 2
    pulled[...] = jnp.zeros_like(pulled)
    gb = jnp.zeros((CHUNK, LANES), F32)
    gc = jnp.zeros((CHUNK, LANES), F32)
    between = jnp.zeros((CHUNK, LANES), F32)
    arrived = jnp.zeros((CHUNK, LANES), F32)
    direct = jnp.zeros((CHUNK, LANES), F32)
    joined = jnp.zeros((8, LANES), F32)

    def conv_part(cols, gact):
        ext[RIM:, cols] = mix_ref[0, :, cols].astype(F32)
        pre = conv_pre(ext, taps_ref, cols)
        sigmoid = jax.nn.sigmoid(pre)
        gp = gact.astype(BF16).astype(F32) * sigmoid * (1.0 + pre * (1.0 - sigmoid))
        gpre[0:CHUNK, cols] = gp
        rim_ref[0, :, cols] = gp[0:8, :]
        total = taps_ref[3:4, cols] * gp
        for k in range(3):
            total = total + taps_ref[k : k + 1, cols] * gpre[pl.ds(3 - k, CHUNK), cols]
            gtaps_ref[k : k + 1, cols] += jnp.sum(
                gp * ext[pl.ds(RIM - 3 + k, CHUNK), cols], axis=0, keepdims=True
            )
        gtaps_ref[3:4, cols] += jnp.sum(gp * ext[RIM:, cols], axis=0, keepdims=True)
        gtaps_ref[4:5, cols] += jnp.sum(gp, axis=0, keepdims=True)
        gmix_ref[0, :, cols] = total.astype(BF16)

    for cols in strips(inner):
        held = spread_ref[:, cols]
        collect = collect_ref[cols, :]
        x = xbc_ref[0, :, cols].astype(F32)
        dt_wide = spread_heads(dt, held)
        fade_wide = spread_heads(fade, held)
        u = x * dt_wide
        u_low = u.astype(BF16)
        weighted = (u * fade_wide).astype(BF16)
        gy_low = gy_ref[0, :, cols]
        gy = gy_low.astype(F32)
        gy_turned = jnp.transpose(gy).astype(BF16)
        reached = (gy * spread_heads(reach, held)).astype(BF16)
        later = back[:, cols]
        later_low = later.astype(BF16)
        entered = enter_ref[0, 0, :, cols]
        gb = gb + dot_nt(weighted, later_low)
        gc = gc + dot_nt(reached, entered)
        gu_carried = dot(b_low, later_low) * fade_wide
        sums = jnp.sum(later * entered.astype(F32), axis=0, keepdims=True)
        joined = joined + gather_heads(jnp.broadcast_to(sums, (8, STRIP)), collect)
        back[:, cols] = later * spread_heads(decay, held)[0:1, :] + dot(c_turned, reached)
        parts = []
        for pair in range(STRIP // LANES):
            lanes = slice(pair * LANES, (pair + 1) * LANES)
            top = gu_carried[0:HALF, lanes]
            bottom = gu_carried[HALF:, lanes]
            gy_pair = gy_turned[lanes, :]
            for side in range(2):
                head = (cols.start + pair * LANES) // (LANES // 2) + side
                keep = first if side == 0 else ~first
                gy_mine = jnp.where(keep, gy[:, lanes], 0.0).astype(BF16)
                u_mine = jnp.where(keep, u[:, lanes], 0.0).astype(BF16)
                column = cumul[:, head : head + 1]
                row = across[head : head + 1, :]
                corner = jnp.where(causal, jnp.exp(row[:, 0:HALF] - column[0:HALF]), 0.0)
                side_right = jnp.exp(row[:, HALF:] - column[0:HALF])
                low_right = jnp.where(causal, jnp.exp(row[:, HALF:] - column[HALF:]), 0.0)
                top = top + dot((score[0:HALF, 0:HALF] * corner).astype(BF16), gy_mine[0:HALF])
                top = top + dot((score[0:HALF, HALF:] * side_right).astype(BF16), gy_mine[HALF:])
                bottom = bottom + dot((score[HALF:, HALF:] * low_right).astype(BF16), gy_mine[HALF:])
                upper = dot(u_mine[0:HALF], gy_pair)
                pulled[0:HALF, 0:HALF] += upper[:, 0:HALF] * corner
                pulled[0:HALF, HALF:] += upper[:, HALF:] * side_right
                pulled[HALF:, HALF:] += dot(u_mine[HALF:], gy_pair[:, HALF:]) * low_right
            parts.append(jnp.concatenate([top, bottom], axis=0))
        gu = jnp.concatenate(parts, axis=1)
        u_kept = u_low.astype(F32)
        between = between + gather_heads(gy * y_ref[0, :, cols] - u_kept * gu, collect)
        arrived = arrived + gather_heads(u_kept * gu_carried, collect)
        direct = direct + gather_heads(x * gu, collect)
        gskip_ref[:, cols] += jnp.broadcast_to(jnp.sum(gy * x, axis=0, keepdims=True), (8, STRIP))
        conv_part(cols, dt_wide * gu + rows_ref[0:1, cols] * gy)

    pulled_low = pulled[...].astype(BF16)
    gb = gb + dot(pulled_low, c_low)
    gc = gc + dot(jnp.transpose(pulled[...]).astype(BF16), b_low)
    conv_part(slice(inner, inner + 2 * LANES), jnp.concatenate([gb, gc], axis=1))

    upper = (iota2(CHUNK, CHUNK, 0) <= iota2(CHUNK, CHUNK, 1)).astype(F32).astype(BF16)
    whole = jnp.sum(arrived, axis=0, keepdims=True) + decay[0:1, :] * joined[0:1, :]
    glg = running_sum(between, upper) + whole
    rate = heads_ref[1:2, :]
    gdt = direct + rate * glg
    raw = step_ref[0].astype(F32) + heads_ref[0:1, :]
    gsi = gdt * jax.nn.sigmoid(raw) * heads_ref[2:3, :]
    gmix_ref[0, :, inner + 2 * LANES :] = gsi.astype(BF16)
    gheads_ref[0:1, :] += jnp.sum(gsi, axis=0, keepdims=True)
    gheads_ref[1:2, :] += jnp.sum(glg * dt * rate, axis=0, keepdims=True)


def flat(width, order=lambda i: i, column=0):
    return pl.BlockSpec((1, CHUNK, width), lambda g, i: (g, order(i), column))


def whole(*shape):
    return pl.BlockSpec((1,) + shape, lambda g, i: (g,) + (0,) * len(shape))


def fixed(shape):
    return pl.BlockSpec(shape, lambda g, i: (0,) * len(shape))


def shaped(shape, dtype=F32):
    return jax.ShapeDtypeStruct(shape, dtype)


def run(kernel, grid, ins, outs, scratch, flops, moved, after=()):
    count = len(ins)
    extra = list(after)

    def body(*refs):
        kernel(*refs[:count], *refs[count + len(extra) :])

    steps = grid[0] * grid[1]
    return pl.pallas_call(
        body,
        grid=grid,
        in_specs=[spec for _, spec in ins] + [pl.BlockSpec(memory_space=pl.ANY)] * len(extra),
        out_specs=[spec for _, spec in outs],
        out_shape=[shape for shape, _ in outs],
        scratch_shapes=scratch,
        compiler_params=pltpu.CompilerParams(
            dimension_semantics=("arbitrary", "arbitrary"), vmem_limit_bytes=VMEM_BYTES
        ),
        cost_estimate=pl.CostEstimate(
            flops=steps * flops, bytes_accessed=steps * moved, transcendentals=0
        ),
    )(*[array for array, _ in ins], *extra)


def local_states(xw, halo, taps, heads, spread, after):
    groups, length, _ = xw.shape
    inner = spread.shape[1]
    width = inner + 2 * LANES
    return run(
        state_kernel,
        (groups, length // CHUNK),
        [
            (xw, flat(width)),
            (halo, whole(RIM, width)),
            (xw, flat(LANES, column=width // LANES)),
            (taps, fixed(taps.shape)),
            (heads, fixed(heads.shape)),
            (spread, fixed(spread.shape)),
        ],
        [
            (shaped((groups, length, width), BF16), flat(width)),
            (shaped((groups, length, LANES)), flat(LANES)),
            (shaped((groups, length, LANES)), flat(LANES)),
            (shaped((groups, LANES, inner)), whole(LANES, inner)),
            (shaped((groups, 8, LANES)), whole(8, LANES)),
            (shaped((groups, LANES + RIM, inner), BF16), whole(LANES + RIM, inner)),
        ],
        [pltpu.VMEM((RIM + CHUNK, width), F32)],
        1_500_000_000,
        2_000_000,
        after,
    )


def mixer(xbc, cumul, dt, start, gate, gm, rows, spread, after):
    groups, length, width = xbc.shape
    inner = spread.shape[1]
    chunks = length // CHUNK
    return run(
        scan_kernel,
        (groups, chunks),
        [
            (xbc, flat(width)),
            (cumul, flat(LANES)),
            (dt, flat(LANES)),
            (start[0], whole(LANES + RIM, inner)),
            (start[1], whole(LANES, inner)),
            (start[2], whole(LANES, inner)),
            (gate, flat(inner)),
            (gm, flat(inner)),
            (rows, fixed(rows.shape)),
            (spread, fixed(spread.shape)),
        ],
        [
            (shaped((groups, length, inner)), flat(inner)),
            (shaped(gate.shape, BF16), flat(inner)),
            (
                shaped((groups, chunks, LANES, inner), BF16),
                pl.BlockSpec((1, 1, LANES, inner), lambda g, i: (g, i, 0, 0)),
            ),
            (shaped((groups, 8, length)), pl.BlockSpec((1, 8, CHUNK), lambda g, i: (g, 0, i))),
        ],
        [pltpu.VMEM((LANES, inner), F32)],
        2_500_000_000,
        4_000_000,
        after,
    )


def gate_back(inner_full, y, xbc, gate, gm, stats, cumul, total, rows, spread, after):
    groups, length, width = xbc.shape
    inner = spread.shape[1]
    chunks = length // CHUNK
    back = lambda i: chunks - 1 - i
    return run(
        functools.partial(gate_kernel, float(inner_full)),
        (groups, chunks),
        [
            (y, flat(inner, back)),
            (xbc, flat(width, back)),
            (gate, flat(inner, back)),
            (gm, flat(inner, back)),
            (stats, pl.BlockSpec((1, 8, CHUNK), lambda g, i: (g, 0, back(i)))),
            (cumul, flat(LANES, back)),
            (total, whole(8, LANES)),
            (rows, fixed(rows.shape)),
            (spread, fixed(spread.shape)),
        ],
        [
            (shaped((groups, length, inner), BF16), flat(inner, back)),
            (shaped(gate.shape, BF16), flat(inner, back)),
            (shaped(gate.shape, BF16), flat(inner, back)),
            (shaped((groups, LANES, inner)), whole(LANES, inner)),
            (shaped((8, inner)), fixed((8, inner))),
            (shaped((groups, LANES + RIM, inner), BF16), whole(LANES + RIM, inner)),
        ],
        [],
        1_500_000_000,
        4_500_000,
        after,
    )


def adjoint(xbc, cumul, dt, gy, y, enter, gin, xw, halo, taps, heads, rows, spread, collect, after):
    groups, length, width = xbc.shape
    inner = spread.shape[1]
    chunks = length // CHUNK
    back = lambda i: chunks - 1 - i
    per = CHUNK // RIM
    return run(
        adjoint_kernel,
        (groups, chunks),
        [
            (xbc, flat(width, back)),
            (cumul, flat(LANES, back)),
            (dt, flat(LANES, back)),
            (gy, flat(inner, back)),
            (y, flat(inner, back)),
            (enter, pl.BlockSpec((1, 1, LANES, inner), lambda g, i: (g, back(i), 0, 0))),
            (gin[0], whole(LANES + RIM, inner)),
            (gin[1], whole(LANES, inner)),
            (gin[2], whole(LANES, inner)),
            (xw, flat(width, back)),
            (
                xw,
                pl.BlockSpec(
                    (1, RIM, width), lambda g, i: (g, jnp.maximum(back(i) * per - 1, 0), 0)
                ),
            ),
            (halo, whole(RIM, width)),
            (xw, flat(LANES, back, width // LANES)),
            (taps, fixed(taps.shape)),
            (heads, fixed(heads.shape)),
            (rows, fixed(rows.shape)),
            (spread, fixed(spread.shape)),
            (collect, fixed(collect.shape)),
        ],
        [
            (shaped((groups, length, width + LANES), BF16), flat(width + LANES, back)),
            (shaped((groups, 8, width)), whole(8, width)),
            (shaped((8, width)), fixed((8, width))),
            (shaped((8, LANES)), fixed((8, LANES))),
            (shaped((8, inner)), fixed((8, inner))),
        ],
        [
            pltpu.VMEM((LANES, inner), F32),
            pltpu.VMEM((RIM + CHUNK, width), F32),
            pltpu.VMEM((CHUNK + 8, width), F32),
            pltpu.VMEM((CHUNK, CHUNK), F32),
        ],
        8_000_000_000,
        6_000_000,
        after,
    )


def leave(ends, totals, packed, spread):
    groups, states, inner = ends.shape

    def one(*shape):
        return pl.BlockSpec((1,) + shape, lambda g: (g,) + (0,) * len(shape))

    return pl.pallas_call(
        leave_kernel,
        grid=(groups,),
        in_specs=[
            one(states, inner), one(8, LANES), one(states + RIM, inner),
            pl.BlockSpec(spread.shape, lambda g: (0, 0)),
        ],
        out_specs=one(states, inner),
        out_shape=shaped(ends.shape, BF16),
        compiler_params=pltpu.CompilerParams(
            dimension_semantics=("arbitrary",), vmem_limit_bytes=VMEM_BYTES
        ),
        cost_estimate=pl.CostEstimate(
            flops=0, bytes_accessed=8 * groups * states * inner, transcendentals=0
        ),
    )(ends, totals, packed, spread)


def place_kernel(at_ref, first, first_y, second, second_x, full_ref):
    step = pl.program_id(0)
    for number, ref in enumerate((first, first_y, second, second_x)):

        @pl.when(step // 2 == number)
        def _(ref=ref):
            full_ref[0, 0, 0] = ref[0]


def place_row(number, step, at):
    x, core, y = at[0], at[1], at[2]
    later = number // 2
    side = number % 2
    row = x + jnp.where(later == 0, step, side)
    column = y + jnp.where(later == 0, side, step)
    return row % 2, jnp.where(later == 0, core, 1 - core), column % 2, 0, 0


def place(first, first_y, second, second_x):
    _, rows, columns = first.shape
    at = jnp.stack([lax.axis_index(name) for name in ("x", "core", "y")]).astype(jnp.int32)

    def piece(number):
        return pl.BlockSpec(
            (1, rows, columns), lambda i, at: (jnp.clip(i - 2 * number, 0, 1), 0, 0)
        )

    full = pl.pallas_call(
        place_kernel,
        grid_spec=pltpu.PrefetchScalarGridSpec(
            num_scalar_prefetch=1,
            grid=(8,),
            in_specs=[piece(number) for number in range(4)],
            out_specs=pl.BlockSpec(
                (1, 1, 1, rows, columns), lambda i, at: place_row(i // 2, i % 2, at)
            ),
        ),
        out_shape=shaped((2, 2, 2, rows, columns), first.dtype),
        compiler_params=pltpu.CompilerParams(
            dimension_semantics=("arbitrary",), vmem_limit_bytes=VMEM_BYTES
        ),
        cost_estimate=pl.CostEstimate(
            flops=0, bytes_accessed=rows * columns, transcendentals=0
        ),
    )(at, first, first_y, second, second_x)
    return full.reshape(8 * rows, columns)


def join_kernel(at_ref, own, got, far_own, far_got, full_ref):
    half_is_own = pl.program_id(1) == at_ref[0]
    for core, (mine, other) in enumerate(((own, got), (far_own, far_got))):
        for ref, wanted in ((mine, half_is_own), (other, ~half_is_own)):

            @pl.when(wanted & (pl.program_id(0) == core))
            def _(ref=ref):
                full_ref[0] = ref[...]


def joined(own, got, far_own, far_got, part=0):
    _, rows, columns = own.shape
    at = lax.axis_index("zq").astype(jnp.int32)[None]
    piece = pl.BlockSpec((None, rows, columns), lambda c, h, at: (part, 0, 0))
    return pl.pallas_call(
        join_kernel,
        grid_spec=pltpu.PrefetchScalarGridSpec(
            num_scalar_prefetch=1,
            grid=(2, 2),
            in_specs=[piece] * 4,
            out_specs=pl.BlockSpec((1, rows, columns), lambda c, h, at: (c, h, 0)),
        ),
        out_shape=shaped((2, 2 * rows, columns), own.dtype),
        compiler_params=pltpu.CompilerParams(
            dimension_semantics=("arbitrary", "arbitrary"), vmem_limit_bytes=VMEM_BYTES
        ),
        cost_estimate=pl.CostEstimate(
            flops=0, bytes_accessed=16 * rows * columns, transcendentals=0
        ),
    )(at, own, got, far_own, far_got)


def swap(value, axis):
    return lax.ppermute(value, axis, [(0, 1), (1, 0)])


def sum_axis(value, axis):
    if lax.axis_size(axis) == 2:
        return value + swap(value, axis)
    return lax.psum(value, axis)


def cut(value, axis, dim):
    size = value.shape[dim] // 2
    at = lax.axis_index(axis)
    kept = lax.dynamic_slice_in_dim(value, at * size, size, dim)
    return kept, lax.dynamic_slice_in_dim(value, (1 - at) * size, size, dim)


def added(kept, got, dtype=BF16):
    return (kept.astype(F32) + got.astype(F32)).astype(dtype)


def hold(value, *before):
    if not before:
        return value
    return lax.optimization_barrier((value,) + before)[0]


def shift(value, by):
    blocks = lax.axis_size(("y", "zp"))
    pairs = [(i, i + by) for i in range(blocks) if 0 <= i + by < blocks]
    return lax.ppermute(value, ("y", "zp"), pairs)


def row_hop(packed, way, *before):
    return hold(lax.ppermute(packed, "zp", [(0, 1)] if way == 1 else [(1, 0)]), *before)


def column_hops(leaving, way, *before):
    source = 1 if way == 1 else 2
    pairs = [[(source, source + way * (1 + to))] for to in range(2)]
    return [hold(lax.ppermute(leaving, ("y", "zp"), pair), *before) for pair in pairs]


def chained(packed, way):
    blocks = lax.axis_size(("y", "zp"))
    groups, _, inner = packed.shape
    heads = inner // (LANES // 2)
    entering = jnp.zeros((groups, LANES, inner), F32)
    passed = jnp.zeros((groups, 1, LANES), F32)
    for by in range(1, blocks):
        got = shift(packed, by * way).astype(F32)
        weight = jnp.repeat(jnp.exp(passed[:, :, 0:heads]), LANES // 2, axis=2)
        entering = entering + weight * got[:, 0:LANES]
        passed = passed + jnp.sum(got[:, LANES:, 0:LANES], axis=1, keepdims=True)
    none = jnp.zeros(entering.shape, BF16)
    return jnp.pad(entering.astype(BF16), ((0, 0), (0, RIM), (0, 0))), none, none


def all_pairs():
    return all(lax.axis_size(name) == 2 for name in ("x", "y", "zp"))


NEAR = [(0, 1), (3, 2), (1, 3), (2, 0)]
FAR = [(1, 2), (2, 1)]
HOME = [(to, source) for source, to in NEAR]


def fetched(piece, near, far):
    at_home = lax.axis_index("core") == lax.axis_index("zp")
    return jnp.where(at_home, piece, near), jnp.where(at_home, near, far)


def fetch(piece):
    return lax.ppermute(piece, ("core", "zp"), NEAR), lax.ppermute(piece, ("core", "zp"), FAR)


def gather_slice(piece):
    owners = lax.axis_size("zp")
    rows = lax.all_gather(piece, ("x", "core", "y"), axis=0, tiled=True)
    parts = lax.all_gather(rows, "zp")
    return lax.dynamic_slice_in_dim(parts, lax.axis_index("core") * (owners // 2), owners // 2, 0)


def reduce_slice(parts):
    owners = lax.axis_size("zp")
    full = jnp.zeros((owners,) + parts.shape[1:], parts.dtype)
    full = lax.dynamic_update_slice_in_dim(
        full, parts, lax.axis_index("core") * (owners // 2), axis=0
    )
    mine = lax.psum_scatter(full, "zp", scatter_dimension=0, tiled=True)[0]
    mine = lax.psum_scatter(mine, ("x", "core", "y"), scatter_dimension=0, tiled=True)
    return mine.astype(F32)


def cut_rows(fulls):
    core = lax.axis_index("core")
    same, cross = [], []
    for full in fulls:
        rows, columns = full.shape[0] // 8, full.shape[1]
        full = full.reshape(2, 2, 2, rows, columns)
        same.append(cut(lax.dynamic_index_in_dim(full, core, 1, False), "x", 0))
        cross.append(cut(lax.dynamic_index_in_dim(full, 1 - core, 1, False), "y", 1))
    return (
        [kept[0] for kept, _ in same],
        [kept[:, 0] for kept, _ in cross],
        jnp.stack([sent[0] for _, sent in same]),
        jnp.stack([sent[:, 0] for _, sent in cross]),
    )


def cut_again(sames, crosses):
    same = [cut(value, "y", 0) for value in sames]
    cross = [cut(value, "x", 0) for value in crosses]
    return (
        [kept[0] for kept, _ in same],
        [kept[0] for kept, _ in cross],
        jnp.stack([sent[0] for _, sent in same]),
        jnp.stack([sent[0] for _, sent in cross]),
    )


def both(kept, got):
    return [
        [added(mine, other[k]) for k, mine in enumerate(values)]
        for values, other in zip(kept[0:2], got)
    ]


def home_parts(sames, crosses):
    at_home = lax.axis_index("core") == lax.axis_index("zp")
    cross = jnp.stack(crosses)
    return jnp.where(at_home, cross, jnp.stack(sames)), cross


def at_owner(near, far, sames):
    at_home = lax.axis_index("core") == lax.axis_index("zp")
    return [
        near[k].astype(F32) + jnp.where(at_home, same.astype(F32), far[k].astype(F32))
        for k, same in enumerate(sames)
    ]


def go_home(sent):
    return (
        lax.ppermute(sent[0], ("core", "zp"), HOME),
        lax.ppermute(sent[1], ("core", "zp"), FAR),
    )


def own_of_slice(value):
    owners = lax.axis_size("zp")
    core, part = lax.axis_index("core"), lax.axis_index("zp")
    other = swap(value, "core")
    share = value.shape[-1] // (owners // 2)
    wanted = jnp.where(part // (owners // 2) == core, value, other)
    return lax.dynamic_slice_in_dim(wanted, (part % (owners // 2)) * share, share, value.ndim - 1)


def slice_of_own(value, after):
    owners = lax.axis_size("zp")
    core = lax.axis_index("core")
    if owners == 2:
        other = hold(swap(value, "zp"), after)
        return jnp.where(core == lax.axis_index("zp"), value, other)[None]
    parts = lax.all_gather(value, "zp")
    return lax.dynamic_slice_in_dim(parts, core * (owners // 2), owners // 2, 0)


def per_device(
    hidden,
    cotangent,
    norm_gain,
    w_z,
    w_x,
    w_bc,
    w_dt,
    conv_x,
    conv_x_bias,
    conv_bc,
    conv_bc_bias,
    dt_bias,
    a_log,
    d_skip,
    inner_gain,
    w_out,
):
    micro, own_len, model = hidden.shape
    owners = lax.axis_size("zp")
    share = w_x.shape[1]
    own_heads = w_dt.shape[1]
    inner_full = share * 2 * owners
    states2 = w_bc.shape[1]
    halves = owners // 2
    inner = share * halves
    heads = own_heads * halves
    head_width = inner // heads
    width = inner + states2

    def matmul(left, right, contract, dtype=F32):
        return lax.dot_general(
            left, right, (contract, ((), ())), preferred_element_type=F32
        ).astype(dtype)

    def spliced(parts, sizes):
        if halves == 1:
            return parts[0]
        columns, at = [], 0
        for size, copies in sizes:
            columns += [parts[k][:, at : at + size] for k in range(halves if copies else 1)]
            at += size
        return jnp.concatenate(columns, axis=1)

    parts = range(micro)

    own = hidden.astype(F32)
    gain_in = norm_gain.astype(F32)
    r0 = lax.rsqrt(jnp.mean(own * own, axis=-1, keepdims=True) + EPS)
    filler = LANES // halves - own_heads
    own_first = jnp.concatenate(
        [w_x, w_bc, w_dt, jnp.zeros((w_dt.shape[0], filler), BF16)], axis=1
    )
    own_second = jnp.concatenate([w_z, jnp.transpose(w_out)], axis=1)
    normed_own = [(own[part : part + 1] * r0[part : part + 1] * gain_in).astype(BF16) for part in parts]
    fast = all_pairs()

    def tokens_of(value, *before):
        got = hold(swap(value, "zq"), *before)
        return value, got, swap(value, "core"), swap(got, "core")

    if fast:
        got = fetch(own_first)
    fours = [tokens_of(normed_own[0])]
    if fast:
        same, cross = fetched(own_first, *got)
        moved = hold((swap(same, "x"), swap(cross, "y")), fours[0][1])
        first, second = jnp.stack([same, moved[0]]), jnp.stack([cross, moved[1]])
        own_second = hold(own_second, fours[0][1], *moved)
        got = fetch(own_second)
        rest = swap(first, "y"), swap(second, "x")
        later = first, second
    else:
        later = (fours[0][1],)
    for part in parts[1:]:
        fours.append(tokens_of(hold(normed_own[part], fours[0][1]), *later))
        later = (fours[-1][1],)
    if fast:
        w_first = place(first, rest[0], second, rest[1])
        got = hold(got, w_first)
        same, cross = fetched(own_second, *got)
        moved = swap(same, "x"), swap(cross, "y")
    else:
        w_first = spliced(
            gather_slice(own_first), ((share, 1), (states2, 0), (own_heads, 1), (filler, 1))
        )
    normed = [joined(*four) for four in fours]
    per_head = jnp.concatenate([dt_bias, a_log, d_skip])
    per_head = jnp.pad(per_head, (0, share - 3 * own_heads))
    small = jnp.concatenate([conv_x, conv_x_bias[None], inner_gain[None]], axis=0).astype(F32)
    small = jnp.concatenate([small, per_head[None], jnp.zeros((1, share), F32)])
    small = slice_of_own(small, w_first)
    channel_rows = jnp.concatenate([small[k, 0:6] for k in range(halves)], axis=1)
    head_rows = jnp.concatenate(
        [small[k, 6, 0 : 3 * own_heads].reshape(3, own_heads) for k in range(halves)], axis=1
    )
    conv_shared = jnp.concatenate([conv_bc, conv_bc_bias[None]], axis=0).astype(F32)
    taps = jnp.pad(jnp.concatenate([channel_rows[0:5], conv_shared], axis=1), ((0, 3), (0, 0)))
    head_in = jnp.stack([head_rows[0], -jnp.exp(head_rows[1]), jnp.ones((heads,), F32)])
    head_in = jnp.pad(head_in, ((0, 5), (0, LANES - heads)))
    rows = jnp.stack([jnp.repeat(head_rows[2], head_width), channel_rows[5]])
    rows = jnp.pad(rows, ((0, 6), (0, 0)))
    spread = (
        lax.broadcasted_iota(jnp.int32, (LANES, inner), 1) // head_width
        == lax.broadcasted_iota(jnp.int32, (LANES, inner), 0)
    ).astype(BF16)

    scans = []
    for part in parts:
        xw = matmul(normed[part], w_first, ((2,), (0,)), BF16)
        scans.append((xw, shift(xw[:, -RIM:, 0:width], 1)))
        if part == 0:
            normed[-1] = hold(normed[-1], xw)
    if fast:
        moved = hold(moved, scans[0][0])
        first, second = jnp.stack([same, moved[0]]), jnp.stack([cross, moved[1]])
        got_second = first, swap(first, "y"), second, swap(second, "x")
    local = []
    for part in parts:
        before = [k[5] for k in local[-1:]]
        local.append(local_states(*scans[part], taps, head_in, spread, before))
        if part == 0:
            cot_own = hold(cotangent, local[0][5], scans[-1][1])
            cot_own = [cot_own[k : k + 1] for k in parts]
            cot_got = [swap(value, "zq") for value in cot_own]
    totals = [local[part][4] for part in parts]
    packed = [local[part][5] for part in parts]
    if fast:
        w_second = place(*hold(got_second, packed[-1]))
    else:
        w_second = spliced(
            gather_slice(hold(own_second, packed[-1])), ((share, 1), (share, 1))
        )
    w_gate, w_down = w_second[:, 0:inner], w_second[:, inner:]
    def hop(part, packed, ends, way, *before):
        if not fast:
            return packed, packed
        got = row_hop(packed, way, *before)
        return got, leave(ends, totals[part], got, spread)

    def entering(found, way, *before):
        if not fast:
            return chained(found[0], way)
        return found[0], *column_hops(found[1], way, *before)

    found = [hop(0, packed[0], local[0][3], 1, w_second)]
    gate = [
        matmul(hold(normed[part], found[0][1]), w_gate, ((2,), (0,)), BF16) for part in parts
    ]
    cot_far = (
        swap(hold(cotangent, local[0][5]), "core"),
        [swap(hold(cot_got[k], gate[k]), "core") for k in parts],
    )

    def whole_cot(part, *before):
        far = hold((cot_far[0], cot_far[1][part]), *before)
        return joined(cot_own[part], cot_got[part], far[0][part : part + 1], far[1])

    cot = [whole_cot(0, gate[-1])]

    w_down_held = hold(w_down, found[0][1])
    gm = [matmul(cot[0], w_down_held, ((2,), (0,)))]
    mixes, stats, branches, gates = [], [], [], []
    g_gate = g_down = 0.0
    tokens = ((0, 1), (0, 1))
    for part in parts:
        xbc, cumul, dt = local[part][0:3]
        before = (gm[0],) if part == 0 else (gates[part - 1][5], gm[part])
        start = entering(found[part], 1, *before)
        y, gained, enter, stat = mixer(xbc, cumul, dt, start, gate[part], gm[part], rows, spread, before)
        mixes.append((y, enter))
        other = swap(stat, "core")
        if part + 1 < micro:
            following = hold(packed[part + 1], found[part][1])
            found.append(hop(part + 1, following, local[part + 1][3], 1, y))
            cot.append(whole_cot(part + 1, found[-1][1]))
            gm.append(matmul(cot[-1], w_down, ((2,), (0,))))
            other = hold(other, cot[-1])
        else:
            g_gate = matmul(normed[0], hold(gates[0][1], y), tokens)
            other = hold(other, g_gate)
        stat = stat + jnp.flip(other, 0)
        other = swap(stat, "zq")
        branch = matmul(hold(gained, stat, gm[-1]), w_down, ((2,), (1,)), BF16)
        stats.append(stat + hold(other, branch))
        branches.append((branch, swap(branch[1], "core")))
        gates.append(
            gate_back(
                inner_full, y, xbc, gate[part], gm[part], stats[part], cumul, totals[part],
                rows, spread, [branch],
            )
        )
    back_packed = [g[5] for g in gates]

    found = [hop(0, back_packed[0], gates[0][3], -1, back_packed[-1])]
    for part in parts:
        g_down = g_down + matmul(cot[part], hold(gates[part][2], found[0][1]), tokens)
        if part == 0:
            branch_cut = [
                cut(added(branch[0], hold(got, g_down)), "zq", 0) for branch, got in branches
            ]
            branch_sent = jnp.stack([sent for _, sent in branch_cut])
            branch_got = swap(branch_sent, "zq")
        else:
            g_gate = g_gate + matmul(normed[part], hold(gates[part][1], g_down), tokens)
    g_gate, g_down = g_gate.astype(BF16), g_down.astype(BF16)
    g_normed_gate = [matmul(hold(gates[0][1], g_gate), w_gate, ((2,), (1,)))]
    gin = entering(found[0], -1, g_normed_gate[0])
    for part in parts[1:]:
        following = hold(back_packed[part], found[part - 1][1])
        found.append(hop(part, following, gates[part][3], -1, g_normed_gate[0]))
    wait_for = [found[-1][1], branch_sent]
    if fast:
        second = cut_rows(hold([g_gate, g_down], *gin))
        moved = swap(second[2], "x"), swap(second[3], "y")
        wait_for += second[2:]

    g_first, heads_out, g_hidden, g_norm_gain = 0.0, [], [], 0.0

    def token_grad(part, kept, got):
        x, r, g = own[part], r0[part], added(kept, got, F32)
        q0 = g * gain_in
        grad = (
            cotangent[part].astype(F32) + r * q0
            - x * (r * r * r) * jnp.mean(q0 * x, axis=-1, keepdims=True)
        )
        return grad, jnp.sum(g * x * r, axis=0)

    def whole_output(*before):
        outputs = []
        for part in parts:
            square = lax.dynamic_slice_in_dim(
                stats[part][0, 0], lax.axis_index("zq") * own_len, own_len, 0
            )
            r1 = lax.rsqrt(square / inner_full + EPS)[:, None]
            got = hold(branch_got, *before)[part]
            outputs.append((own[part] + r1 * added(branch_cut[part][0], got, F32)).astype(BF16))
        return jnp.stack(outputs)

    for part in parts:
        xbc, cumul, dt = local[part][0:3]
        gmix, rim, *sums = adjoint(
            xbc, cumul, dt, gates[part][0], mixes[part][0], mixes[part][1], gin,
            *scans[part], taps, head_in, rows, spread, jnp.transpose(spread), wait_for,
        )
        if part == micro - 1 and fast and micro > 1:
            got_home = hold(got_home, gmix)
            g_gate, g_down = at_owner(*got_home, pair[0])
            rim = hold(rim, g_gate, g_down)
        if part < micro - 1:
            gin = entering(found[part + 1], -1)
            gmix, rim, *sums = hold(
                (gmix, rim, *sums), *gin, branch_got, *(moved if fast else ())
            )
        heads_out.append(sums)
        ahead = shift(rim, -1)
        last_part = part == micro - 1
        if last_part:
            if micro > 1:
                kept, got = norm_cut
                grad, gain = token_grad(part - 1, kept, hold(got, gmix))
                g_hidden.append(grad)
                g_norm_gain = g_norm_gain + gain
                ahead = hold(ahead, grad)
        else:
            if fast:
                moved = hold(moved, gmix)
                second = cut_again(*both(second, moved))
                moved = swap(second[2], "y"), swap(second[3], "x")
        fix = jnp.stack(
            [sum(taps[k, :] * ahead[:, r - k] for k in range(r + 1)) for r in range(3)], axis=1
        )
        length = gmix.shape[1]
        last = gmix[:, length - RIM :].astype(F32)
        last = last + jnp.pad(fix, ((0, 0), (RIM - 3, 0), (0, LANES)))
        gmix = lax.dynamic_update_slice_in_dim(gmix, last.astype(BF16), length - RIM, 1)

        def for_weights(gmix):
            return g_first + matmul(normed[part], gmix, tokens)

        def for_tokens(gmix):
            total = g_normed_gate[part] + matmul(gmix, w_first, ((2,), (1,)))
            return total.astype(BF16)

        total = for_tokens(gmix)
        other = swap(total[1], "core")
        g_first = for_weights(hold(gmix, total))
        if last_part:
            g_first = g_first.astype(BF16)
            if fast:
                first = cut_rows([g_first])
                moved_first = swap(first[2], "x"), swap(first[3], "y")
        else:
            g_normed_gate.append(
                matmul(hold(gates[part + 1][1], g_first), w_gate, ((2,), (1,)))
            )
            kept, sent = cut(added(total[0], hold(other, g_first)), "zq", 0)
            norm_cut = kept, swap(sent, "zq")
            if part == micro - 2:
                outputs = whole_output(g_normed_gate[-1], sent)
            gin = hold(gin, outputs)
            wait_for = [sent, outputs]
            if fast and part == micro - 2:
                moved = hold(moved, g_normed_gate[-1])
                pair = both(second, moved)
                home = home_parts(*pair)
                wait_for += home
                got_home = go_home(home)

    kept, sent = cut(added(total[0], hold(other, g_first, *(first[2:] if fast else ()))), "zq", 0)
    got_norm = swap(sent, "zq")
    if fast:
        first = cut_again(*both(first, hold(moved_first, sent)))
        moved = swap(first[2], "y"), swap(first[3], "x")
        got_norm = hold(got_norm, *first[2:])
        pair = both(first, hold(moved, got_norm))
        home = home_parts(*pair)
        got_home = go_home(home)
        grad, gain = token_grad(micro - 1, kept, hold(got_norm, *home))
        g_first = at_owner(*hold(got_home, grad), pair[0])[0]
    else:
        g_gate, g_down = [
            reduce_slice(jnp.stack(jnp.split(value, halves, axis=1))) for value in (g_gate.astype(BF16), g_down.astype(BF16))
        ]
        grad, gain = token_grad(micro - 1, kept, got_norm)
        g_first = reduce_slice(
            jnp.concatenate(
                [
                    jnp.stack(jnp.split(g_first[:, 0:inner], halves, axis=1)),
                    jnp.concatenate(
                        [
                            g_first[None, :, inner:width],
                            jnp.zeros((halves - 1, model, states2), BF16),
                        ]
                    ),
                    jnp.stack(jnp.split(g_first[:, width : width + heads], halves, axis=1)),
                ],
                axis=2,
            )
        )
    g_hidden = jnp.stack(g_hidden + [grad])
    g_norm_gain = g_norm_gain + gain
    g_bc = g_first[:, share : share + states2]
    if fast:
        across = lax.ppermute(g_bc, ("zp", "zq"), [(0, 3), (3, 0), (1, 2), (2, 1)])
        g_bc = (g_bc + swap(g_bc, "zq")) + (swap(g_bc, "zp") + across)
    else:
        g_bc = sum_axis(sum_axis(g_bc, "zp"), "zq")

    g_taps, g_heads, g_skip = (sum(b[k] for b in heads_out) for k in range(3))
    g_gain = sum(g[4] for g in gates)
    skip_heads = jnp.sum(g_skip[0].reshape(heads, head_width), axis=1)
    small = jnp.concatenate(
        [g_taps[0:5, 0:inner].reshape(-1), g_gain[0], g_heads[0, 0:heads], g_heads[1, 0:heads], skip_heads]
    )
    size = small.shape[0]
    packed = jnp.concatenate([small, g_taps[0:5, inner:width].reshape(-1), g_norm_gain])
    packed = sum_axis(sum_axis(packed, "x"), "y")
    packed = sum_axis(hold(packed, g_first), "zp")
    small = packed[:size]
    shared = sum_axis(sum_axis(packed[size:], "core"), "zq")
    bc_rows = shared[0 : 5 * states2].reshape(5, states2)
    channel = own_of_slice(small[0 : 6 * inner].reshape(6, inner))
    per_head = own_of_slice(small[6 * inner :].reshape(3, heads))
    return (
        outputs,
        g_hidden,
        shared[5 * states2 :],
        g_gate,
        g_first[:, 0:share],
        g_bc,
        g_first[:, share + states2 : share + states2 + own_heads],
        channel[0:4],
        channel[4],
        bc_rows[0:4],
        bc_rows[4],
        per_head[0],
        per_head[1],
        per_head[2],
        channel[5],
        jnp.transpose(g_down),
    )


def solution(mesh):
    dp, seq, tensor = (mesh.shape[name] for name in ("dp", "seq", "tensor"))
    fine = Mesh(
        mesh.devices.reshape(dp // 2, 2, seq, tensor // 2, 2), ("x", "core", "y", "zp", "zq")
    )
    data, tens = ("x", "core", "y"), ("zp", "zq")
    tokens = P(("x", "core"), ("y", "zp", "zq"), None)
    params = (
        P(),
        P(data, tens),
        P(data, tens),
        P(data, None),
        P(data, tens),
        P(None, tens),
        P(tens),
        P(),
        P(),
        P(tens),
        P(tens),
        P(tens),
        P(tens),
        P(tens, data),
    )
    return jax.shard_map(
        per_device,
        mesh=fine,
        in_specs=(tokens, tokens) + params,
        out_specs=(tokens, tokens) + params,
        check_vma=False,
    )
```

```python
import functools

import jax
import jax.numpy as jnp
from jax import lax
from jax.experimental import pallas as pl
from jax.experimental.pallas import tpu as pltpu
from jax.sharding import Mesh
from jax.sharding import PartitionSpec as P

CHUNK = 256
HALF = CHUNK // 2
LANES = 128
STRIP = 256
RIM = 16
EPS = 1e-05
F32 = jnp.float32
BF16 = jnp.bfloat16
VMEM_BYTES = 48 * 1024 * 1024


def dot(left, right):
    return lax.dot_general(left, right, (((1,), (0,)), ((), ())), preferred_element_type=F32)


def dot_nt(left, right):
    return lax.dot_general(left, right, (((1,), (1,)), ((), ())), preferred_element_type=F32)


def pieces(value, count):
    terms = []
    for _ in range(count):
        term = value.astype(BF16)
        terms.append(term)
        value = value - term.astype(F32)
    return terms


def spread_heads(value, spread):
    return sum(dot(term, spread) for term in pieces(value, 2))


def gather_heads(value, spread):
    return sum(dot_nt(term, spread) for term in pieces(value, 2))


def running_sum(value, mask):
    return sum(dot(mask, term) for term in pieces(value, 3))


def iota2(rows, cols, dim):
    return lax.broadcasted_iota(jnp.int32, (rows, cols), dim)


def turned(value):
    return jnp.transpose(value.astype(F32)).astype(BF16)


def strips(width):
    return [slice(at, at + STRIP) for at in range(0, width, STRIP)]


def conv_pre(ext, taps, cols):
    total = taps[4:5, cols] + taps[0:1, cols] * ext[pl.ds(RIM - 3, CHUNK), cols]
    for k in range(1, 4):
        total = total + taps[k : k + 1, cols] * ext[pl.ds(RIM - 3 + k, CHUNK), cols]
    return total


def softplus(value):
    return jnp.maximum(value, 0.0) + jnp.log1p(jnp.exp(-jnp.abs(value)))


def write_packed(packed_ref, end, total):
    packed_ref[0, 0:LANES, :] = end.astype(BF16)
    packed_ref[0, LANES:, :] = jnp.zeros((RIM, end.shape[1]), BF16)
    row = iota2(RIM, LANES, 0)
    logs = jnp.zeros((RIM, LANES), F32)
    for k, term in enumerate(pieces(total, 3)):
        logs = jnp.where(row == k, term.astype(F32), logs)
    packed_ref[0, LANES:, 0:LANES] = logs.astype(BF16)


def widened(log, spread):
    return spread_heads(jnp.broadcast_to(jnp.exp(log), (8, LANES)), spread)[0:1, :]


def entering_state(packed_ref, first_ref, second_ref, spread_ref):
    passed = jnp.sum(packed_ref[0, LANES:, 0:LANES].astype(F32), axis=0, keepdims=True)
    from_row = first_ref[0].astype(F32) + second_ref[0].astype(F32)
    return packed_ref[0, 0:LANES, :].astype(F32) + widened(passed, spread_ref[...]) * from_row


def leave_kernel(end_ref, total_ref, packed_ref, spread_ref, leaving_ref):
    kept = packed_ref[0, 0:LANES, :].astype(F32) * widened(total_ref[0, 0:1, :], spread_ref[...])
    leaving_ref[0] = (end_ref[0] + kept).astype(BF16)


def state_kernel(
    mix_ref, halo_ref, step_ref, taps_ref, heads_ref, spread_ref,
    xbc_ref, sum_ref, dt_ref, end_ref, total_ref, packed_ref, ext,
):
    inner = spread_ref.shape[1]
    place = pl.program_id(1)

    @pl.when(place == 0)
    def _():
        ext[0:RIM, :] = halo_ref[0].astype(F32)
        end_ref[...] = jnp.zeros_like(end_ref)
        total_ref[...] = jnp.zeros_like(total_ref)

    @pl.when(place > 0)
    def _():
        ext[0:RIM, :] = ext[CHUNK : CHUNK + RIM, :]

    dt = softplus(step_ref[0].astype(F32) + heads_ref[0:1, :])
    lower = (iota2(CHUNK, CHUNK, 0) >= iota2(CHUNK, CHUNK, 1)).astype(F32).astype(BF16)
    cumul = running_sum(dt * heads_ref[1:2, :], lower)
    sum_ref[0] = cumul
    dt_ref[0] = dt
    last = cumul[CHUNK - 1 : CHUNK, :]
    total_ref[0] += jnp.broadcast_to(last, total_ref.shape[1:])
    tail = jnp.exp(last - cumul) * dt
    decay = jnp.broadcast_to(jnp.exp(last), (8, LANES))
    b_turned = None
    for cols in reversed(strips(xbc_ref.shape[2])):
        ext[RIM:, cols] = mix_ref[0, :, cols].astype(F32)
        pre = conv_pre(ext, taps_ref, cols)
        act = (pre * jax.nn.sigmoid(pre)).astype(BF16)
        xbc_ref[0, :, cols] = act
        if cols.start >= inner:
            b_turned = turned(act[:, 0:LANES])
        else:
            held = spread_ref[:, cols]
            weighted = (act.astype(F32) * spread_heads(tail, held)).astype(BF16)
            kept = end_ref[0, :, cols] * spread_heads(decay, held)[0:1, :]
            end_ref[0, :, cols] = kept + dot(b_turned, weighted)

    @pl.when(place == pl.num_programs(1) - 1)
    def _():
        write_packed(packed_ref, end_ref[0], total_ref[0, 0:1, :])


def scan_kernel(
    xbc_ref, sum_ref, dt_ref, packed_ref, first_ref, second_ref, gate_ref, gm_ref, rows_ref, spread_ref,
    y_ref, mixed_ref, enter_ref, stat_ref, state,
):
    inner = spread_ref.shape[1]

    @pl.when(pl.program_id(1) == 0)
    def _():
        state[...] = entering_state(packed_ref, first_ref, second_ref, spread_ref)

    cumul = sum_ref[0]
    dt = dt_ref[0]
    across = jnp.transpose(cumul)
    last = cumul[CHUNK - 1 : CHUNK, :]
    tail = jnp.exp(last - cumul) * dt
    reach = jnp.exp(cumul)
    decay = jnp.broadcast_to(jnp.exp(last), (8, LANES))
    b_low = xbc_ref[0, :, inner : inner + LANES]
    c_low = xbc_ref[0, :, inner + LANES :]
    b_turned = turned(b_low)
    score = dot_nt(c_low, b_low)
    causal = iota2(HALF, HALF, 0) >= iota2(HALF, HALF, 1)
    first = iota2(1, LANES, 1) < LANES // 2
    squares = jnp.zeros((CHUNK, STRIP), F32)
    crossed = jnp.zeros((CHUNK, STRIP), F32)
    for cols in strips(inner):
        held = spread_ref[:, cols]
        x = xbc_ref[0, :, cols].astype(F32)
        u = x * spread_heads(dt, held)
        weighted = (x * spread_heads(tail, held)).astype(BF16)
        entering = state[:, cols].astype(BF16)
        enter_ref[0, 0, :, cols] = entering
        carried = dot(c_low, entering) * spread_heads(reach, held)
        state[:, cols] = state[:, cols] * spread_heads(decay, held)[0:1, :] + dot(b_turned, weighted)
        for pair in range(STRIP // LANES):
            lanes = slice(pair * LANES, (pair + 1) * LANES)
            top = carried[0:HALF, lanes]
            bottom = carried[HALF:, lanes]
            for side in range(2):
                head = (cols.start + pair * LANES) // (LANES // 2) + side
                mine = jnp.where(first if side == 0 else ~first, u[:, lanes], 0.0).astype(BF16)
                column = cumul[:, head : head + 1]
                row = across[head : head + 1, :]
                corner = jnp.where(causal, jnp.exp(column[0:HALF] - row[:, 0:HALF]), 0.0)
                top = top + dot((score[0:HALF, 0:HALF] * corner).astype(BF16), mine[0:HALF])
                left = jnp.exp(column[HALF:] - row[:, 0:HALF])
                right = jnp.where(causal, jnp.exp(column[HALF:] - row[:, HALF:]), 0.0)
                bottom = bottom + dot((score[HALF:, 0:HALF] * left).astype(BF16), mine[0:HALF])
                bottom = bottom + dot((score[HALF:, HALF:] * right).astype(BF16), mine[HALF:])
            into = slice(cols.start + pair * LANES, cols.start + (pair + 1) * LANES)
            y_ref[0, 0:HALF, into] = top
            y_ref[0, HALF:, into] = bottom
        y = y_ref[0, :, cols] + rows_ref[0:1, cols] * x
        gate = gate_ref[0, :, cols].astype(F32)
        gated = y * gate * jax.nn.sigmoid(gate)
        gained = gated * rows_ref[1:2, cols]
        mixed_ref[0, :, cols] = gained.astype(BF16)
        squares = squares + gated * gated
        crossed = crossed + gained * gm_ref[0, :, cols]
    ones = jnp.ones((8, STRIP), BF16)
    square_row = sum(dot_nt(ones, term) for term in pieces(squares, 3))
    cross_row = sum(dot_nt(ones, term) for term in pieces(crossed, 3))
    stat_ref[0] = jnp.where(iota2(8, CHUNK, 0) == 0, square_row, cross_row)


def gate_kernel(
    inner_full, y_ref, xbc_ref, gate_ref, gm_ref, stat_ref, sum_ref, total_ref, rows_ref, spread_ref,
    gy_ref, gz_ref, mixed_ref, back_ref, gain_ref, packed_ref,
):
    inner = spread_ref.shape[1]

    @pl.when(pl.program_id(1) == 0)
    def _():
        back_ref[...] = jnp.zeros_like(back_ref)

    @pl.when((pl.program_id(0) == 0) & (pl.program_id(1) == 0))
    def _():
        gain_ref[...] = jnp.zeros_like(gain_ref)

    stats = jnp.transpose(stat_ref[0])
    scale = lax.rsqrt(stats[:, 0:1] / inner_full + EPS)
    bent = scale * scale * scale * (stats[:, 1:2] / inner_full)
    cumul = sum_ref[0]
    reach = jnp.exp(cumul)
    decay = jnp.broadcast_to(jnp.exp(cumul[CHUNK - 1 : CHUNK, :]), (8, LANES))
    c_turned = turned(xbc_ref[0, :, inner + LANES :])
    for cols in strips(inner):
        held = spread_ref[:, cols]
        x = xbc_ref[0, :, cols].astype(F32)
        y = y_ref[0, :, cols] + rows_ref[0:1, cols] * x
        gate = gate_ref[0, :, cols].astype(F32)
        sigmoid = jax.nn.sigmoid(gate)
        silu = gate * sigmoid
        gated = y * silu
        scaled = gated * scale
        gm = gm_ref[0, :, cols]
        gain = rows_ref[1:2, cols]
        gg = scale * gm * gain - gated * bent
        gy = (gg * silu).astype(BF16)
        gy_ref[0, :, cols] = gy
        gz_ref[0, :, cols] = (gg * y * sigmoid * (1.0 + gate * (1.0 - sigmoid))).astype(BF16)
        mixed_ref[0, :, cols] = (scaled * gain).astype(BF16)
        gain_ref[:, cols] += jnp.broadcast_to(jnp.sum(gm * scaled, axis=0, keepdims=True), (8, STRIP))
        reached = (gy.astype(F32) * spread_heads(reach, held)).astype(BF16)
        kept = back_ref[0, :, cols] * spread_heads(decay, held)[0:1, :]
        back_ref[0, :, cols] = kept + dot(c_turned, reached)

    @pl.when(pl.program_id(1) == pl.num_programs(1) - 1)
    def _():
        write_packed(packed_ref, back_ref[0], total_ref[0, 0:1, :])


def adjoint_kernel(
    xbc_ref, sum_ref, dt_ref, gy_ref, y_ref, enter_ref, packed_ref, first_ref, second_ref, mix_ref, before_ref, halo_ref,
    step_ref, taps_ref, heads_ref, rows_ref, spread_ref,
    gmix_ref, rim_ref, gtaps_ref, gheads_ref, gskip_ref, back, ext, gpre, pulled,
):
    inner = spread_ref.shape[1]
    chunks = pl.num_programs(1)
    order = pl.program_id(1)

    @pl.when((pl.program_id(0) == 0) & (order == 0))
    def _():
        gtaps_ref[...] = jnp.zeros_like(gtaps_ref)
        gheads_ref[...] = jnp.zeros_like(gheads_ref)
        gskip_ref[...] = jnp.zeros_like(gskip_ref)

    @pl.when(order == 0)
    def _():
        back[...] = entering_state(packed_ref, first_ref, second_ref, spread_ref)
        gpre[CHUNK:, :] = jnp.zeros((8, gpre.shape[1]), F32)

    @pl.when(order > 0)
    def _():
        gpre[CHUNK:, :] = gpre[0:8, :]

    @pl.when(order == chunks - 1)
    def _():
        ext[0:RIM, :] = halo_ref[0].astype(F32)

    @pl.when(order < chunks - 1)
    def _():
        ext[0:RIM, :] = before_ref[0].astype(F32)

    cumul = sum_ref[0]
    dt = dt_ref[0]
    across = jnp.transpose(cumul)
    last = cumul[CHUNK - 1 : CHUNK, :]
    fade = jnp.exp(last - cumul)
    reach = jnp.exp(cumul)
    decay = jnp.broadcast_to(jnp.exp(last), (8, LANES))
    b_low = xbc_ref[0, :, inner : inner + LANES]
    c_low = xbc_ref[0, :, inner + LANES :]
    c_turned = turned(c_low)
    score = dot_nt(b_low, c_low)
    causal = iota2(HALF, HALF, 0) <= iota2(HALF, HALF, 1)
    first = iota2(1, LANES, 1) < LANES // 2
    pulled[...] = jnp.zeros_like(pulled)
    gb = jnp.zeros((CHUNK, LANES), F32)
    gc = jnp.zeros((CHUNK, LANES), F32)
    between = jnp.zeros((CHUNK, LANES), F32)
    arrived = jnp.zeros((CHUNK, LANES), F32)
    direct = jnp.zeros((CHUNK, LANES), F32)
    joined = jnp.zeros((8, LANES), F32)

    def conv_part(cols, gact):
        ext[RIM:, cols] = mix_ref[0, :, cols].astype(F32)
        pre = conv_pre(ext, taps_ref, cols)
        sigmoid = jax.nn.sigmoid(pre)
        gp = gact.astype(BF16).astype(F32) * sigmoid * (1.0 + pre * (1.0 - sigmoid))
        gpre[0:CHUNK, cols] = gp
        rim_ref[0, :, cols] = gp[0:8, :]
        total = taps_ref[3:4, cols] * gp
        for k in range(3):
            total = total + taps_ref[k : k + 1, cols] * gpre[pl.ds(3 - k, CHUNK), cols]
            gtaps_ref[k : k + 1, cols] += jnp.sum(
                gp * ext[pl.ds(RIM - 3 + k, CHUNK), cols], axis=0, keepdims=True
            )
        gtaps_ref[3:4, cols] += jnp.sum(gp * ext[RIM:, cols], axis=0, keepdims=True)
        gtaps_ref[4:5, cols] += jnp.sum(gp, axis=0, keepdims=True)
        gmix_ref[0, :, cols] = total.astype(BF16)

    for cols in strips(inner):
        held = spread_ref[:, cols]
        x = xbc_ref[0, :, cols].astype(F32)
        dt_wide = spread_heads(dt, held)
        fade_wide = spread_heads(fade, held)
        u = x * dt_wide
        u_low = u.astype(BF16)
        weighted = (u * fade_wide).astype(BF16)
        gy_low = gy_ref[0, :, cols]
        gy = gy_low.astype(F32)
        reached = (gy * spread_heads(reach, held)).astype(BF16)
        later = back[:, cols]
        later_low = later.astype(BF16)
        entered = enter_ref[0, 0, :, cols]
        gb = gb + dot_nt(weighted, later_low)
        gc = gc + dot_nt(reached, entered)
        gu_carried = dot(b_low, later_low) * fade_wide
        sums = jnp.sum(later * entered.astype(F32), axis=0, keepdims=True)
        joined = joined + gather_heads(jnp.broadcast_to(sums, (8, STRIP)), held)
        back[:, cols] = later * spread_heads(decay, held)[0:1, :] + dot(c_turned, reached)
        parts = []
        for pair in range(STRIP // LANES):
            lanes = slice(pair * LANES, (pair + 1) * LANES)
            top = gu_carried[0:HALF, lanes]
            bottom = gu_carried[HALF:, lanes]
            gy_pair = gy_low[:, lanes]
            for side in range(2):
                head = (cols.start + pair * LANES) // (LANES // 2) + side
                keep = first if side == 0 else ~first
                gy_mine = jnp.where(keep, gy[:, lanes], 0.0).astype(BF16)
                u_mine = jnp.where(keep, u[:, lanes], 0.0).astype(BF16)
                column = cumul[:, head : head + 1]
                row = across[head : head + 1, :]
                corner = jnp.where(causal, jnp.exp(row[:, 0:HALF] - column[0:HALF]), 0.0)
                side_right = jnp.exp(row[:, HALF:] - column[0:HALF])
                low_right = jnp.where(causal, jnp.exp(row[:, HALF:] - column[HALF:]), 0.0)
                top = top + dot((score[0:HALF, 0:HALF] * corner).astype(BF16), gy_mine[0:HALF])
                top = top + dot((score[0:HALF, HALF:] * side_right).astype(BF16), gy_mine[HALF:])
                bottom = bottom + dot((score[HALF:, HALF:] * low_right).astype(BF16), gy_mine[HALF:])
                upper = dot_nt(u_mine[0:HALF], gy_pair)
                pulled[0:HALF, 0:HALF] += upper[:, 0:HALF] * corner
                pulled[0:HALF, HALF:] += upper[:, HALF:] * side_right
                pulled[HALF:, HALF:] += dot_nt(u_mine[HALF:], gy_pair[HALF:]) * low_right
            parts.append(jnp.concatenate([top, bottom], axis=0))
        gu = jnp.concatenate(parts, axis=1)
        u_kept = u_low.astype(F32)
        between = between + gather_heads(gy * y_ref[0, :, cols] - u_kept * gu, held)
        arrived = arrived + gather_heads(u_kept * gu_carried, held)
        direct = direct + gather_heads(x * gu, held)
        gskip_ref[:, cols] += jnp.broadcast_to(jnp.sum(gy * x, axis=0, keepdims=True), (8, STRIP))
        conv_part(cols, dt_wide * gu + rows_ref[0:1, cols] * gy)

    pulled_low = pulled[...].astype(BF16)
    gb = gb + dot(pulled_low, c_low)
    gc = gc + dot(jnp.transpose(pulled[...]).astype(BF16), b_low)
    conv_part(slice(inner, inner + 2 * LANES), jnp.concatenate([gb, gc], axis=1))

    upper = (iota2(CHUNK, CHUNK, 0) <= iota2(CHUNK, CHUNK, 1)).astype(F32).astype(BF16)
    whole = jnp.sum(arrived, axis=0, keepdims=True) + decay[0:1, :] * joined[0:1, :]
    glg = running_sum(between, upper) + whole
    rate = heads_ref[1:2, :]
    gdt = direct + rate * glg
    raw = step_ref[0].astype(F32) + heads_ref[0:1, :]
    gsi = gdt * jax.nn.sigmoid(raw) * heads_ref[2:3, :]
    gmix_ref[0, :, inner + 2 * LANES :] = gsi.astype(BF16)
    gheads_ref[0:1, :] += jnp.sum(gsi, axis=0, keepdims=True)
    gheads_ref[1:2, :] += jnp.sum(glg * dt * rate, axis=0, keepdims=True)


def flat(width, order=lambda i: i, column=0):
    return pl.BlockSpec((1, CHUNK, width), lambda g, i: (g, order(i), column))


def whole(*shape):
    return pl.BlockSpec((1,) + shape, lambda g, i: (g,) + (0,) * len(shape))


def fixed(shape):
    return pl.BlockSpec(shape, lambda g, i: (0,) * len(shape))


def shaped(shape, dtype=F32):
    return jax.ShapeDtypeStruct(shape, dtype)


def run(kernel, grid, ins, outs, scratch, flops, moved, after=()):
    count = len(ins)
    extra = list(after)

    def body(*refs):
        kernel(*refs[:count], *refs[count + len(extra) :])

    steps = grid[0] * grid[1]
    return pl.pallas_call(
        body,
        grid=grid,
        in_specs=[spec for _, spec in ins] + [pl.BlockSpec(memory_space=pl.ANY)] * len(extra),
        out_specs=[spec for _, spec in outs],
        out_shape=[shape for shape, _ in outs],
        scratch_shapes=scratch,
        compiler_params=pltpu.CompilerParams(
            dimension_semantics=("arbitrary", "arbitrary"), vmem_limit_bytes=VMEM_BYTES
        ),
        cost_estimate=pl.CostEstimate(
            flops=steps * flops, bytes_accessed=steps * moved, transcendentals=0
        ),
    )(*[array for array, _ in ins], *extra)


def local_states(xw, halo, taps, heads, spread, after):
    groups, length, _ = xw.shape
    inner = spread.shape[1]
    width = inner + 2 * LANES
    return run(
        state_kernel,
        (groups, length // CHUNK),
        [
            (xw, flat(width)),
            (halo, whole(RIM, width)),
            (xw, flat(LANES, column=width // LANES)),
            (taps, fixed(taps.shape)),
            (heads, fixed(heads.shape)),
            (spread, fixed(spread.shape)),
        ],
        [
            (shaped((groups, length, width), BF16), flat(width)),
            (shaped((groups, length, LANES)), flat(LANES)),
            (shaped((groups, length, LANES)), flat(LANES)),
            (shaped((groups, LANES, inner)), whole(LANES, inner)),
            (shaped((groups, 8, LANES)), whole(8, LANES)),
            (shaped((groups, LANES + RIM, inner), BF16), whole(LANES + RIM, inner)),
        ],
        [pltpu.VMEM((RIM + CHUNK, width), F32)],
        1_500_000_000,
        2_000_000,
        after,
    )


def mixer(xbc, cumul, dt, start, gate, gm, rows, spread, after):
    groups, length, width = xbc.shape
    inner = spread.shape[1]
    chunks = length // CHUNK
    return run(
        scan_kernel,
        (groups, chunks),
        [
            (xbc, flat(width)),
            (cumul, flat(LANES)),
            (dt, flat(LANES)),
            (start[0], whole(LANES + RIM, inner)),
            (start[1], whole(LANES, inner)),
            (start[2], whole(LANES, inner)),
            (gate, flat(inner)),
            (gm, flat(inner)),
            (rows, fixed(rows.shape)),
            (spread, fixed(spread.shape)),
        ],
        [
            (shaped((groups, length, inner)), flat(inner)),
            (shaped(gate.shape, BF16), flat(inner)),
            (
                shaped((groups, chunks, LANES, inner), BF16),
                pl.BlockSpec((1, 1, LANES, inner), lambda g, i: (g, i, 0, 0)),
            ),
            (shaped((groups, 8, length)), pl.BlockSpec((1, 8, CHUNK), lambda g, i: (g, 0, i))),
        ],
        [pltpu.VMEM((LANES, inner), F32)],
        2_500_000_000,
        4_000_000,
        after,
    )


def gate_back(inner_full, y, xbc, gate, gm, stats, cumul, total, rows, spread, after):
    groups, length, width = xbc.shape
    inner = spread.shape[1]
    chunks = length // CHUNK
    back = lambda i: chunks - 1 - i
    return run(
        functools.partial(gate_kernel, float(inner_full)),
        (groups, chunks),
        [
            (y, flat(inner, back)),
            (xbc, flat(width, back)),
            (gate, flat(inner, back)),
            (gm, flat(inner, back)),
            (stats, pl.BlockSpec((1, 8, CHUNK), lambda g, i: (g, 0, back(i)))),
            (cumul, flat(LANES, back)),
            (total, whole(8, LANES)),
            (rows, fixed(rows.shape)),
            (spread, fixed(spread.shape)),
        ],
        [
            (shaped((groups, length, inner), BF16), flat(inner, back)),
            (shaped(gate.shape, BF16), flat(inner, back)),
            (shaped(gate.shape, BF16), flat(inner, back)),
            (shaped((groups, LANES, inner)), whole(LANES, inner)),
            (shaped((8, inner)), fixed((8, inner))),
            (shaped((groups, LANES + RIM, inner), BF16), whole(LANES + RIM, inner)),
        ],
        [],
        1_500_000_000,
        4_500_000,
        after,
    )


def adjoint(xbc, cumul, dt, gy, y, enter, gin, xw, halo, taps, heads, rows, spread, after):
    groups, length, width = xbc.shape
    inner = spread.shape[1]
    chunks = length // CHUNK
    back = lambda i: chunks - 1 - i
    per = CHUNK // RIM
    return run(
        adjoint_kernel,
        (groups, chunks),
        [
            (xbc, flat(width, back)),
            (cumul, flat(LANES, back)),
            (dt, flat(LANES, back)),
            (gy, flat(inner, back)),
            (y, flat(inner, back)),
            (enter, pl.BlockSpec((1, 1, LANES, inner), lambda g, i: (g, back(i), 0, 0))),
            (gin[0], whole(LANES + RIM, inner)),
            (gin[1], whole(LANES, inner)),
            (gin[2], whole(LANES, inner)),
            (xw, flat(width, back)),
            (
                xw,
                pl.BlockSpec(
                    (1, RIM, width), lambda g, i: (g, jnp.maximum(back(i) * per - 1, 0), 0)
                ),
            ),
            (halo, whole(RIM, width)),
            (xw, flat(LANES, back, width // LANES)),
            (taps, fixed(taps.shape)),
            (heads, fixed(heads.shape)),
            (rows, fixed(rows.shape)),
            (spread, fixed(spread.shape)),
        ],
        [
            (shaped((groups, length, width + LANES), BF16), flat(width + LANES, back)),
            (shaped((groups, 8, width)), whole(8, width)),
            (shaped((8, width)), fixed((8, width))),
            (shaped((8, LANES)), fixed((8, LANES))),
            (shaped((8, inner)), fixed((8, inner))),
        ],
        [
            pltpu.VMEM((LANES, inner), F32),
            pltpu.VMEM((RIM + CHUNK, width), F32),
            pltpu.VMEM((CHUNK + 8, width), F32),
            pltpu.VMEM((CHUNK, CHUNK), F32),
        ],
        8_000_000_000,
        6_000_000,
        after,
    )


def leave(ends, totals, packed, spread):
    groups, states, inner = ends.shape

    def one(*shape):
        return pl.BlockSpec((1,) + shape, lambda g: (g,) + (0,) * len(shape))

    return pl.pallas_call(
        leave_kernel,
        grid=(groups,),
        in_specs=[
            one(states, inner), one(8, LANES), one(states + RIM, inner),
            pl.BlockSpec(spread.shape, lambda g: (0, 0)),
        ],
        out_specs=one(states, inner),
        out_shape=shaped(ends.shape, BF16),
        compiler_params=pltpu.CompilerParams(
            dimension_semantics=("arbitrary",), vmem_limit_bytes=VMEM_BYTES
        ),
        cost_estimate=pl.CostEstimate(
            flops=0, bytes_accessed=8 * groups * states * inner, transcendentals=0
        ),
    )(ends, totals, packed, spread)


def place_kernel(at_ref, first, first_y, second, second_x, full_ref):
    step = pl.program_id(0)
    for number, ref in enumerate((first, first_y, second, second_x)):

        @pl.when(step // 2 == number)
        def _(ref=ref):
            full_ref[0, 0, 0] = ref[0]


def place_row(number, step, at):
    x, core, y = at[0], at[1], at[2]
    later = number // 2
    side = number % 2
    row = x + jnp.where(later == 0, step, side)
    column = y + jnp.where(later == 0, side, step)
    return row % 2, jnp.where(later == 0, core, 1 - core), column % 2, 0, 0


def place(first, first_y, second, second_x):
    _, rows, columns = first.shape
    at = jnp.stack([lax.axis_index(name) for name in ("x", "core", "y")]).astype(jnp.int32)

    def piece(number):
        return pl.BlockSpec(
            (1, rows, columns), lambda i, at: (jnp.clip(i - 2 * number, 0, 1), 0, 0)
        )

    full = pl.pallas_call(
        place_kernel,
        grid_spec=pltpu.PrefetchScalarGridSpec(
            num_scalar_prefetch=1,
            grid=(8,),
            in_specs=[piece(number) for number in range(4)],
            out_specs=pl.BlockSpec(
                (1, 1, 1, rows, columns), lambda i, at: place_row(i // 2, i % 2, at)
            ),
        ),
        out_shape=shaped((2, 2, 2, rows, columns), first.dtype),
        compiler_params=pltpu.CompilerParams(
            dimension_semantics=("arbitrary",), vmem_limit_bytes=VMEM_BYTES
        ),
        cost_estimate=pl.CostEstimate(
            flops=0, bytes_accessed=rows * columns, transcendentals=0
        ),
    )(at, first, first_y, second, second_x)
    return full.reshape(8 * rows, columns)


def join_kernel(at_ref, own, got, far_own, far_got, full_ref):
    half_is_own = pl.program_id(1) == at_ref[0]
    for core, (mine, other) in enumerate(((own, got), (far_own, far_got))):
        for ref, wanted in ((mine, half_is_own), (other, ~half_is_own)):

            @pl.when(wanted & (pl.program_id(0) == core))
            def _(ref=ref):
                full_ref[0] = ref[...]


def joined(own, got, far_own, far_got, part=0):
    _, rows, columns = own.shape
    at = lax.axis_index("zq").astype(jnp.int32)[None]
    piece = pl.BlockSpec((None, rows, columns), lambda c, h, at: (part, 0, 0))
    return pl.pallas_call(
        join_kernel,
        grid_spec=pltpu.PrefetchScalarGridSpec(
            num_scalar_prefetch=1,
            grid=(2, 2),
            in_specs=[piece] * 4,
            out_specs=pl.BlockSpec((1, rows, columns), lambda c, h, at: (c, h, 0)),
        ),
        out_shape=shaped((2, 2 * rows, columns), own.dtype),
        compiler_params=pltpu.CompilerParams(
            dimension_semantics=("arbitrary", "arbitrary"), vmem_limit_bytes=VMEM_BYTES
        ),
        cost_estimate=pl.CostEstimate(
            flops=0, bytes_accessed=16 * rows * columns, transcendentals=0
        ),
    )(at, own, got, far_own, far_got)


def swap(value, axis):
    return lax.ppermute(value, axis, [(0, 1), (1, 0)])


def sum_axis(value, axis):
    if lax.axis_size(axis) == 2:
        return value + swap(value, axis)
    return lax.psum(value, axis)


def cut(value, axis, dim):
    size = value.shape[dim] // 2
    at = lax.axis_index(axis)
    kept = lax.dynamic_slice_in_dim(value, at * size, size, dim)
    return kept, lax.dynamic_slice_in_dim(value, (1 - at) * size, size, dim)


def added(kept, got, dtype=BF16):
    return (kept.astype(F32) + got.astype(F32)).astype(dtype)


def hold(value, *before):
    if not before:
        return value
    return lax.optimization_barrier((value,) + before)[0]


def shift(value, by):
    blocks = lax.axis_size(("y", "zp"))
    pairs = [(i, i + by) for i in range(blocks) if 0 <= i + by < blocks]
    return lax.ppermute(value, ("y", "zp"), pairs)


def row_hop(packed, way, *before):
    return hold(lax.ppermute(packed, "zp", [(0, 1)] if way == 1 else [(1, 0)]), *before)


def column_hops(leaving, way, *before):
    source = 1 if way == 1 else 2
    pairs = [[(source, source + way * (1 + to))] for to in range(2)]
    return [hold(lax.ppermute(leaving, ("y", "zp"), pair), *before) for pair in pairs]


def chained(packed, way):
    blocks = lax.axis_size(("y", "zp"))
    groups, _, inner = packed.shape
    heads = inner // (LANES // 2)
    entering = jnp.zeros((groups, LANES, inner), F32)
    passed = jnp.zeros((groups, 1, LANES), F32)
    for by in range(1, blocks):
        got = shift(packed, by * way).astype(F32)
        weight = jnp.repeat(jnp.exp(passed[:, :, 0:heads]), LANES // 2, axis=2)
        entering = entering + weight * got[:, 0:LANES]
        passed = passed + jnp.sum(got[:, LANES:, 0:LANES], axis=1, keepdims=True)
    none = jnp.zeros(entering.shape, BF16)
    return jnp.pad(entering.astype(BF16), ((0, 0), (0, RIM), (0, 0))), none, none


def all_pairs():
    return all(lax.axis_size(name) == 2 for name in ("x", "y", "zp"))


NEAR = [(0, 1), (3, 2), (1, 3), (2, 0)]
FAR = [(1, 2), (2, 1)]
HOME = [(to, source) for source, to in NEAR]


def fetched(piece, near, far):
    at_home = lax.axis_index("core") == lax.axis_index("zp")
    return jnp.where(at_home, piece, near), jnp.where(at_home, near, far)


def fetch(piece):
    return lax.ppermute(piece, ("core", "zp"), NEAR), lax.ppermute(piece, ("core", "zp"), FAR)


def gather_slice(piece):
    owners = lax.axis_size("zp")
    rows = lax.all_gather(piece, ("x", "core", "y"), axis=0, tiled=True)
    parts = lax.all_gather(rows, "zp")
    return lax.dynamic_slice_in_dim(parts, lax.axis_index("core") * (owners // 2), owners // 2, 0)


def reduce_slice(parts):
    owners = lax.axis_size("zp")
    full = jnp.zeros((owners,) + parts.shape[1:], parts.dtype)
    full = lax.dynamic_update_slice_in_dim(
        full, parts, lax.axis_index("core") * (owners // 2), axis=0
    )
    mine = lax.psum_scatter(full, "zp", scatter_dimension=0, tiled=True)[0]
    mine = lax.psum_scatter(mine, ("x", "core", "y"), scatter_dimension=0, tiled=True)
    return mine.astype(F32)


def cut_rows(fulls):
    core = lax.axis_index("core")
    same, cross = [], []
    for full in fulls:
        rows, columns = full.shape[0] // 8, full.shape[1]
        full = full.reshape(2, 2, 2, rows, columns)
        same.append(cut(lax.dynamic_index_in_dim(full, core, 1, False), "x", 0))
        cross.append(cut(lax.dynamic_index_in_dim(full, 1 - core, 1, False), "y", 1))
    return (
        [kept[0] for kept, _ in same],
        [kept[:, 0] for kept, _ in cross],
        jnp.stack([sent[0] for _, sent in same]),
        jnp.stack([sent[:, 0] for _, sent in cross]),
    )


def cut_again(sames, crosses):
    same = [cut(value, "y", 0) for value in sames]
    cross = [cut(value, "x", 0) for value in crosses]
    return (
        [kept[0] for kept, _ in same],
        [kept[0] for kept, _ in cross],
        jnp.stack([sent[0] for _, sent in same]),
        jnp.stack([sent[0] for _, sent in cross]),
    )


def both(kept, got):
    return [
        [added(mine, other[k]) for k, mine in enumerate(values)]
        for values, other in zip(kept[0:2], got)
    ]


def home_parts(sames, crosses):
    at_home = lax.axis_index("core") == lax.axis_index("zp")
    cross = jnp.stack(crosses)
    return jnp.where(at_home, cross, jnp.stack(sames)), cross


def at_owner(near, far, sames):
    at_home = lax.axis_index("core") == lax.axis_index("zp")
    return [
        near[k].astype(F32) + jnp.where(at_home, same.astype(F32), far[k].astype(F32))
        for k, same in enumerate(sames)
    ]


def go_home(sent):
    return (
        lax.ppermute(sent[0], ("core", "zp"), HOME),
        lax.ppermute(sent[1], ("core", "zp"), FAR),
    )


def own_of_slice(value):
    owners = lax.axis_size("zp")
    core, part = lax.axis_index("core"), lax.axis_index("zp")
    other = swap(value, "core")
    share = value.shape[-1] // (owners // 2)
    wanted = jnp.where(part // (owners // 2) == core, value, other)
    return lax.dynamic_slice_in_dim(wanted, (part % (owners // 2)) * share, share, value.ndim - 1)


def slice_of_own(value, after):
    owners = lax.axis_size("zp")
    core = lax.axis_index("core")
    if owners == 2:
        other = hold(swap(value, "zp"), after)
        return jnp.where(core == lax.axis_index("zp"), value, other)[None]
    parts = lax.all_gather(value, "zp")
    return lax.dynamic_slice_in_dim(parts, core * (owners // 2), owners // 2, 0)


def per_device(
    hidden,
    cotangent,
    norm_gain,
    w_z,
    w_x,
    w_bc,
    w_dt,
    conv_x,
    conv_x_bias,
    conv_bc,
    conv_bc_bias,
    dt_bias,
    a_log,
    d_skip,
    inner_gain,
    w_out,
):
    micro, own_len, model = hidden.shape
    owners = lax.axis_size("zp")
    share = w_x.shape[1]
    own_heads = w_dt.shape[1]
    inner_full = share * 2 * owners
    states2 = w_bc.shape[1]
    halves = owners // 2
    inner = share * halves
    heads = own_heads * halves
    head_width = inner // heads
    width = inner + states2

    def matmul(left, right, contract, dtype=F32):
        return lax.dot_general(
            left, right, (contract, ((), ())), preferred_element_type=F32
        ).astype(dtype)

    def spliced(parts, sizes):
        if halves == 1:
            return parts[0]
        columns, at = [], 0
        for size, copies in sizes:
            columns += [parts[k][:, at : at + size] for k in range(halves if copies else 1)]
            at += size
        return jnp.concatenate(columns, axis=1)

    parts = range(micro)

    own = hidden.astype(F32)
    gain_in = norm_gain.astype(F32)
    r0 = lax.rsqrt(jnp.mean(own * own, axis=-1, keepdims=True) + EPS)
    filler = LANES // halves - own_heads
    own_first = jnp.concatenate(
        [w_x, w_bc, w_dt, jnp.zeros((w_dt.shape[0], filler), BF16)], axis=1
    )
    own_second = jnp.concatenate([w_z, jnp.transpose(w_out)], axis=1)
    normed_own = [(own[part : part + 1] * r0[part : part + 1] * gain_in).astype(BF16) for part in parts]
    fast = all_pairs()

    if fast:
        got = fetch(own_first)
        start = swap(normed_own[0], "zq")
        same, cross = fetched(own_first, *got)
        first = jnp.stack([same, swap(same, "x")])
        second = jnp.stack([cross, swap(cross, "y")])
        rest = swap(first, "y"), swap(second, "x")
        following = hold(normed_own[1:], first, second)
        started = [start] + [swap(value, "zq") for value in following]
        w_first = place(first, rest[0], second, rest[1])
        own_second = hold(own_second, w_first)
        got = fetch(own_second)
        later = [rest] + [(w_first,)] * (micro - 1)
    else:
        started = [swap(value, "zq") for value in normed_own]
        later = [()] * micro
        w_first = spliced(
            gather_slice(own_first), ((share, 1), (states2, 0), (own_heads, 1), (filler, 1))
        )
    fours = []
    for part in parts:
        value, got_tokens = normed_own[part], hold(started[part], *later[part])
        fours.append((value, got_tokens, swap(value, "core"), swap(got_tokens, "core")))
    normed = [joined(*four) for four in fours]

    scans = []
    for part in parts:
        xw = matmul(normed[part], w_first, ((2,), (0,)), BF16)
        scans.append((xw, shift(xw[:, -RIM:, 0:width], 1)))
        if part == 0:
            normed[-1] = hold(normed[-1], xw)
    if fast:
        same, cross = fetched(own_second, *hold(got, scans[-1][0]))
        moved = swap(same, "x"), swap(cross, "y")
        first, second = jnp.stack([same, moved[0]]), jnp.stack([cross, moved[1]])
        got_second = first, swap(first, "y"), second, swap(second, "x")
    per_head = jnp.concatenate([dt_bias, a_log, d_skip])
    per_head = jnp.pad(per_head, (0, share - 3 * own_heads))
    small = jnp.concatenate([conv_x, conv_x_bias[None], inner_gain[None]], axis=0).astype(F32)
    small = jnp.concatenate([small, per_head[None], jnp.zeros((1, share), F32)])
    small = slice_of_own(hold(small, scans[0][0]), scans[0][0])
    channel_rows = jnp.concatenate([small[k, 0:6] for k in range(halves)], axis=1)
    head_rows = jnp.concatenate(
        [small[k, 6, 0 : 3 * own_heads].reshape(3, own_heads) for k in range(halves)], axis=1
    )
    conv_shared = jnp.concatenate([conv_bc, conv_bc_bias[None]], axis=0).astype(F32)
    taps = jnp.pad(jnp.concatenate([channel_rows[0:5], conv_shared], axis=1), ((0, 3), (0, 0)))
    head_in = jnp.stack([head_rows[0], -jnp.exp(head_rows[1]), jnp.ones((heads,), F32)])
    head_in = jnp.pad(head_in, ((0, 5), (0, LANES - heads)))
    rows = jnp.stack([jnp.repeat(head_rows[2], head_width), channel_rows[5]])
    rows = jnp.pad(rows, ((0, 6), (0, 0)))
    spread = (
        lax.broadcasted_iota(jnp.int32, (LANES, inner), 1) // head_width
        == lax.broadcasted_iota(jnp.int32, (LANES, inner), 0)
    ).astype(BF16)

    local = []
    for part in parts:
        before = [k[5] for k in local[-1:]]
        local.append(local_states(*scans[part], taps, head_in, spread, before))
        if part == 0:
            cot_own = hold(cotangent, local[0][5], scans[-1][1])
            cot_own = [cot_own[k : k + 1] for k in parts]
            cot_got = [swap(value, "zq") for value in cot_own]
    totals = [local[part][4] for part in parts]
    packed = [local[part][5] for part in parts]
    if fast:
        w_second = place(*hold(got_second, packed[-1]))
    else:
        w_second = spliced(
            gather_slice(hold(own_second, packed[-1])), ((share, 1), (share, 1))
        )
    w_gate, w_down = w_second[:, 0:inner], w_second[:, inner:]
    def hop(part, packed, ends, way, *before):
        if not fast:
            return packed, packed
        got = row_hop(packed, way, *before)
        return got, leave(ends, totals[part], got, spread)

    def entering(found, way, *before):
        if not fast:
            return chained(found[0], way)
        return found[0], *column_hops(found[1], way, *before)

    found = [hop(0, packed[0], local[0][3], 1, w_second)]
    gate = [
        matmul(hold(normed[part], found[0][1]), w_gate, ((2,), (0,)), BF16) for part in parts
    ]
    cot_far = (
        swap(hold(cotangent, local[0][5]), "core"),
        [swap(hold(cot_got[k], gate[k]), "core") for k in parts],
    )

    def whole_cot(part, *before):
        far = hold((cot_far[0], cot_far[1][part]), *before)
        return joined(cot_own[part], cot_got[part], far[0][part : part + 1], far[1])

    cot = [whole_cot(0, gate[-1])]

    w_down_held = hold(w_down, found[0][1])
    gm = [matmul(cot[0], w_down_held, ((2,), (0,)))]
    mixes, stats, branches, gates = [], [], [], []
    g_gate = g_down = 0.0
    tokens = ((0, 1), (0, 1))
    for part in parts:
        xbc, cumul, dt = local[part][0:3]
        before = (gm[0],) if part == 0 else (gates[part - 1][5], gm[part])
        start = entering(found[part], 1, *before)
        y, gained, enter, stat = mixer(xbc, cumul, dt, start, gate[part], gm[part], rows, spread, before)
        mixes.append((y, enter))
        other = swap(stat, "core")
        if part + 1 < micro:
            following = hold(packed[part + 1], found[part][1])
            found.append(hop(part + 1, following, local[part + 1][3], 1, y))
            cot.append(whole_cot(part + 1, found[-1][1]))
            gm.append(matmul(cot[-1], w_down, ((2,), (0,))))
            other = hold(other, cot[-1])
        else:
            g_gate = matmul(normed[0], hold(gates[0][1], y), tokens)
            other = hold(other, g_gate)
        stat = stat + jnp.flip(other, 0)
        other = swap(stat, "zq")
        branch = matmul(hold(gained, stat, gm[-1]), w_down, ((2,), (1,)), BF16)
        stats.append(stat + hold(other, branch))
        branches.append((branch, swap(branch[1], "core")))
        gates.append(
            gate_back(
                inner_full, y, xbc, gate[part], gm[part], stats[part], cumul, totals[part],
                rows, spread, [branch],
            )
        )
    back_packed = [g[5] for g in gates]

    found = [hop(0, back_packed[0], gates[0][3], -1, back_packed[-1])]
    for part in parts:
        g_down = g_down + matmul(cot[part], hold(gates[part][2], found[0][1]), tokens)
        if part == 0:
            branch_cut = [
                cut(added(branch[0], hold(got, g_down)), "zq", 0) for branch, got in branches
            ]
            branch_sent = jnp.stack([sent for _, sent in branch_cut])
            branch_got = swap(branch_sent, "zq")
        else:
            g_gate = g_gate + matmul(normed[part], hold(gates[part][1], g_down), tokens)
    g_gate, g_down = g_gate.astype(BF16), g_down.astype(BF16)
    g_normed_gate = [matmul(hold(gates[0][1], g_gate), w_gate, ((2,), (1,)))]
    gin = entering(found[0], -1, g_normed_gate[0])
    for part in parts[1:]:
        following = hold(back_packed[part], found[part - 1][1])
        found.append(hop(part, following, gates[part][3], -1, g_normed_gate[0]))
    wait_for = [found[-1][1], branch_sent]
    if fast:
        second = cut_rows(hold([g_gate, g_down], *gin))
        moved = swap(second[2], "x"), swap(second[3], "y")
        wait_for += second[2:]

    g_first, heads_out, g_hidden, g_norm_gain = 0.0, [], [], 0.0

    def token_grad(part, kept, got):
        x, r, g = own[part], r0[part], added(kept, got, F32)
        q0 = g * gain_in
        grad = (
            cotangent[part].astype(F32) + r * q0
            - x * (r * r * r) * jnp.mean(q0 * x, axis=-1, keepdims=True)
        )
        return grad, jnp.sum(g * x * r, axis=0)

    def whole_output(*before):
        outputs = []
        for part in parts:
            square = lax.dynamic_slice_in_dim(
                stats[part][0, 0], lax.axis_index("zq") * own_len, own_len, 0
            )
            r1 = lax.rsqrt(square / inner_full + EPS)[:, None]
            got = hold(branch_got, *before)[part]
            outputs.append((own[part] + r1 * added(branch_cut[part][0], got, F32)).astype(BF16))
        return jnp.stack(outputs)

    for part in parts:
        xbc, cumul, dt = local[part][0:3]
        gmix, rim, *sums = adjoint(
            xbc, cumul, dt, gates[part][0], mixes[part][0], mixes[part][1], gin,
            *scans[part], taps, head_in, rows, spread, wait_for,
        )
        if part == micro - 1 and fast and micro > 1:
            got_home = hold(got_home, gmix)
            g_gate, g_down = at_owner(*got_home, pair[0])
            rim = hold(rim, g_gate, g_down)
        if part < micro - 1:
            gin = entering(found[part + 1], -1)
            gmix, rim, *sums = hold(
                (gmix, rim, *sums), *gin, branch_got, *(moved if fast else ())
            )
        heads_out.append(sums)
        ahead = shift(rim, -1)
        last_part = part == micro - 1
        if last_part:
            if micro > 1:
                kept, got = norm_cut
                grad, gain = token_grad(part - 1, kept, hold(got, gmix))
                g_hidden.append(grad)
                g_norm_gain = g_norm_gain + gain
                ahead = hold(ahead, grad)
        else:
            if fast:
                moved = hold(moved, gmix)
                second = cut_again(*both(second, moved))
                moved = swap(second[2], "y"), swap(second[3], "x")
        fix = jnp.stack(
            [sum(taps[k, :] * ahead[:, r - k] for k in range(r + 1)) for r in range(3)], axis=1
        )
        length = gmix.shape[1]
        last = gmix[:, length - RIM :].astype(F32)
        last = last + jnp.pad(fix, ((0, 0), (RIM - 3, 0), (0, LANES)))
        gmix = lax.dynamic_update_slice_in_dim(gmix, last.astype(BF16), length - RIM, 1)

        def for_weights(gmix):
            return g_first + matmul(normed[part], gmix, tokens)

        def for_tokens(gmix):
            total = g_normed_gate[part] + matmul(gmix, w_first, ((2,), (1,)))
            return total.astype(BF16)

        total = for_tokens(gmix)
        other = swap(total[1], "core")
        g_first = for_weights(hold(gmix, total))
        if last_part:
            g_first = g_first.astype(BF16)
            if fast:
                first = cut_rows([g_first])
                moved_first = swap(first[2], "x"), swap(first[3], "y")
        else:
            g_normed_gate.append(
                matmul(hold(gates[part + 1][1], g_first), w_gate, ((2,), (1,)))
            )
            kept, sent = cut(added(total[0], hold(other, g_first)), "zq", 0)
            norm_cut = kept, swap(sent, "zq")
            if part == micro - 2:
                outputs = whole_output(g_normed_gate[-1], sent)
            gin = hold(gin, outputs)
            wait_for = [sent, outputs]
            if fast and part == micro - 2:
                moved = hold(moved, g_normed_gate[-1])
                pair = both(second, moved)
                home = home_parts(*pair)
                wait_for += home
                got_home = go_home(home)

    kept, sent = cut(added(total[0], hold(other, g_first, *(first[2:] if fast else ()))), "zq", 0)
    got_norm = swap(sent, "zq")
    if fast:
        first = cut_again(*both(first, hold(moved_first, sent)))
        moved = swap(first[2], "y"), swap(first[3], "x")
        got_norm = hold(got_norm, *first[2:])
        pair = both(first, hold(moved, got_norm))
        home = home_parts(*pair)
        got_home = go_home(home)
        grad, gain = token_grad(micro - 1, kept, hold(got_norm, *home))
        g_first = at_owner(*hold(got_home, grad), pair[0])[0]
    else:
        g_gate, g_down = [
            reduce_slice(jnp.stack(jnp.split(value, halves, axis=1))) for value in (g_gate.astype(BF16), g_down.astype(BF16))
        ]
        grad, gain = token_grad(micro - 1, kept, got_norm)
        g_first = reduce_slice(
            jnp.concatenate(
                [
                    jnp.stack(jnp.split(g_first[:, 0:inner], halves, axis=1)),
                    jnp.concatenate(
                        [
                            g_first[None, :, inner:width],
                            jnp.zeros((halves - 1, model, states2), BF16),
                        ]
                    ),
                    jnp.stack(jnp.split(g_first[:, width : width + heads], halves, axis=1)),
                ],
                axis=2,
            )
        )
    g_hidden = jnp.stack(g_hidden + [grad])
    g_norm_gain = g_norm_gain + gain
    g_bc = g_first[:, share : share + states2]
    if fast:
        across = lax.ppermute(g_bc, ("zp", "zq"), [(0, 3), (3, 0), (1, 2), (2, 1)])
        g_bc = (g_bc + swap(g_bc, "zq")) + (swap(g_bc, "zp") + across)
    else:
        g_bc = sum_axis(sum_axis(g_bc, "zp"), "zq")

    g_taps, g_heads, g_skip = (sum(b[k] for b in heads_out) for k in range(3))
    g_gain = sum(g[4] for g in gates)
    skip_heads = jnp.sum(g_skip[0].reshape(heads, head_width), axis=1)
    small = jnp.concatenate(
        [g_taps[0:5, 0:inner].reshape(-1), g_gain[0], g_heads[0, 0:heads], g_heads[1, 0:heads], skip_heads]
    )
    size = small.shape[0]
    packed = jnp.concatenate([small, g_taps[0:5, inner:width].reshape(-1), g_norm_gain])
    packed = sum_axis(sum_axis(packed, "x"), "y")
    packed = sum_axis(hold(packed, g_first), "zp")
    small = packed[:size]
    shared = sum_axis(sum_axis(packed[size:], "core"), "zq")
    bc_rows = shared[0 : 5 * states2].reshape(5, states2)
    channel = own_of_slice(small[0 : 6 * inner].reshape(6, inner))
    per_head = own_of_slice(small[6 * inner :].reshape(3, heads))
    return (
        outputs,
        g_hidden,
        shared[5 * states2 :],
        g_gate,
        g_first[:, 0:share],
        g_bc,
        g_first[:, share + states2 : share + states2 + own_heads],
        channel[0:4],
        channel[4],
        bc_rows[0:4],
        bc_rows[4],
        per_head[0],
        per_head[1],
        per_head[2],
        channel[5],
        jnp.transpose(g_down),
    )


def solution(mesh):
    dp, seq, tensor = (mesh.shape[name] for name in ("dp", "seq", "tensor"))
    fine = Mesh(
        mesh.devices.reshape(dp // 2, 2, seq, tensor // 2, 2), ("x", "core", "y", "zp", "zq")
    )
    data, tens = ("x", "core", "y"), ("zp", "zq")
    tokens = P(("x", "core"), ("y", "zp", "zq"), None)
    params = (
        P(),
        P(data, tens),
        P(data, tens),
        P(data, None),
        P(data, tens),
        P(None, tens),
        P(tens),
        P(),
        P(),
        P(tens),
        P(tens),
        P(tens),
        P(tens),
        P(tens, data),
    )
    return jax.shard_map(
        per_device,
        mesh=fine,
        in_specs=(tokens, tokens) + params,
        out_specs=(tokens, tokens) + params,
        check_vma=False,
    )
```

```python
import functools

import jax
import jax.numpy as jnp
from jax import lax
from jax.experimental import pallas as pl
from jax.experimental.pallas import tpu as pltpu
from jax.sharding import Mesh
from jax.sharding import PartitionSpec as P

CHUNK = 256
HALF = CHUNK // 2
LANES = 128
STRIP = 256
RIM = 16
EPS = 1e-05
F32 = jnp.float32
BF16 = jnp.bfloat16
VMEM_BYTES = 48 * 1024 * 1024


def dot(left, right):
    return lax.dot_general(left, right, (((1,), (0,)), ((), ())), preferred_element_type=F32)


def dot_nt(left, right):
    return lax.dot_general(left, right, (((1,), (1,)), ((), ())), preferred_element_type=F32)


def pieces(value, count):
    terms = []
    for _ in range(count):
        term = value.astype(BF16)
        terms.append(term)
        value = value - term.astype(F32)
    return terms


def spread_heads(value, spread):
    return sum(dot(term, spread) for term in pieces(value, 2))


def gather_heads(value, spread):
    return sum(dot_nt(term, spread) for term in pieces(value, 2))


def running_sum(value, mask):
    return sum(dot(mask, term) for term in pieces(value, 3))


def iota2(rows, cols, dim):
    return lax.broadcasted_iota(jnp.int32, (rows, cols), dim)


def turned(value):
    return jnp.transpose(value.astype(F32)).astype(BF16)


def strips(width):
    return [slice(at, at + STRIP) for at in range(0, width, STRIP)]


def conv_pre(ext, taps, cols):
    total = taps[4:5, cols] + taps[0:1, cols] * ext[pl.ds(RIM - 3, CHUNK), cols]
    for k in range(1, 4):
        total = total + taps[k : k + 1, cols] * ext[pl.ds(RIM - 3 + k, CHUNK), cols]
    return total


def softplus(value):
    return jnp.maximum(value, 0.0) + jnp.log1p(jnp.exp(-jnp.abs(value)))


def write_packed(packed_ref, end, total):
    packed_ref[0, 0:LANES, :] = end.astype(BF16)
    packed_ref[0, LANES:, :] = jnp.zeros((RIM, end.shape[1]), BF16)
    row = iota2(RIM, LANES, 0)
    logs = jnp.zeros((RIM, LANES), F32)
    for k, term in enumerate(pieces(total, 3)):
        logs = jnp.where(row == k, term.astype(F32), logs)
    packed_ref[0, LANES:, 0:LANES] = logs.astype(BF16)


def widened(log, spread):
    return spread_heads(jnp.broadcast_to(jnp.exp(log), (8, LANES)), spread)[0:1, :]


def entering_state(packed_ref, first_ref, second_ref, spread_ref):
    passed = jnp.sum(packed_ref[0, LANES:, 0:LANES].astype(F32), axis=0, keepdims=True)
    from_row = first_ref[0].astype(F32) + second_ref[0].astype(F32)
    return packed_ref[0, 0:LANES, :].astype(F32) + widened(passed, spread_ref[...]) * from_row


def leave_kernel(end_ref, total_ref, packed_ref, spread_ref, leaving_ref):
    kept = packed_ref[0, 0:LANES, :].astype(F32) * widened(total_ref[0, 0:1, :], spread_ref[...])
    leaving_ref[0] = (end_ref[0] + kept).astype(BF16)


def state_kernel(
    mix_ref, halo_ref, step_ref, taps_ref, heads_ref, spread_ref,
    xbc_ref, sum_ref, dt_ref, end_ref, total_ref, packed_ref, ext,
):
    inner = spread_ref.shape[1]
    place = pl.program_id(1)

    @pl.when(place == 0)
    def _():
        ext[0:RIM, :] = halo_ref[0].astype(F32)
        end_ref[...] = jnp.zeros_like(end_ref)
        total_ref[...] = jnp.zeros_like(total_ref)

    @pl.when(place > 0)
    def _():
        ext[0:RIM, :] = ext[CHUNK : CHUNK + RIM, :]

    dt = softplus(step_ref[0].astype(F32) + heads_ref[0:1, :])
    lower = (iota2(CHUNK, CHUNK, 0) >= iota2(CHUNK, CHUNK, 1)).astype(F32).astype(BF16)
    cumul = running_sum(dt * heads_ref[1:2, :], lower)
    sum_ref[0] = cumul
    dt_ref[0] = dt
    last = cumul[CHUNK - 1 : CHUNK, :]
    total_ref[0] += jnp.broadcast_to(last, total_ref.shape[1:])
    tail = jnp.exp(last - cumul) * dt
    decay = jnp.broadcast_to(jnp.exp(last), (8, LANES))
    b_turned = None
    for cols in reversed(strips(xbc_ref.shape[2])):
        ext[RIM:, cols] = mix_ref[0, :, cols].astype(F32)
        pre = conv_pre(ext, taps_ref, cols)
        act = (pre * jax.nn.sigmoid(pre)).astype(BF16)
        xbc_ref[0, :, cols] = act
        if cols.start >= inner:
            b_turned = turned(act[:, 0:LANES])
        else:
            held = spread_ref[:, cols]
            weighted = (act.astype(F32) * spread_heads(tail, held)).astype(BF16)
            kept = end_ref[0, :, cols] * spread_heads(decay, held)[0:1, :]
            end_ref[0, :, cols] = kept + dot(b_turned, weighted)

    @pl.when(place == pl.num_programs(1) - 1)
    def _():
        write_packed(packed_ref, end_ref[0], total_ref[0, 0:1, :])


def scan_kernel(
    xbc_ref, sum_ref, dt_ref, packed_ref, first_ref, second_ref, gate_ref, gm_ref, rows_ref, spread_ref,
    y_ref, mixed_ref, enter_ref, stat_ref, state,
):
    inner = spread_ref.shape[1]

    @pl.when(pl.program_id(1) == 0)
    def _():
        state[...] = entering_state(packed_ref, first_ref, second_ref, spread_ref)

    cumul = sum_ref[0]
    dt = dt_ref[0]
    across = jnp.transpose(cumul)
    last = cumul[CHUNK - 1 : CHUNK, :]
    tail = jnp.exp(last - cumul) * dt
    reach = jnp.exp(cumul)
    decay = jnp.broadcast_to(jnp.exp(last), (8, LANES))
    b_low = xbc_ref[0, :, inner : inner + LANES]
    c_low = xbc_ref[0, :, inner + LANES :]
    b_turned = turned(b_low)
    score = dot_nt(c_low, b_low)
    causal = iota2(HALF, HALF, 0) >= iota2(HALF, HALF, 1)
    first = iota2(1, LANES, 1) < LANES // 2
    squares = jnp.zeros((CHUNK, STRIP), F32)
    crossed = jnp.zeros((CHUNK, STRIP), F32)
    for cols in strips(inner):
        held = spread_ref[:, cols]
        x = xbc_ref[0, :, cols].astype(F32)
        u = x * spread_heads(dt, held)
        weighted = (x * spread_heads(tail, held)).astype(BF16)
        entering = state[:, cols].astype(BF16)
        enter_ref[0, 0, :, cols] = entering
        carried = dot(c_low, entering) * spread_heads(reach, held)
        state[:, cols] = state[:, cols] * spread_heads(decay, held)[0:1, :] + dot(b_turned, weighted)
        for pair in range(STRIP // LANES):
            lanes = slice(pair * LANES, (pair + 1) * LANES)
            top = carried[0:HALF, lanes]
            bottom = carried[HALF:, lanes]
            for side in range(2):
                head = (cols.start + pair * LANES) // (LANES // 2) + side
                mine = jnp.where(first if side == 0 else ~first, u[:, lanes], 0.0).astype(BF16)
                column = cumul[:, head : head + 1]
                row = across[head : head + 1, :]
                corner = jnp.where(causal, jnp.exp(column[0:HALF] - row[:, 0:HALF]), 0.0)
                top = top + dot((score[0:HALF, 0:HALF] * corner).astype(BF16), mine[0:HALF])
                left = jnp.exp(column[HALF:] - row[:, 0:HALF])
                right = jnp.where(causal, jnp.exp(column[HALF:] - row[:, HALF:]), 0.0)
                bottom = bottom + dot((score[HALF:, 0:HALF] * left).astype(BF16), mine[0:HALF])
                bottom = bottom + dot((score[HALF:, HALF:] * right).astype(BF16), mine[HALF:])
            into = slice(cols.start + pair * LANES, cols.start + (pair + 1) * LANES)
            y_ref[0, 0:HALF, into] = top
            y_ref[0, HALF:, into] = bottom
        y = y_ref[0, :, cols] + rows_ref[0:1, cols] * x
        gate = gate_ref[0, :, cols].astype(F32)
        gated = y * gate * jax.nn.sigmoid(gate)
        gained = gated * rows_ref[1:2, cols]
        mixed_ref[0, :, cols] = gained.astype(BF16)
        squares = squares + gated * gated
        crossed = crossed + gained * gm_ref[0, :, cols].astype(F32)
    ones = jnp.ones((8, STRIP), BF16)
    square_row = sum(dot_nt(ones, term) for term in pieces(squares, 3))
    cross_row = sum(dot_nt(ones, term) for term in pieces(crossed, 3))
    stat_ref[0] = jnp.where(iota2(8, CHUNK, 0) == 0, square_row, cross_row)


def gate_kernel(
    inner_full, y_ref, xbc_ref, gate_ref, gm_ref, stat_ref, sum_ref, total_ref, rows_ref, spread_ref,
    gy_ref, gz_ref, mixed_ref, back_ref, gain_ref, packed_ref,
):
    inner = spread_ref.shape[1]

    @pl.when(pl.program_id(1) == 0)
    def _():
        back_ref[...] = jnp.zeros_like(back_ref)

    @pl.when((pl.program_id(0) == 0) & (pl.program_id(1) == 0))
    def _():
        gain_ref[...] = jnp.zeros_like(gain_ref)

    stats = jnp.transpose(stat_ref[0])
    scale = lax.rsqrt(stats[:, 0:1] / inner_full + EPS)
    bent = scale * scale * scale * (stats[:, 1:2] / inner_full)
    cumul = sum_ref[0]
    reach = jnp.exp(cumul)
    decay = jnp.broadcast_to(jnp.exp(cumul[CHUNK - 1 : CHUNK, :]), (8, LANES))
    c_turned = turned(xbc_ref[0, :, inner + LANES :])
    for cols in strips(inner):
        held = spread_ref[:, cols]
        x = xbc_ref[0, :, cols].astype(F32)
        y = y_ref[0, :, cols] + rows_ref[0:1, cols] * x
        gate = gate_ref[0, :, cols].astype(F32)
        sigmoid = jax.nn.sigmoid(gate)
        silu = gate * sigmoid
        gated = y * silu
        scaled = gated * scale
        gm = gm_ref[0, :, cols].astype(F32)
        gain = rows_ref[1:2, cols]
        gg = scale * gm * gain - gated * bent
        gy = (gg * silu).astype(BF16)
        gy_ref[0, :, cols] = gy
        gz_ref[0, :, cols] = (gg * y * sigmoid * (1.0 + gate * (1.0 - sigmoid))).astype(BF16)
        mixed_ref[0, :, cols] = (scaled * gain).astype(BF16)
        gain_ref[:, cols] += jnp.broadcast_to(jnp.sum(gm * scaled, axis=0, keepdims=True), (8, STRIP))
        reached = (gy.astype(F32) * spread_heads(reach, held)).astype(BF16)
        kept = back_ref[0, :, cols] * spread_heads(decay, held)[0:1, :]
        back_ref[0, :, cols] = kept + dot(c_turned, reached)

    @pl.when(pl.program_id(1) == pl.num_programs(1) - 1)
    def _():
        write_packed(packed_ref, back_ref[0], total_ref[0, 0:1, :])


def adjoint_kernel(
    xbc_ref, sum_ref, dt_ref, gy_ref, y_ref, enter_ref, packed_ref, first_ref, second_ref, mix_ref, before_ref, halo_ref,
    step_ref, taps_ref, heads_ref, rows_ref, spread_ref,
    gmix_ref, rim_ref, gtaps_ref, gheads_ref, gskip_ref, back, ext, gpre, pulled,
):
    inner = spread_ref.shape[1]
    chunks = pl.num_programs(1)
    order = pl.program_id(1)

    @pl.when((pl.program_id(0) == 0) & (order == 0))
    def _():
        gtaps_ref[...] = jnp.zeros_like(gtaps_ref)
        gheads_ref[...] = jnp.zeros_like(gheads_ref)
        gskip_ref[...] = jnp.zeros_like(gskip_ref)

    @pl.when(order == 0)
    def _():
        back[...] = entering_state(packed_ref, first_ref, second_ref, spread_ref)
        gpre[CHUNK:, :] = jnp.zeros((8, gpre.shape[1]), F32)

    @pl.when(order > 0)
    def _():
        gpre[CHUNK:, :] = gpre[0:8, :]

    @pl.when(order == chunks - 1)
    def _():
        ext[0:RIM, :] = halo_ref[0].astype(F32)

    @pl.when(order < chunks - 1)
    def _():
        ext[0:RIM, :] = before_ref[0].astype(F32)

    cumul = sum_ref[0]
    dt = dt_ref[0]
    across = jnp.transpose(cumul)
    last = cumul[CHUNK - 1 : CHUNK, :]
    fade = jnp.exp(last - cumul)
    reach = jnp.exp(cumul)
    decay = jnp.broadcast_to(jnp.exp(last), (8, LANES))
    b_low = xbc_ref[0, :, inner : inner + LANES]
    c_low = xbc_ref[0, :, inner + LANES :]
    c_turned = turned(c_low)
    score = dot_nt(b_low, c_low)
    causal = iota2(HALF, HALF, 0) <= iota2(HALF, HALF, 1)
    first = iota2(1, LANES, 1) < LANES // 2
    pulled[...] = jnp.zeros_like(pulled)
    gb = jnp.zeros((CHUNK, LANES), F32)
    gc = jnp.zeros((CHUNK, LANES), F32)
    between = jnp.zeros((CHUNK, LANES), F32)
    arrived = jnp.zeros((CHUNK, LANES), F32)
    direct = jnp.zeros((CHUNK, LANES), F32)
    joined = jnp.zeros((8, LANES), F32)

    def conv_part(cols, gact):
        ext[RIM:, cols] = mix_ref[0, :, cols].astype(F32)
        pre = conv_pre(ext, taps_ref, cols)
        sigmoid = jax.nn.sigmoid(pre)
        gp = gact.astype(BF16).astype(F32) * sigmoid * (1.0 + pre * (1.0 - sigmoid))
        gpre[0:CHUNK, cols] = gp
        rim_ref[0, :, cols] = gp[0:8, :]
        total = taps_ref[3:4, cols] * gp
        for k in range(3):
            total = total + taps_ref[k : k + 1, cols] * gpre[pl.ds(3 - k, CHUNK), cols]
            gtaps_ref[k : k + 1, cols] += jnp.sum(
                gp * ext[pl.ds(RIM - 3 + k, CHUNK), cols], axis=0, keepdims=True
            )
        gtaps_ref[3:4, cols] += jnp.sum(gp * ext[RIM:, cols], axis=0, keepdims=True)
        gtaps_ref[4:5, cols] += jnp.sum(gp, axis=0, keepdims=True)
        gmix_ref[0, :, cols] = total.astype(BF16)

    for cols in strips(inner):
        held = spread_ref[:, cols]
        x = xbc_ref[0, :, cols].astype(F32)
        dt_wide = spread_heads(dt, held)
        fade_wide = spread_heads(fade, held)
        u = x * dt_wide
        u_low = u.astype(BF16)
        weighted = (u * fade_wide).astype(BF16)
        gy_low = gy_ref[0, :, cols]
        gy = gy_low.astype(F32)
        reached = (gy * spread_heads(reach, held)).astype(BF16)
        later = back[:, cols]
        later_low = later.astype(BF16)
        entered = enter_ref[0, 0, :, cols]
        gb = gb + dot_nt(weighted, later_low)
        gc = gc + dot_nt(reached, entered)
        gu_carried = dot(b_low, later_low) * fade_wide
        sums = jnp.sum(later * entered.astype(F32), axis=0, keepdims=True)
        joined = joined + gather_heads(jnp.broadcast_to(sums, (8, STRIP)), held)
        back[:, cols] = later * spread_heads(decay, held)[0:1, :] + dot(c_turned, reached)
        parts = []
        for pair in range(STRIP // LANES):
            lanes = slice(pair * LANES, (pair + 1) * LANES)
            top = gu_carried[0:HALF, lanes]
            bottom = gu_carried[HALF:, lanes]
            gy_pair = gy_low[:, lanes]
            for side in range(2):
                head = (cols.start + pair * LANES) // (LANES // 2) + side
                keep = first if side == 0 else ~first
                gy_mine = jnp.where(keep, gy[:, lanes], 0.0).astype(BF16)
                u_mine = jnp.where(keep, u[:, lanes], 0.0).astype(BF16)
                column = cumul[:, head : head + 1]
                row = across[head : head + 1, :]
                corner = jnp.where(causal, jnp.exp(row[:, 0:HALF] - column[0:HALF]), 0.0)
                side_right = jnp.exp(row[:, HALF:] - column[0:HALF])
                low_right = jnp.where(causal, jnp.exp(row[:, HALF:] - column[HALF:]), 0.0)
                top = top + dot((score[0:HALF, 0:HALF] * corner).astype(BF16), gy_mine[0:HALF])
                top = top + dot((score[0:HALF, HALF:] * side_right).astype(BF16), gy_mine[HALF:])
                bottom = bottom + dot((score[HALF:, HALF:] * low_right).astype(BF16), gy_mine[HALF:])
                upper = dot_nt(u_mine[0:HALF], gy_pair)
                pulled[0:HALF, 0:HALF] += upper[:, 0:HALF] * corner
                pulled[0:HALF, HALF:] += upper[:, HALF:] * side_right
                pulled[HALF:, HALF:] += dot_nt(u_mine[HALF:], gy_pair[HALF:]) * low_right
            parts.append(jnp.concatenate([top, bottom], axis=0))
        gu = jnp.concatenate(parts, axis=1)
        u_kept = u_low.astype(F32)
        between = between + gather_heads(gy * y_ref[0, :, cols] - u_kept * gu, held)
        arrived = arrived + gather_heads(u_kept * gu_carried, held)
        direct = direct + gather_heads(x * gu, held)
        gskip_ref[:, cols] += jnp.broadcast_to(jnp.sum(gy * x, axis=0, keepdims=True), (8, STRIP))
        conv_part(cols, dt_wide * gu + rows_ref[0:1, cols] * gy)

    pulled_low = pulled[...].astype(BF16)
    gb = gb + dot(pulled_low, c_low)
    gc = gc + dot(jnp.transpose(pulled[...]).astype(BF16), b_low)
    conv_part(slice(inner, inner + 2 * LANES), jnp.concatenate([gb, gc], axis=1))

    upper = (iota2(CHUNK, CHUNK, 0) <= iota2(CHUNK, CHUNK, 1)).astype(F32).astype(BF16)
    whole = jnp.sum(arrived, axis=0, keepdims=True) + decay[0:1, :] * joined[0:1, :]
    glg = running_sum(between, upper) + whole
    rate = heads_ref[1:2, :]
    gdt = direct + rate * glg
    raw = step_ref[0].astype(F32) + heads_ref[0:1, :]
    gsi = gdt * jax.nn.sigmoid(raw) * heads_ref[2:3, :]
    gmix_ref[0, :, inner + 2 * LANES :] = gsi.astype(BF16)
    gheads_ref[0:1, :] += jnp.sum(gsi, axis=0, keepdims=True)
    gheads_ref[1:2, :] += jnp.sum(glg * dt * rate, axis=0, keepdims=True)


def flat(width, order=lambda i: i, column=0):
    return pl.BlockSpec((1, CHUNK, width), lambda g, i: (g, order(i), column))


def whole(*shape):
    return pl.BlockSpec((1,) + shape, lambda g, i: (g,) + (0,) * len(shape))


def fixed(shape):
    return pl.BlockSpec(shape, lambda g, i: (0,) * len(shape))


def shaped(shape, dtype=F32):
    return jax.ShapeDtypeStruct(shape, dtype)


def run(kernel, grid, ins, outs, scratch, flops, moved, after=()):
    count = len(ins)
    extra = list(after)

    def body(*refs):
        kernel(*refs[:count], *refs[count + len(extra) :])

    steps = grid[0] * grid[1]
    return pl.pallas_call(
        body,
        grid=grid,
        in_specs=[spec for _, spec in ins] + [pl.BlockSpec(memory_space=pl.ANY)] * len(extra),
        out_specs=[spec for _, spec in outs],
        out_shape=[shape for shape, _ in outs],
        scratch_shapes=scratch,
        compiler_params=pltpu.CompilerParams(
            dimension_semantics=("arbitrary", "arbitrary"), vmem_limit_bytes=VMEM_BYTES
        ),
        cost_estimate=pl.CostEstimate(
            flops=steps * flops, bytes_accessed=steps * moved, transcendentals=0
        ),
    )(*[array for array, _ in ins], *extra)


def local_states(xw, halo, taps, heads, spread, after):
    groups, length, _ = xw.shape
    inner = spread.shape[1]
    width = inner + 2 * LANES
    return run(
        state_kernel,
        (groups, length // CHUNK),
        [
            (xw, flat(width)),
            (halo, whole(RIM, width)),
            (xw, flat(LANES, column=width // LANES)),
            (taps, fixed(taps.shape)),
            (heads, fixed(heads.shape)),
            (spread, fixed(spread.shape)),
        ],
        [
            (shaped((groups, length, width), BF16), flat(width)),
            (shaped((groups, length, LANES)), flat(LANES)),
            (shaped((groups, length, LANES)), flat(LANES)),
            (shaped((groups, LANES, inner)), whole(LANES, inner)),
            (shaped((groups, 8, LANES)), whole(8, LANES)),
            (shaped((groups, LANES + RIM, inner), BF16), whole(LANES + RIM, inner)),
        ],
        [pltpu.VMEM((RIM + CHUNK, width), F32)],
        1_500_000_000,
        2_000_000,
        after,
    )


def mixer(xbc, cumul, dt, start, gate, gm, rows, spread, after):
    groups, length, width = xbc.shape
    inner = spread.shape[1]
    chunks = length // CHUNK
    return run(
        scan_kernel,
        (groups, chunks),
        [
            (xbc, flat(width)),
            (cumul, flat(LANES)),
            (dt, flat(LANES)),
            (start[0], whole(LANES + RIM, inner)),
            (start[1], whole(LANES, inner)),
            (start[2], whole(LANES, inner)),
            (gate, flat(inner)),
            (gm, flat(inner)),
            (rows, fixed(rows.shape)),
            (spread, fixed(spread.shape)),
        ],
        [
            (shaped((groups, length, inner)), flat(inner)),
            (shaped(gate.shape, BF16), flat(inner)),
            (
                shaped((groups, chunks, LANES, inner), BF16),
                pl.BlockSpec((1, 1, LANES, inner), lambda g, i: (g, i, 0, 0)),
            ),
            (shaped((groups, 8, length)), pl.BlockSpec((1, 8, CHUNK), lambda g, i: (g, 0, i))),
        ],
        [pltpu.VMEM((LANES, inner), F32)],
        2_500_000_000,
        4_000_000,
        after,
    )


def gate_back(inner_full, y, xbc, gate, gm, stats, cumul, total, rows, spread, after):
    groups, length, width = xbc.shape
    inner = spread.shape[1]
    chunks = length // CHUNK
    back = lambda i: chunks - 1 - i
    return run(
        functools.partial(gate_kernel, float(inner_full)),
        (groups, chunks),
        [
            (y, flat(inner, back)),
            (xbc, flat(width, back)),
            (gate, flat(inner, back)),
            (gm, flat(inner, back)),
            (stats, pl.BlockSpec((1, 8, CHUNK), lambda g, i: (g, 0, back(i)))),
            (cumul, flat(LANES, back)),
            (total, whole(8, LANES)),
            (rows, fixed(rows.shape)),
            (spread, fixed(spread.shape)),
        ],
        [
            (shaped((groups, length, inner), BF16), flat(inner, back)),
            (shaped(gate.shape, BF16), flat(inner, back)),
            (shaped(gate.shape, BF16), flat(inner, back)),
            (shaped((groups, LANES, inner)), whole(LANES, inner)),
            (shaped((8, inner)), fixed((8, inner))),
            (shaped((groups, LANES + RIM, inner), BF16), whole(LANES + RIM, inner)),
        ],
        [],
        1_500_000_000,
        4_500_000,
        after,
    )


def adjoint(xbc, cumul, dt, gy, y, enter, gin, xw, halo, taps, heads, rows, spread, after):
    groups, length, width = xbc.shape
    inner = spread.shape[1]
    chunks = length // CHUNK
    back = lambda i: chunks - 1 - i
    per = CHUNK // RIM
    return run(
        adjoint_kernel,
        (groups, chunks),
        [
            (xbc, flat(width, back)),
            (cumul, flat(LANES, back)),
            (dt, flat(LANES, back)),
            (gy, flat(inner, back)),
            (y, flat(inner, back)),
            (enter, pl.BlockSpec((1, 1, LANES, inner), lambda g, i: (g, back(i), 0, 0))),
            (gin[0], whole(LANES + RIM, inner)),
            (gin[1], whole(LANES, inner)),
            (gin[2], whole(LANES, inner)),
            (xw, flat(width, back)),
            (
                xw,
                pl.BlockSpec(
                    (1, RIM, width), lambda g, i: (g, jnp.maximum(back(i) * per - 1, 0), 0)
                ),
            ),
            (halo, whole(RIM, width)),
            (xw, flat(LANES, back, width // LANES)),
            (taps, fixed(taps.shape)),
            (heads, fixed(heads.shape)),
            (rows, fixed(rows.shape)),
            (spread, fixed(spread.shape)),
        ],
        [
            (shaped((groups, length, width + LANES), BF16), flat(width + LANES, back)),
            (shaped((groups, 8, width)), whole(8, width)),
            (shaped((8, width)), fixed((8, width))),
            (shaped((8, LANES)), fixed((8, LANES))),
            (shaped((8, inner)), fixed((8, inner))),
        ],
        [
            pltpu.VMEM((LANES, inner), F32),
            pltpu.VMEM((RIM + CHUNK, width), F32),
            pltpu.VMEM((CHUNK + 8, width), F32),
            pltpu.VMEM((CHUNK, CHUNK), F32),
        ],
        8_000_000_000,
        6_000_000,
        after,
    )


def leave(ends, totals, packed, spread):
    groups, states, inner = ends.shape

    def one(*shape):
        return pl.BlockSpec((1,) + shape, lambda g: (g,) + (0,) * len(shape))

    return pl.pallas_call(
        leave_kernel,
        grid=(groups,),
        in_specs=[
            one(states, inner), one(8, LANES), one(states + RIM, inner),
            pl.BlockSpec(spread.shape, lambda g: (0, 0)),
        ],
        out_specs=one(states, inner),
        out_shape=shaped(ends.shape, BF16),
        compiler_params=pltpu.CompilerParams(
            dimension_semantics=("arbitrary",), vmem_limit_bytes=VMEM_BYTES
        ),
        cost_estimate=pl.CostEstimate(
            flops=0, bytes_accessed=8 * groups * states * inner, transcendentals=0
        ),
    )(ends, totals, packed, spread)


def place_kernel(at_ref, first, first_y, second, second_x, full_ref):
    step = pl.program_id(0)
    for number, ref in enumerate((first, first_y, second, second_x)):

        @pl.when(step // 2 == number)
        def _(ref=ref):
            full_ref[0, 0, 0] = ref[0]


def place_row(number, step, at):
    x, core, y = at[0], at[1], at[2]
    later = number // 2
    side = number % 2
    row = x + jnp.where(later == 0, step, side)
    column = y + jnp.where(later == 0, side, step)
    return row % 2, jnp.where(later == 0, core, 1 - core), column % 2, 0, 0


def place(first, first_y, second, second_x):
    _, rows, columns = first.shape
    at = jnp.stack([lax.axis_index(name) for name in ("x", "core", "y")]).astype(jnp.int32)

    def piece(number):
        return pl.BlockSpec(
            (1, rows, columns), lambda i, at: (jnp.clip(i - 2 * number, 0, 1), 0, 0)
        )

    full = pl.pallas_call(
        place_kernel,
        grid_spec=pltpu.PrefetchScalarGridSpec(
            num_scalar_prefetch=1,
            grid=(8,),
            in_specs=[piece(number) for number in range(4)],
            out_specs=pl.BlockSpec(
                (1, 1, 1, rows, columns), lambda i, at: place_row(i // 2, i % 2, at)
            ),
        ),
        out_shape=shaped((2, 2, 2, rows, columns), first.dtype),
        compiler_params=pltpu.CompilerParams(
            dimension_semantics=("arbitrary",), vmem_limit_bytes=VMEM_BYTES
        ),
        cost_estimate=pl.CostEstimate(
            flops=0, bytes_accessed=rows * columns, transcendentals=0
        ),
    )(at, first, first_y, second, second_x)
    return full.reshape(8 * rows, columns)


def join_kernel(at_ref, own, got, far_own, far_got, full_ref):
    half_is_own = pl.program_id(1) == at_ref[0]
    for core, (mine, other) in enumerate(((own, got), (far_own, far_got))):
        for ref, wanted in ((mine, half_is_own), (other, ~half_is_own)):

            @pl.when(wanted & (pl.program_id(0) == core))
            def _(ref=ref):
                full_ref[0] = ref[...]


def joined(own, got, far_own, far_got, part=0):
    _, rows, columns = own.shape
    at = lax.axis_index("zq").astype(jnp.int32)[None]
    piece = pl.BlockSpec((None, rows, columns), lambda c, h, at: (part, 0, 0))
    return pl.pallas_call(
        join_kernel,
        grid_spec=pltpu.PrefetchScalarGridSpec(
            num_scalar_prefetch=1,
            grid=(2, 2),
            in_specs=[piece] * 4,
            out_specs=pl.BlockSpec((1, rows, columns), lambda c, h, at: (c, h, 0)),
        ),
        out_shape=shaped((2, 2 * rows, columns), own.dtype),
        compiler_params=pltpu.CompilerParams(
            dimension_semantics=("arbitrary", "arbitrary"), vmem_limit_bytes=VMEM_BYTES
        ),
        cost_estimate=pl.CostEstimate(
            flops=0, bytes_accessed=16 * rows * columns, transcendentals=0
        ),
    )(at, own, got, far_own, far_got)


def swap(value, axis):
    return lax.ppermute(value, axis, [(0, 1), (1, 0)])


def sum_axis(value, axis):
    if lax.axis_size(axis) == 2:
        return value + swap(value, axis)
    return lax.psum(value, axis)


def cut(value, axis, dim):
    size = value.shape[dim] // 2
    at = lax.axis_index(axis)
    kept = lax.dynamic_slice_in_dim(value, at * size, size, dim)
    return kept, lax.dynamic_slice_in_dim(value, (1 - at) * size, size, dim)


def added(kept, got, dtype=BF16):
    return (kept.astype(F32) + got.astype(F32)).astype(dtype)


def hold(value, *before):
    if not before:
        return value
    return lax.optimization_barrier((value,) + before)[0]


def shift(value, by):
    blocks = lax.axis_size(("y", "zp"))
    pairs = [(i, i + by) for i in range(blocks) if 0 <= i + by < blocks]
    return lax.ppermute(value, ("y", "zp"), pairs)


def row_hop(packed, way, *before):
    return hold(lax.ppermute(packed, "zp", [(0, 1)] if way == 1 else [(1, 0)]), *before)


def column_hops(leaving, way, *before):
    source = 1 if way == 1 else 2
    pairs = [[(source, source + way * (1 + to))] for to in range(2)]
    return [hold(lax.ppermute(leaving, ("y", "zp"), pair), *before) for pair in pairs]


def chained(packed, way):
    blocks = lax.axis_size(("y", "zp"))
    groups, _, inner = packed.shape
    heads = inner // (LANES // 2)
    entering = jnp.zeros((groups, LANES, inner), F32)
    passed = jnp.zeros((groups, 1, LANES), F32)
    for by in range(1, blocks):
        got = shift(packed, by * way).astype(F32)
        weight = jnp.repeat(jnp.exp(passed[:, :, 0:heads]), LANES // 2, axis=2)
        entering = entering + weight * got[:, 0:LANES]
        passed = passed + jnp.sum(got[:, LANES:, 0:LANES], axis=1, keepdims=True)
    none = jnp.zeros(entering.shape, BF16)
    return jnp.pad(entering.astype(BF16), ((0, 0), (0, RIM), (0, 0))), none, none


def all_pairs():
    return all(lax.axis_size(name) == 2 for name in ("x", "y", "zp"))


NEAR = [(0, 1), (3, 2), (1, 3), (2, 0)]
FAR = [(1, 2), (2, 1)]
HOME = [(to, source) for source, to in NEAR]


def fetched(piece, near, far):
    at_home = lax.axis_index("core") == lax.axis_index("zp")
    return jnp.where(at_home, piece, near), jnp.where(at_home, near, far)


def fetch(piece):
    return lax.ppermute(piece, ("core", "zp"), NEAR), lax.ppermute(piece, ("core", "zp"), FAR)


def gather_slice(piece):
    owners = lax.axis_size("zp")
    rows = lax.all_gather(piece, ("x", "core", "y"), axis=0, tiled=True)
    parts = lax.all_gather(rows, "zp")
    return lax.dynamic_slice_in_dim(parts, lax.axis_index("core") * (owners // 2), owners // 2, 0)


def reduce_slice(parts):
    owners = lax.axis_size("zp")
    full = jnp.zeros((owners,) + parts.shape[1:], parts.dtype)
    full = lax.dynamic_update_slice_in_dim(
        full, parts, lax.axis_index("core") * (owners // 2), axis=0
    )
    mine = lax.psum_scatter(full, "zp", scatter_dimension=0, tiled=True)[0]
    mine = lax.psum_scatter(mine, ("x", "core", "y"), scatter_dimension=0, tiled=True)
    return mine.astype(F32)


def cut_rows(fulls):
    core = lax.axis_index("core")
    same, cross = [], []
    for full in fulls:
        rows, columns = full.shape[0] // 8, full.shape[1]
        full = full.reshape(2, 2, 2, rows, columns)
        same.append(cut(lax.dynamic_index_in_dim(full, core, 1, False), "x", 0))
        cross.append(cut(lax.dynamic_index_in_dim(full, 1 - core, 1, False), "y", 1))
    return (
        [kept[0] for kept, _ in same],
        [kept[:, 0] for kept, _ in cross],
        jnp.stack([sent[0] for _, sent in same]),
        jnp.stack([sent[:, 0] for _, sent in cross]),
    )


def cut_again(sames, crosses):
    same = [cut(value, "y", 0) for value in sames]
    cross = [cut(value, "x", 0) for value in crosses]
    return (
        [kept[0] for kept, _ in same],
        [kept[0] for kept, _ in cross],
        jnp.stack([sent[0] for _, sent in same]),
        jnp.stack([sent[0] for _, sent in cross]),
    )


def both(kept, got):
    return [
        [added(mine, other[k]) for k, mine in enumerate(values)]
        for values, other in zip(kept[0:2], got)
    ]


def home_parts(sames, crosses):
    at_home = lax.axis_index("core") == lax.axis_index("zp")
    cross = jnp.stack(crosses)
    return jnp.where(at_home, cross, jnp.stack(sames)), cross


def at_owner(near, far, sames):
    at_home = lax.axis_index("core") == lax.axis_index("zp")
    return [
        near[k].astype(F32) + jnp.where(at_home, same.astype(F32), far[k].astype(F32))
        for k, same in enumerate(sames)
    ]


def go_home(sent):
    return (
        lax.ppermute(sent[0], ("core", "zp"), HOME),
        lax.ppermute(sent[1], ("core", "zp"), FAR),
    )


def own_of_slice(value):
    owners = lax.axis_size("zp")
    core, part = lax.axis_index("core"), lax.axis_index("zp")
    other = swap(value, "core")
    share = value.shape[-1] // (owners // 2)
    wanted = jnp.where(part // (owners // 2) == core, value, other)
    return lax.dynamic_slice_in_dim(wanted, (part % (owners // 2)) * share, share, value.ndim - 1)


def slice_of_own(value, after):
    owners = lax.axis_size("zp")
    core = lax.axis_index("core")
    if owners == 2:
        other = hold(swap(value, "zp"), after)
        return jnp.where(core == lax.axis_index("zp"), value, other)[None]
    parts = lax.all_gather(value, "zp")
    return lax.dynamic_slice_in_dim(parts, core * (owners // 2), owners // 2, 0)


def per_device(
    hidden,
    cotangent,
    norm_gain,
    w_z,
    w_x,
    w_bc,
    w_dt,
    conv_x,
    conv_x_bias,
    conv_bc,
    conv_bc_bias,
    dt_bias,
    a_log,
    d_skip,
    inner_gain,
    w_out,
):
    micro, own_len, model = hidden.shape
    owners = lax.axis_size("zp")
    share = w_x.shape[1]
    own_heads = w_dt.shape[1]
    inner_full = share * 2 * owners
    states2 = w_bc.shape[1]
    halves = owners // 2
    inner = share * halves
    heads = own_heads * halves
    head_width = inner // heads
    width = inner + states2

    def matmul(left, right, contract, dtype=F32):
        return lax.dot_general(
            left, right, (contract, ((), ())), preferred_element_type=F32
        ).astype(dtype)

    def spliced(parts, sizes):
        if halves == 1:
            return parts[0]
        columns, at = [], 0
        for size, copies in sizes:
            columns += [parts[k][:, at : at + size] for k in range(halves if copies else 1)]
            at += size
        return jnp.concatenate(columns, axis=1)

    parts = range(micro)

    own = hidden.astype(F32)
    gain_in = norm_gain.astype(F32)
    r0 = lax.rsqrt(jnp.mean(own * own, axis=-1, keepdims=True) + EPS)
    filler = LANES // halves - own_heads
    own_first = jnp.concatenate(
        [w_x, w_bc, w_dt, jnp.zeros((w_dt.shape[0], filler), BF16)], axis=1
    )
    own_second = jnp.concatenate([w_z, jnp.transpose(w_out)], axis=1)
    normed_own = [(own[part : part + 1] * r0[part : part + 1] * gain_in).astype(BF16) for part in parts]
    fast = all_pairs()

    def tokens_of(value, *before):
        got = hold(swap(value, "zq"), *before)
        return value, got, swap(value, "core"), swap(got, "core")

    if fast:
        got = fetch(own_first)
    fours = [tokens_of(normed_own[0])]
    if fast:
        same, cross = fetched(own_first, *got)
        moved = hold((swap(same, "x"), swap(cross, "y")), fours[0][1])
        first, second = jnp.stack([same, moved[0]]), jnp.stack([cross, moved[1]])
        own_second = hold(own_second, fours[0][1], *moved)
        got = fetch(own_second)
        rest = swap(first, "y"), swap(second, "x")
        later = first, second
    else:
        later = (fours[0][1],)
    for part in parts[1:]:
        fours.append(tokens_of(hold(normed_own[part], fours[0][1]), *later))
        later = (fours[-1][1],)
    if fast:
        w_first = place(first, rest[0], second, rest[1])
        got = hold(got, w_first)
        same, cross = fetched(own_second, *got)
        moved = swap(same, "x"), swap(cross, "y")
    else:
        w_first = spliced(
            gather_slice(own_first), ((share, 1), (states2, 0), (own_heads, 1), (filler, 1))
        )
    normed = [joined(*four) for four in fours]
    per_head = jnp.concatenate([dt_bias, a_log, d_skip])
    per_head = jnp.pad(per_head, (0, share - 3 * own_heads))
    small = jnp.concatenate([conv_x, conv_x_bias[None], inner_gain[None]], axis=0).astype(F32)
    small = jnp.concatenate([small, per_head[None], jnp.zeros((1, share), F32)])
    small = slice_of_own(small, w_first)
    channel_rows = jnp.concatenate([small[k, 0:6] for k in range(halves)], axis=1)
    head_rows = jnp.concatenate(
        [small[k, 6, 0 : 3 * own_heads].reshape(3, own_heads) for k in range(halves)], axis=1
    )
    conv_shared = jnp.concatenate([conv_bc, conv_bc_bias[None]], axis=0).astype(F32)
    taps = jnp.pad(jnp.concatenate([channel_rows[0:5], conv_shared], axis=1), ((0, 3), (0, 0)))
    head_in = jnp.stack([head_rows[0], -jnp.exp(head_rows[1]), jnp.ones((heads,), F32)])
    head_in = jnp.pad(head_in, ((0, 5), (0, LANES - heads)))
    rows = jnp.stack([jnp.repeat(head_rows[2], head_width), channel_rows[5]])
    rows = jnp.pad(rows, ((0, 6), (0, 0)))
    spread = (
        lax.broadcasted_iota(jnp.int32, (LANES, inner), 1) // head_width
        == lax.broadcasted_iota(jnp.int32, (LANES, inner), 0)
    ).astype(BF16)

    scans = []
    for part in parts:
        xw = matmul(normed[part], w_first, ((2,), (0,)), BF16)
        scans.append((xw, shift(xw[:, -RIM:, 0:width], 1)))
        if part == 0:
            normed[-1] = hold(normed[-1], xw)
    if fast:
        moved = hold(moved, scans[0][0])
        first, second = jnp.stack([same, moved[0]]), jnp.stack([cross, moved[1]])
        got_second = first, swap(first, "y"), second, swap(second, "x")
    local = []
    for part in parts:
        before = [k[5] for k in local[-1:]]
        local.append(local_states(*scans[part], taps, head_in, spread, before))
        if part == 0:
            cot_own = hold(cotangent, local[0][5], scans[-1][1])
            cot_own = [cot_own[k : k + 1] for k in parts]
            cot_got = [swap(value, "zq") for value in cot_own]
    totals = [local[part][4] for part in parts]
    packed = [local[part][5] for part in parts]
    if fast:
        w_second = place(*hold(got_second, packed[-1]))
    else:
        w_second = spliced(
            gather_slice(hold(own_second, packed[-1])), ((share, 1), (share, 1))
        )
    w_gate, w_down = w_second[:, 0:inner], w_second[:, inner:]
    def hop(part, packed, ends, way, *before):
        if not fast:
            return packed, packed
        got = row_hop(packed, way, *before)
        return got, leave(ends, totals[part], got, spread)

    def entering(found, way, *before):
        if not fast:
            return chained(found[0], way)
        return found[0], *column_hops(found[1], way, *before)

    found = [hop(0, packed[0], local[0][3], 1, w_second)]
    gate = [
        matmul(hold(normed[part], found[0][1]), w_gate, ((2,), (0,)), BF16) for part in parts
    ]
    cot_far = (
        swap(hold(cotangent, local[0][5]), "core"),
        [swap(hold(cot_got[k], gate[k]), "core") for k in parts],
    )

    def whole_cot(part, *before):
        far = hold((cot_far[0], cot_far[1][part]), *before)
        return joined(cot_own[part], cot_got[part], far[0][part : part + 1], far[1])

    cot = [whole_cot(0, gate[-1])]

    w_down_held = hold(w_down, found[0][1])
    gm = [matmul(cot[0], w_down_held, ((2,), (0,)), BF16)]
    mixes, stats, branches, gates = [], [], [], []
    g_gate = g_down = 0.0
    tokens = ((0, 1), (0, 1))
    for part in parts:
        xbc, cumul, dt = local[part][0:3]
        before = (gm[0],) if part == 0 else (gates[part - 1][5], gm[part])
        start = entering(found[part], 1, *before)
        y, gained, enter, stat = mixer(xbc, cumul, dt, start, gate[part], gm[part], rows, spread, before)
        mixes.append((y, enter))
        other = swap(stat, "core")
        if part + 1 < micro:
            following = hold(packed[part + 1], found[part][1])
            found.append(hop(part + 1, following, local[part + 1][3], 1, y))
            cot.append(whole_cot(part + 1, found[-1][1]))
            gm.append(matmul(cot[-1], w_down, ((2,), (0,)), BF16))
            other = hold(other, cot[-1])
        else:
            g_gate = matmul(normed[0], hold(gates[0][1], y), tokens, BF16)
            other = hold(other, g_gate)
        stat = stat + jnp.flip(other, 0)
        other = swap(stat, "zq")
        branch = matmul(hold(gained, stat, gm[-1]), w_down, ((2,), (1,)), BF16)
        stats.append(stat + hold(other, branch))
        branches.append((branch, swap(branch[1], "core")))
        gates.append(
            gate_back(
                inner_full, y, xbc, gate[part], gm[part], stats[part], cumul, totals[part],
                rows, spread, [branch],
            )
        )
    back_packed = [g[5] for g in gates]

    found = [hop(0, back_packed[0], gates[0][3], -1, back_packed[-1])]
    for part in parts:
        g_down = (g_down + matmul(cot[part], hold(gates[part][2], found[0][1]), tokens)).astype(BF16)
        if part == 0:
            branch_cut = [
                cut(added(branch[0], hold(got, g_down)), "zq", 0) for branch, got in branches
            ]
            branch_sent = jnp.stack([sent for _, sent in branch_cut])
            branch_got = swap(branch_sent, "zq")
        else:
            g_gate = g_gate + matmul(normed[part], hold(gates[part][1], g_down), tokens)
    g_gate, g_down = g_gate.astype(BF16), g_down.astype(BF16)
    g_normed_gate = [matmul(hold(gates[0][1], g_gate), w_gate, ((2,), (1,)), BF16)]
    gin = entering(found[0], -1, g_normed_gate[0])
    for part in parts[1:]:
        following = hold(back_packed[part], found[part - 1][1])
        found.append(hop(part, following, gates[part][3], -1, g_normed_gate[0]))
    wait_for = [found[-1][1], branch_sent]
    if fast:
        second = cut_rows(hold([g_gate, g_down], *gin))
        moved = swap(second[2], "x"), swap(second[3], "y")
        wait_for += second[2:]

    g_first, heads_out, g_hidden, g_norm_gain = 0.0, [], [], 0.0

    def token_grad(part, kept, got):
        x, r, g = own[part], r0[part], added(kept, got, F32)
        q0 = g * gain_in
        grad = (
            cotangent[part].astype(F32) + r * q0
            - x * (r * r * r) * jnp.mean(q0 * x, axis=-1, keepdims=True)
        )
        return grad, jnp.sum(g * x * r, axis=0)

    def whole_output(*before):
        outputs = []
        for part in parts:
            square = lax.dynamic_slice_in_dim(
                stats[part][0, 0], lax.axis_index("zq") * own_len, own_len, 0
            )
            r1 = lax.rsqrt(square / inner_full + EPS)[:, None]
            got = hold(branch_got, *before)[part]
            outputs.append((own[part] + r1 * added(branch_cut[part][0], got, F32)).astype(BF16))
        return jnp.stack(outputs)

    for part in parts:
        xbc, cumul, dt = local[part][0:3]
        gmix, rim, *sums = adjoint(
            xbc, cumul, dt, gates[part][0], mixes[part][0], mixes[part][1], gin,
            *scans[part], taps, head_in, rows, spread, wait_for,
        )
        if part == micro - 1 and fast and micro > 1:
            got_home = hold(got_home, gmix)
            g_gate, g_down = at_owner(*got_home, pair[0])
            rim = hold(rim, g_gate, g_down)
        if part < micro - 1:
            gin = entering(found[part + 1], -1)
            gmix, rim, *sums = hold(
                (gmix, rim, *sums), *gin, branch_got, *(moved if fast else ())
            )
        heads_out.append(sums)
        ahead = shift(rim, -1)
        last_part = part == micro - 1
        if last_part:
            if micro > 1:
                kept, got = norm_cut
                grad, gain = token_grad(part - 1, kept, hold(got, gmix))
                g_hidden.append(grad)
                g_norm_gain = g_norm_gain + gain
                ahead = hold(ahead, grad)
        else:
            if fast:
                moved = hold(moved, gmix)
                second = cut_again(*both(second, moved))
                moved = swap(second[2], "y"), swap(second[3], "x")
        fix = jnp.stack(
            [sum(taps[k, :] * ahead[:, r - k] for k in range(r + 1)) for r in range(3)], axis=1
        )
        length = gmix.shape[1]
        last = gmix[:, length - RIM :].astype(F32)
        last = last + jnp.pad(fix, ((0, 0), (RIM - 3, 0), (0, LANES)))
        gmix = lax.dynamic_update_slice_in_dim(gmix, last.astype(BF16), length - RIM, 1)

        def for_weights(gmix):
            return (g_first + matmul(normed[part], gmix, tokens)).astype(BF16)

        def for_tokens(gmix):
            total = g_normed_gate[part] + matmul(gmix, w_first, ((2,), (1,)))
            return total.astype(BF16)

        total = for_tokens(gmix)
        other = swap(total[1], "core")
        g_first = for_weights(hold(gmix, total))
        if last_part:
            g_first = g_first.astype(BF16)
            if fast:
                first = cut_rows([g_first])
                moved_first = swap(first[2], "x"), swap(first[3], "y")
        else:
            g_normed_gate.append(
                matmul(hold(gates[part + 1][1], g_first), w_gate, ((2,), (1,)), BF16)
            )
            kept, sent = cut(added(total[0], hold(other, g_first)), "zq", 0)
            norm_cut = kept, swap(sent, "zq")
            if part == micro - 2:
                outputs = whole_output(g_normed_gate[-1], sent)
            gin = hold(gin, outputs)
            wait_for = [sent, outputs]
            if fast and part == micro - 2:
                moved = hold(moved, g_normed_gate[-1])
                pair = both(second, moved)
                home = home_parts(*pair)
                wait_for += home
                got_home = go_home(home)

    kept, sent = cut(added(total[0], hold(other, g_first, *(first[2:] if fast else ()))), "zq", 0)
    got_norm = swap(sent, "zq")
    if fast:
        first = cut_again(*both(first, hold(moved_first, sent)))
        moved = swap(first[2], "y"), swap(first[3], "x")
        got_norm = hold(got_norm, *first[2:])
        pair = both(first, hold(moved, got_norm))
        home = home_parts(*pair)
        got_home = go_home(home)
        grad, gain = token_grad(micro - 1, kept, hold(got_norm, *home))
        g_first = at_owner(*hold(got_home, grad), pair[0])[0]
    else:
        g_gate, g_down = [
            reduce_slice(jnp.stack(jnp.split(value, halves, axis=1))) for value in (g_gate.astype(BF16), g_down.astype(BF16))
        ]
        grad, gain = token_grad(micro - 1, kept, got_norm)
        g_first = reduce_slice(
            jnp.concatenate(
                [
                    jnp.stack(jnp.split(g_first[:, 0:inner], halves, axis=1)),
                    jnp.concatenate(
                        [
                            g_first[None, :, inner:width],
                            jnp.zeros((halves - 1, model, states2), BF16),
                        ]
                    ),
                    jnp.stack(jnp.split(g_first[:, width : width + heads], halves, axis=1)),
                ],
                axis=2,
            )
        )
    g_hidden = jnp.stack(g_hidden + [grad])
    g_norm_gain = g_norm_gain + gain
    g_bc = g_first[:, share : share + states2]
    if fast:
        across = lax.ppermute(g_bc, ("zp", "zq"), [(0, 3), (3, 0), (1, 2), (2, 1)])
        g_bc = (g_bc + swap(g_bc, "zq")) + (swap(g_bc, "zp") + across)
    else:
        g_bc = sum_axis(sum_axis(g_bc, "zp"), "zq")

    g_taps, g_heads, g_skip = (sum(b[k] for b in heads_out) for k in range(3))
    g_gain = sum(g[4] for g in gates)
    skip_heads = jnp.sum(g_skip[0].reshape(heads, head_width), axis=1)
    small = jnp.concatenate(
        [g_taps[0:5, 0:inner].reshape(-1), g_gain[0], g_heads[0, 0:heads], g_heads[1, 0:heads], skip_heads]
    )
    size = small.shape[0]
    packed = jnp.concatenate([small, g_taps[0:5, inner:width].reshape(-1), g_norm_gain])
    packed = sum_axis(sum_axis(packed, "x"), "y")
    packed = sum_axis(hold(packed, g_first), "zp")
    small = packed[:size]
    shared = sum_axis(sum_axis(packed[size:], "core"), "zq")
    bc_rows = shared[0 : 5 * states2].reshape(5, states2)
    channel = own_of_slice(small[0 : 6 * inner].reshape(6, inner))
    per_head = own_of_slice(small[6 * inner :].reshape(3, heads))
    return (
        outputs,
        g_hidden,
        shared[5 * states2 :],
        g_gate,
        g_first[:, 0:share],
        g_bc,
        g_first[:, share + states2 : share + states2 + own_heads],
        channel[0:4],
        channel[4],
        bc_rows[0:4],
        bc_rows[4],
        per_head[0],
        per_head[1],
        per_head[2],
        channel[5],
        jnp.transpose(g_down),
    )


def solution(mesh):
    dp, seq, tensor = (mesh.shape[name] for name in ("dp", "seq", "tensor"))
    fine = Mesh(
        mesh.devices.reshape(dp // 2, 2, seq, tensor // 2, 2), ("x", "core", "y", "zp", "zq")
    )
    data, tens = ("x", "core", "y"), ("zp", "zq")
    tokens = P(("x", "core"), ("y", "zp", "zq"), None)
    params = (
        P(),
        P(data, tens),
        P(data, tens),
        P(data, None),
        P(data, tens),
        P(None, tens),
        P(tens),
        P(),
        P(),
        P(tens),
        P(tens),
        P(tens),
        P(tens),
        P(tens, data),
    )
    return jax.shard_map(
        per_device,
        mesh=fine,
        in_specs=(tokens, tokens) + params,
        out_specs=(tokens, tokens) + params,
        check_vma=False,
    )
```

```python
import functools

import jax
import jax.numpy as jnp
from jax import lax
from jax.experimental import pallas as pl
from jax.experimental.pallas import tpu as pltpu
from jax.sharding import Mesh
from jax.sharding import PartitionSpec as P

CHUNK = 256
HALF = CHUNK // 2
LANES = 128
STRIP = 256
RIM = 16
EPS = 1e-05
F32 = jnp.float32
BF16 = jnp.bfloat16
VMEM_BYTES = 32 * 1024 * 1024


def dot(left, right):
    return lax.dot_general(left, right, (((1,), (0,)), ((), ())), preferred_element_type=F32)


def dot_nt(left, right):
    return lax.dot_general(left, right, (((1,), (1,)), ((), ())), preferred_element_type=F32)


def pieces(value, count):
    terms = []
    for _ in range(count):
        term = value.astype(BF16)
        terms.append(term)
        value = value - term.astype(F32)
    return terms


def spread_heads(value, spread):
    return sum(dot(term, spread) for term in pieces(value, 2))


def gather_heads(value, spread):
    return sum(dot_nt(term, spread) for term in pieces(value, 2))


def running_sum(value, mask):
    return sum(dot(mask, term) for term in pieces(value, 3))


def iota2(rows, cols, dim):
    return lax.broadcasted_iota(jnp.int32, (rows, cols), dim)


def turned(value):
    return jnp.transpose(value.astype(F32)).astype(BF16)


def strips(width):
    return [slice(at, at + STRIP) for at in range(0, width, STRIP)]


def conv_pre(ext, taps, cols):
    total = taps[4:5, cols] + taps[0:1, cols] * ext[pl.ds(RIM - 3, CHUNK), cols]
    for k in range(1, 4):
        total = total + taps[k : k + 1, cols] * ext[pl.ds(RIM - 3 + k, CHUNK), cols]
    return total


def softplus(value):
    return jnp.maximum(value, 0.0) + jnp.log1p(jnp.exp(-jnp.abs(value)))


def write_packed(packed_ref, end, total):
    packed_ref[0, 0:LANES, :] = end.astype(BF16)
    packed_ref[0, LANES:, :] = jnp.zeros((RIM, end.shape[1]), BF16)
    row = iota2(RIM, LANES, 0)
    logs = jnp.zeros((RIM, LANES), F32)
    for k, term in enumerate(pieces(total, 3)):
        logs = jnp.where(row == k, term.astype(F32), logs)
    packed_ref[0, LANES:, 0:LANES] = logs.astype(BF16)


def widened(log, spread):
    return spread_heads(jnp.broadcast_to(jnp.exp(log), (8, LANES)), spread)[0:1, :]


def entering_state(packed_ref, first_ref, second_ref, spread_ref):
    passed = jnp.sum(packed_ref[0, LANES:, 0:LANES].astype(F32), axis=0, keepdims=True)
    from_row = first_ref[0].astype(F32) + second_ref[0].astype(F32)
    return packed_ref[0, 0:LANES, :].astype(F32) + widened(passed, spread_ref[...]) * from_row


def leave_kernel(end_ref, total_ref, packed_ref, spread_ref, leaving_ref):
    kept = packed_ref[0, 0:LANES, :].astype(F32) * widened(total_ref[0, 0:1, :], spread_ref[...])
    leaving_ref[0] = (end_ref[0] + kept).astype(BF16)


def state_kernel(
    mix_ref, halo_ref, step_ref, taps_ref, heads_ref, spread_ref,
    xbc_ref, sum_ref, dt_ref, end_ref, total_ref, packed_ref, ext,
):
    inner = spread_ref.shape[1]
    place = pl.program_id(1)

    @pl.when(place == 0)
    def _():
        ext[0:RIM, :] = halo_ref[0].astype(F32)
        end_ref[...] = jnp.zeros_like(end_ref)
        total_ref[...] = jnp.zeros_like(total_ref)

    @pl.when(place > 0)
    def _():
        ext[0:RIM, :] = ext[CHUNK : CHUNK + RIM, :]

    dt = softplus(step_ref[0].astype(F32) + heads_ref[0:1, :])
    lower = (iota2(CHUNK, CHUNK, 0) >= iota2(CHUNK, CHUNK, 1)).astype(F32).astype(BF16)
    cumul = running_sum(dt * heads_ref[1:2, :], lower)
    sum_ref[0] = cumul
    dt_ref[0] = dt
    last = cumul[CHUNK - 1 : CHUNK, :]
    total_ref[0] += jnp.broadcast_to(last, total_ref.shape[1:])
    tail = jnp.exp(last - cumul) * dt
    decay = jnp.broadcast_to(jnp.exp(last), (8, LANES))
    b_turned = None
    for cols in reversed(strips(xbc_ref.shape[2])):
        ext[RIM:, cols] = mix_ref[0, :, cols].astype(F32)
        pre = conv_pre(ext, taps_ref, cols)
        act = (pre * jax.nn.sigmoid(pre)).astype(BF16)
        xbc_ref[0, :, cols] = act
        if cols.start >= inner:
            b_turned = turned(act[:, 0:LANES])
        else:
            held = spread_ref[:, cols]
            weighted = (act.astype(F32) * spread_heads(tail, held)).astype(BF16)
            kept = end_ref[0, :, cols] * spread_heads(decay, held)[0:1, :]
            end_ref[0, :, cols] = kept + dot(b_turned, weighted)

    @pl.when(place == pl.num_programs(1) - 1)
    def _():
        write_packed(packed_ref, end_ref[0], total_ref[0, 0:1, :])


def scan_kernel(
    xbc_ref, sum_ref, dt_ref, packed_ref, first_ref, second_ref, gate_ref, gm_ref, rows_ref, spread_ref,
    y_ref, mixed_ref, enter_ref, stat_ref, state,
):
    inner = spread_ref.shape[1]

    @pl.when(pl.program_id(1) == 0)
    def _():
        state[...] = entering_state(packed_ref, first_ref, second_ref, spread_ref)

    cumul = sum_ref[0]
    dt = dt_ref[0]
    across = jnp.transpose(cumul)
    last = cumul[CHUNK - 1 : CHUNK, :]
    tail = jnp.exp(last - cumul) * dt
    reach = jnp.exp(cumul)
    decay = jnp.broadcast_to(jnp.exp(last), (8, LANES))
    b_low = xbc_ref[0, :, inner : inner + LANES]
    c_low = xbc_ref[0, :, inner + LANES :]
    b_turned = turned(b_low)
    score = dot_nt(c_low, b_low)
    causal = iota2(HALF, HALF, 0) >= iota2(HALF, HALF, 1)
    first = iota2(1, LANES, 1) < LANES // 2
    squares = jnp.zeros((CHUNK, STRIP), F32)
    crossed = jnp.zeros((CHUNK, STRIP), F32)
    for cols in strips(inner):
        held = spread_ref[:, cols]
        x = xbc_ref[0, :, cols].astype(F32)
        u = x * spread_heads(dt, held)
        weighted = (x * spread_heads(tail, held)).astype(BF16)
        entering = state[:, cols].astype(BF16)
        enter_ref[0, 0, :, cols] = entering
        carried = dot(c_low, entering) * spread_heads(reach, held)
        state[:, cols] = state[:, cols] * spread_heads(decay, held)[0:1, :] + dot(b_turned, weighted)
        for pair in range(STRIP // LANES):
            lanes = slice(pair * LANES, (pair + 1) * LANES)
            top = carried[0:HALF, lanes]
            bottom = carried[HALF:, lanes]
            for side in range(2):
                head = (cols.start + pair * LANES) // (LANES // 2) + side
                mine = jnp.where(first if side == 0 else ~first, u[:, lanes], 0.0).astype(BF16)
                column = cumul[:, head : head + 1]
                row = across[head : head + 1, :]
                corner = jnp.where(causal, jnp.exp(column[0:HALF] - row[:, 0:HALF]), 0.0)
                top = top + dot((score[0:HALF, 0:HALF] * corner).astype(BF16), mine[0:HALF])
                left = jnp.exp(column[HALF:] - row[:, 0:HALF])
                right = jnp.where(causal, jnp.exp(column[HALF:] - row[:, HALF:]), 0.0)
                bottom = bottom + dot((score[HALF:, 0:HALF] * left).astype(BF16), mine[0:HALF])
                bottom = bottom + dot((score[HALF:, HALF:] * right).astype(BF16), mine[HALF:])
            into = slice(cols.start + pair * LANES, cols.start + (pair + 1) * LANES)
            y_ref[0, 0:HALF, into] = top
            y_ref[0, HALF:, into] = bottom
        y = y_ref[0, :, cols] + rows_ref[0:1, cols] * x
        gate = gate_ref[0, :, cols].astype(F32)
        gated = y * gate * jax.nn.sigmoid(gate)
        gained = gated * rows_ref[1:2, cols]
        mixed_ref[0, :, cols] = gained.astype(BF16)
        squares = squares + gated * gated
        crossed = crossed + gained * gm_ref[0, :, cols].astype(F32)
    ones = jnp.ones((8, STRIP), BF16)
    square_row = sum(dot_nt(ones, term) for term in pieces(squares, 3))
    cross_row = sum(dot_nt(ones, term) for term in pieces(crossed, 3))
    stat_ref[0] = jnp.where(iota2(8, CHUNK, 0) == 0, square_row, cross_row)


def gate_kernel(
    inner_full, y_ref, xbc_ref, gate_ref, gm_ref, stat_ref, sum_ref, total_ref, rows_ref, spread_ref,
    gy_ref, gz_ref, mixed_ref, back_ref, gain_ref, packed_ref,
):
    inner = spread_ref.shape[1]

    @pl.when(pl.program_id(1) == 0)
    def _():
        back_ref[...] = jnp.zeros_like(back_ref)

    @pl.when((pl.program_id(0) == 0) & (pl.program_id(1) == 0))
    def _():
        gain_ref[...] = jnp.zeros_like(gain_ref)

    stats = jnp.transpose(stat_ref[0])
    scale = lax.rsqrt(stats[:, 0:1] / inner_full + EPS)
    bent = scale * scale * scale * (stats[:, 1:2] / inner_full)
    cumul = sum_ref[0]
    reach = jnp.exp(cumul)
    decay = jnp.broadcast_to(jnp.exp(cumul[CHUNK - 1 : CHUNK, :]), (8, LANES))
    c_turned = turned(xbc_ref[0, :, inner + LANES :])
    for cols in strips(inner):
        held = spread_ref[:, cols]
        x = xbc_ref[0, :, cols].astype(F32)
        y = y_ref[0, :, cols] + rows_ref[0:1, cols] * x
        gate = gate_ref[0, :, cols].astype(F32)
        sigmoid = jax.nn.sigmoid(gate)
        silu = gate * sigmoid
        gated = y * silu
        scaled = gated * scale
        gm = gm_ref[0, :, cols].astype(F32)
        gain = rows_ref[1:2, cols]
        gg = scale * gm * gain - gated * bent
        gy = (gg * silu).astype(BF16)
        gy_ref[0, :, cols] = gy
        gz_ref[0, :, cols] = (gg * y * sigmoid * (1.0 + gate * (1.0 - sigmoid))).astype(BF16)
        mixed_ref[0, :, cols] = (scaled * gain).astype(BF16)
        gain_ref[:, cols] += jnp.broadcast_to(jnp.sum(gm * scaled, axis=0, keepdims=True), (8, STRIP))
        reached = (gy.astype(F32) * spread_heads(reach, held)).astype(BF16)
        kept = back_ref[0, :, cols] * spread_heads(decay, held)[0:1, :]
        back_ref[0, :, cols] = kept + dot(c_turned, reached)

    @pl.when(pl.program_id(1) == pl.num_programs(1) - 1)
    def _():
        write_packed(packed_ref, back_ref[0], total_ref[0, 0:1, :])


def adjoint_kernel(
    xbc_ref, sum_ref, dt_ref, gy_ref, y_ref, enter_ref, packed_ref, first_ref, second_ref, mix_ref, before_ref, halo_ref,
    step_ref, taps_ref, heads_ref, rows_ref, spread_ref,
    gmix_ref, rim_ref, gtaps_ref, gheads_ref, gskip_ref, back, ext, gpre, pulled,
):
    inner = spread_ref.shape[1]
    chunks = pl.num_programs(1)
    order = pl.program_id(1)

    @pl.when((pl.program_id(0) == 0) & (order == 0))
    def _():
        gtaps_ref[...] = jnp.zeros_like(gtaps_ref)
        gheads_ref[...] = jnp.zeros_like(gheads_ref)
        gskip_ref[...] = jnp.zeros_like(gskip_ref)

    @pl.when(order == 0)
    def _():
        back[...] = entering_state(packed_ref, first_ref, second_ref, spread_ref)
        gpre[CHUNK:, :] = jnp.zeros((8, gpre.shape[1]), F32)

    @pl.when(order > 0)
    def _():
        gpre[CHUNK:, :] = gpre[0:8, :]

    @pl.when(order == chunks - 1)
    def _():
        ext[0:RIM, :] = halo_ref[0].astype(F32)

    @pl.when(order < chunks - 1)
    def _():
        ext[0:RIM, :] = before_ref[0].astype(F32)

    cumul = sum_ref[0]
    dt = dt_ref[0]
    across = jnp.transpose(cumul)
    last = cumul[CHUNK - 1 : CHUNK, :]
    fade = jnp.exp(last - cumul)
    reach = jnp.exp(cumul)
    decay = jnp.broadcast_to(jnp.exp(last), (8, LANES))
    b_low = xbc_ref[0, :, inner : inner + LANES]
    c_low = xbc_ref[0, :, inner + LANES :]
    c_turned = turned(c_low)
    score = dot_nt(b_low, c_low)
    causal = iota2(HALF, HALF, 0) <= iota2(HALF, HALF, 1)
    first = iota2(1, LANES, 1) < LANES // 2
    pulled[...] = jnp.zeros_like(pulled)
    gb = jnp.zeros((CHUNK, LANES), F32)
    gc = jnp.zeros((CHUNK, LANES), F32)
    between = jnp.zeros((CHUNK, LANES), F32)
    arrived = jnp.zeros((CHUNK, LANES), F32)
    direct = jnp.zeros((CHUNK, LANES), F32)
    joined = jnp.zeros((8, LANES), F32)

    def conv_part(cols, gact):
        ext[RIM:, cols] = mix_ref[0, :, cols].astype(F32)
        pre = conv_pre(ext, taps_ref, cols)
        sigmoid = jax.nn.sigmoid(pre)
        gp = gact.astype(BF16).astype(F32) * sigmoid * (1.0 + pre * (1.0 - sigmoid))
        gpre[0:CHUNK, cols] = gp
        rim_ref[0, :, cols] = gp[0:8, :]
        total = taps_ref[3:4, cols] * gp
        for k in range(3):
            total = total + taps_ref[k : k + 1, cols] * gpre[pl.ds(3 - k, CHUNK), cols]
            gtaps_ref[k : k + 1, cols] += jnp.sum(
                gp * ext[pl.ds(RIM - 3 + k, CHUNK), cols], axis=0, keepdims=True
            )
        gtaps_ref[3:4, cols] += jnp.sum(gp * ext[RIM:, cols], axis=0, keepdims=True)
        gtaps_ref[4:5, cols] += jnp.sum(gp, axis=0, keepdims=True)
        gmix_ref[0, :, cols] = total.astype(BF16)

    for cols in strips(inner):
        held = spread_ref[:, cols]
        x = xbc_ref[0, :, cols].astype(F32)
        dt_wide = spread_heads(dt, held)
        fade_wide = spread_heads(fade, held)
        u = x * dt_wide
        u_low = u.astype(BF16)
        weighted = (u * fade_wide).astype(BF16)
        gy_low = gy_ref[0, :, cols]
        gy = gy_low.astype(F32)
        reached = (gy * spread_heads(reach, held)).astype(BF16)
        later = back[:, cols]
        later_low = later.astype(BF16)
        entered = enter_ref[0, 0, :, cols]
        gb = gb + dot_nt(weighted, later_low)
        gc = gc + dot_nt(reached, entered)
        gu_carried = dot(b_low, later_low) * fade_wide
        sums = jnp.sum(later * entered.astype(F32), axis=0, keepdims=True)
        joined = joined + gather_heads(jnp.broadcast_to(sums, (8, STRIP)), held)
        back[:, cols] = later * spread_heads(decay, held)[0:1, :] + dot(c_turned, reached)
        parts = []
        for pair in range(STRIP // LANES):
            lanes = slice(pair * LANES, (pair + 1) * LANES)
            top = gu_carried[0:HALF, lanes]
            bottom = gu_carried[HALF:, lanes]
            gy_pair = gy_low[:, lanes]
            for side in range(2):
                head = (cols.start + pair * LANES) // (LANES // 2) + side
                keep = first if side == 0 else ~first
                gy_mine = jnp.where(keep, gy[:, lanes], 0.0).astype(BF16)
                u_mine = jnp.where(keep, u[:, lanes], 0.0).astype(BF16)
                column = cumul[:, head : head + 1]
                row = across[head : head + 1, :]
                corner = jnp.where(causal, jnp.exp(row[:, 0:HALF] - column[0:HALF]), 0.0)
                side_right = jnp.exp(row[:, HALF:] - column[0:HALF])
                low_right = jnp.where(causal, jnp.exp(row[:, HALF:] - column[HALF:]), 0.0)
                top = top + dot((score[0:HALF, 0:HALF] * corner).astype(BF16), gy_mine[0:HALF])
                top = top + dot((score[0:HALF, HALF:] * side_right).astype(BF16), gy_mine[HALF:])
                bottom = bottom + dot((score[HALF:, HALF:] * low_right).astype(BF16), gy_mine[HALF:])
                upper = dot_nt(u_mine[0:HALF], gy_pair)
                pulled[0:HALF, 0:HALF] += upper[:, 0:HALF] * corner
                pulled[0:HALF, HALF:] += upper[:, HALF:] * side_right
                pulled[HALF:, HALF:] += dot_nt(u_mine[HALF:], gy_pair[HALF:]) * low_right
            parts.append(jnp.concatenate([top, bottom], axis=0))
        gu = jnp.concatenate(parts, axis=1)
        u_kept = u_low.astype(F32)
        between = between + gather_heads(gy * y_ref[0, :, cols] - u_kept * gu, held)
        arrived = arrived + gather_heads(u_kept * gu_carried, held)
        direct = direct + gather_heads(x * gu, held)
        gskip_ref[:, cols] += jnp.broadcast_to(jnp.sum(gy * x, axis=0, keepdims=True), (8, STRIP))
        conv_part(cols, dt_wide * gu + rows_ref[0:1, cols] * gy)

    pulled_low = pulled[...].astype(BF16)
    gb = gb + dot(pulled_low, c_low)
    gc = gc + dot(jnp.transpose(pulled[...]).astype(BF16), b_low)
    conv_part(slice(inner, inner + 2 * LANES), jnp.concatenate([gb, gc], axis=1))

    upper = (iota2(CHUNK, CHUNK, 0) <= iota2(CHUNK, CHUNK, 1)).astype(F32).astype(BF16)
    whole = jnp.sum(arrived, axis=0, keepdims=True) + decay[0:1, :] * joined[0:1, :]
    glg = running_sum(between, upper) + whole
    rate = heads_ref[1:2, :]
    gdt = direct + rate * glg
    raw = step_ref[0].astype(F32) + heads_ref[0:1, :]
    gsi = gdt * jax.nn.sigmoid(raw) * heads_ref[2:3, :]
    gmix_ref[0, :, inner + 2 * LANES :] = gsi.astype(BF16)
    gheads_ref[0:1, :] += jnp.sum(gsi, axis=0, keepdims=True)
    gheads_ref[1:2, :] += jnp.sum(glg * dt * rate, axis=0, keepdims=True)


def flat(width, order=lambda i: i, column=0):
    return pl.BlockSpec((1, CHUNK, width), lambda g, i: (g, order(i), column))


def whole(*shape):
    return pl.BlockSpec((1,) + shape, lambda g, i: (g,) + (0,) * len(shape))


def fixed(shape):
    return pl.BlockSpec(shape, lambda g, i: (0,) * len(shape))


def shaped(shape, dtype=F32):
    return jax.ShapeDtypeStruct(shape, dtype)


def run(kernel, grid, ins, outs, scratch, flops, moved, after=()):
    count = len(ins)
    extra = list(after)

    def body(*refs):
        kernel(*refs[:count], *refs[count + len(extra) :])

    steps = grid[0] * grid[1]
    return pl.pallas_call(
        body,
        grid=grid,
        in_specs=[spec for _, spec in ins] + [pl.BlockSpec(memory_space=pl.ANY)] * len(extra),
        out_specs=[spec for _, spec in outs],
        out_shape=[shape for shape, _ in outs],
        scratch_shapes=scratch,
        compiler_params=pltpu.CompilerParams(
            dimension_semantics=("arbitrary", "arbitrary"), vmem_limit_bytes=VMEM_BYTES
        ),
        cost_estimate=pl.CostEstimate(
            flops=steps * flops, bytes_accessed=steps * moved, transcendentals=0
        ),
    )(*[array for array, _ in ins], *extra)


def local_states(xw, halo, taps, heads, spread, after):
    groups, length, _ = xw.shape
    inner = spread.shape[1]
    width = inner + 2 * LANES
    return run(
        state_kernel,
        (groups, length // CHUNK),
        [
            (xw, flat(width)),
            (halo, whole(RIM, width)),
            (xw, flat(LANES, column=width // LANES)),
            (taps, fixed(taps.shape)),
            (heads, fixed(heads.shape)),
            (spread, fixed(spread.shape)),
        ],
        [
            (shaped((groups, length, width), BF16), flat(width)),
            (shaped((groups, length, LANES)), flat(LANES)),
            (shaped((groups, length, LANES)), flat(LANES)),
            (shaped((groups, LANES, inner)), whole(LANES, inner)),
            (shaped((groups, 8, LANES)), whole(8, LANES)),
            (shaped((groups, LANES + RIM, inner), BF16), whole(LANES + RIM, inner)),
        ],
        [pltpu.VMEM((RIM + CHUNK, width), F32)],
        1_500_000_000,
        2_000_000,
        after,
    )


def mixer(xbc, cumul, dt, start, gate, gm, rows, spread, after):
    groups, length, width = xbc.shape
    inner = spread.shape[1]
    chunks = length // CHUNK
    return run(
        scan_kernel,
        (groups, chunks),
        [
            (xbc, flat(width)),
            (cumul, flat(LANES)),
            (dt, flat(LANES)),
            (start[0], whole(LANES + RIM, inner)),
            (start[1], whole(LANES, inner)),
            (start[2], whole(LANES, inner)),
            (gate, flat(inner)),
            (gm, flat(inner)),
            (rows, fixed(rows.shape)),
            (spread, fixed(spread.shape)),
        ],
        [
            (shaped((groups, length, inner)), flat(inner)),
            (shaped(gate.shape, BF16), flat(inner)),
            (
                shaped((groups, chunks, LANES, inner), BF16),
                pl.BlockSpec((1, 1, LANES, inner), lambda g, i: (g, i, 0, 0)),
            ),
            (shaped((groups, 8, length)), pl.BlockSpec((1, 8, CHUNK), lambda g, i: (g, 0, i))),
        ],
        [pltpu.VMEM((LANES, inner), F32)],
        2_500_000_000,
        4_000_000,
        after,
    )


def gate_back(inner_full, y, xbc, gate, gm, stats, cumul, total, rows, spread, after):
    groups, length, width = xbc.shape
    inner = spread.shape[1]
    chunks = length // CHUNK
    back = lambda i: chunks - 1 - i
    return run(
        functools.partial(gate_kernel, float(inner_full)),
        (groups, chunks),
        [
            (y, flat(inner, back)),
            (xbc, flat(width, back)),
            (gate, flat(inner, back)),
            (gm, flat(inner, back)),
            (stats, pl.BlockSpec((1, 8, CHUNK), lambda g, i: (g, 0, back(i)))),
            (cumul, flat(LANES, back)),
            (total, whole(8, LANES)),
            (rows, fixed(rows.shape)),
            (spread, fixed(spread.shape)),
        ],
        [
            (shaped((groups, length, inner), BF16), flat(inner, back)),
            (shaped(gate.shape, BF16), flat(inner, back)),
            (shaped(gate.shape, BF16), flat(inner, back)),
            (shaped((groups, LANES, inner)), whole(LANES, inner)),
            (shaped((8, inner)), fixed((8, inner))),
            (shaped((groups, LANES + RIM, inner), BF16), whole(LANES + RIM, inner)),
        ],
        [],
        1_500_000_000,
        4_500_000,
        after,
    )


def adjoint(xbc, cumul, dt, gy, y, enter, gin, xw, halo, taps, heads, rows, spread, after):
    groups, length, width = xbc.shape
    inner = spread.shape[1]
    chunks = length // CHUNK
    back = lambda i: chunks - 1 - i
    per = CHUNK // RIM
    return run(
        adjoint_kernel,
        (groups, chunks),
        [
            (xbc, flat(width, back)),
            (cumul, flat(LANES, back)),
            (dt, flat(LANES, back)),
            (gy, flat(inner, back)),
            (y, flat(inner, back)),
            (enter, pl.BlockSpec((1, 1, LANES, inner), lambda g, i: (g, back(i), 0, 0))),
            (gin[0], whole(LANES + RIM, inner)),
            (gin[1], whole(LANES, inner)),
            (gin[2], whole(LANES, inner)),
            (xw, flat(width, back)),
            (
                xw,
                pl.BlockSpec(
                    (1, RIM, width), lambda g, i: (g, jnp.maximum(back(i) * per - 1, 0), 0)
                ),
            ),
            (halo, whole(RIM, width)),
            (xw, flat(LANES, back, width // LANES)),
            (taps, fixed(taps.shape)),
            (heads, fixed(heads.shape)),
            (rows, fixed(rows.shape)),
            (spread, fixed(spread.shape)),
        ],
        [
            (shaped((groups, length, width + LANES), BF16), flat(width + LANES, back)),
            (shaped((groups, 8, width)), whole(8, width)),
            (shaped((8, width)), fixed((8, width))),
            (shaped((8, LANES)), fixed((8, LANES))),
            (shaped((8, inner)), fixed((8, inner))),
        ],
        [
            pltpu.VMEM((LANES, inner), F32),
            pltpu.VMEM((RIM + CHUNK, width), F32),
            pltpu.VMEM((CHUNK + 8, width), F32),
            pltpu.VMEM((CHUNK, CHUNK), F32),
        ],
        8_000_000_000,
        6_000_000,
        after,
    )


def leave(ends, totals, packed, spread):
    groups, states, inner = ends.shape

    def one(*shape):
        return pl.BlockSpec((1,) + shape, lambda g: (g,) + (0,) * len(shape))

    return pl.pallas_call(
        leave_kernel,
        grid=(groups,),
        in_specs=[
            one(states, inner), one(8, LANES), one(states + RIM, inner),
            pl.BlockSpec(spread.shape, lambda g: (0, 0)),
        ],
        out_specs=one(states, inner),
        out_shape=shaped(ends.shape, BF16),
        compiler_params=pltpu.CompilerParams(
            dimension_semantics=("arbitrary",), vmem_limit_bytes=VMEM_BYTES
        ),
        cost_estimate=pl.CostEstimate(
            flops=0, bytes_accessed=8 * groups * states * inner, transcendentals=0
        ),
    )(ends, totals, packed, spread)


def place_kernel(at_ref, first, first_y, second, second_x, full_ref):
    step = pl.program_id(0)
    for number, ref in enumerate((first, first_y, second, second_x)):

        @pl.when(step // 2 == number)
        def _(ref=ref):
            full_ref[0, 0, 0] = ref[0]


def place_row(number, step, at):
    x, core, y = at[0], at[1], at[2]
    later = number // 2
    side = number % 2
    row = x + jnp.where(later == 0, step, side)
    column = y + jnp.where(later == 0, side, step)
    return row % 2, jnp.where(later == 0, core, 1 - core), column % 2, 0, 0


def place(first, first_y, second, second_x):
    _, rows, columns = first.shape
    at = jnp.stack([lax.axis_index(name) for name in ("x", "core", "y")]).astype(jnp.int32)

    def piece(number):
        return pl.BlockSpec(
            (1, rows, columns), lambda i, at: (jnp.clip(i - 2 * number, 0, 1), 0, 0)
        )

    full = pl.pallas_call(
        place_kernel,
        grid_spec=pltpu.PrefetchScalarGridSpec(
            num_scalar_prefetch=1,
            grid=(8,),
            in_specs=[piece(number) for number in range(4)],
            out_specs=pl.BlockSpec(
                (1, 1, 1, rows, columns), lambda i, at: place_row(i // 2, i % 2, at)
            ),
        ),
        out_shape=shaped((2, 2, 2, rows, columns), first.dtype),
        compiler_params=pltpu.CompilerParams(
            dimension_semantics=("arbitrary",), vmem_limit_bytes=VMEM_BYTES
        ),
        cost_estimate=pl.CostEstimate(
            flops=0, bytes_accessed=rows * columns, transcendentals=0
        ),
    )(at, first, first_y, second, second_x)
    return full.reshape(8 * rows, columns)


def join_kernel(at_ref, own, got, far_own, far_got, full_ref):
    half_is_own = pl.program_id(1) == at_ref[0]
    for core, (mine, other) in enumerate(((own, got), (far_own, far_got))):
        for ref, wanted in ((mine, half_is_own), (other, ~half_is_own)):

            @pl.when(wanted & (pl.program_id(0) == core))
            def _(ref=ref):
                full_ref[0] = ref[...]


def joined(own, got, far_own, far_got, part=0):
    _, rows, columns = own.shape
    at = lax.axis_index("zq").astype(jnp.int32)[None]
    piece = pl.BlockSpec((None, rows, columns), lambda c, h, at: (part, 0, 0))
    return pl.pallas_call(
        join_kernel,
        grid_spec=pltpu.PrefetchScalarGridSpec(
            num_scalar_prefetch=1,
            grid=(2, 2),
            in_specs=[piece] * 4,
            out_specs=pl.BlockSpec((1, rows, columns), lambda c, h, at: (c, h, 0)),
        ),
        out_shape=shaped((2, 2 * rows, columns), own.dtype),
        compiler_params=pltpu.CompilerParams(
            dimension_semantics=("arbitrary", "arbitrary"), vmem_limit_bytes=VMEM_BYTES
        ),
        cost_estimate=pl.CostEstimate(
            flops=0, bytes_accessed=16 * rows * columns, transcendentals=0
        ),
    )(at, own, got, far_own, far_got)


def swap(value, axis):
    return lax.ppermute(value, axis, [(0, 1), (1, 0)])


def sum_axis(value, axis):
    if lax.axis_size(axis) == 2:
        return value + swap(value, axis)
    return lax.psum(value, axis)


def cut(value, axis, dim):
    size = value.shape[dim] // 2
    at = lax.axis_index(axis)
    kept = lax.dynamic_slice_in_dim(value, at * size, size, dim)
    return kept, lax.dynamic_slice_in_dim(value, (1 - at) * size, size, dim)


def added(kept, got, dtype=BF16):
    return (kept.astype(F32) + got.astype(F32)).astype(dtype)


def hold(value, *before):
    if not before:
        return value
    return lax.optimization_barrier((value,) + before)[0]


def shift(value, by):
    blocks = lax.axis_size(("y", "zp"))
    pairs = [(i, i + by) for i in range(blocks) if 0 <= i + by < blocks]
    return lax.ppermute(value, ("y", "zp"), pairs)


def row_hop(packed, way, *before):
    return hold(lax.ppermute(packed, "zp", [(0, 1)] if way == 1 else [(1, 0)]), *before)


def column_hops(leaving, way, *before):
    source = 1 if way == 1 else 2
    pairs = [[(source, source + way * (1 + to))] for to in range(2)]
    return [hold(lax.ppermute(leaving, ("y", "zp"), pair), *before) for pair in pairs]


def chained(packed, way):
    blocks = lax.axis_size(("y", "zp"))
    groups, _, inner = packed.shape
    heads = inner // (LANES // 2)
    entering = jnp.zeros((groups, LANES, inner), F32)
    passed = jnp.zeros((groups, 1, LANES), F32)
    for by in range(1, blocks):
        got = shift(packed, by * way).astype(F32)
        weight = jnp.repeat(jnp.exp(passed[:, :, 0:heads]), LANES // 2, axis=2)
        entering = entering + weight * got[:, 0:LANES]
        passed = passed + jnp.sum(got[:, LANES:, 0:LANES], axis=1, keepdims=True)
    none = jnp.zeros(entering.shape, BF16)
    return jnp.pad(entering.astype(BF16), ((0, 0), (0, RIM), (0, 0))), none, none


def all_pairs():
    return all(lax.axis_size(name) == 2 for name in ("x", "y", "zp"))


NEAR = [(0, 1), (3, 2), (1, 3), (2, 0)]
FAR = [(1, 2), (2, 1)]
HOME = [(to, source) for source, to in NEAR]


def fetched(piece, near, far):
    at_home = lax.axis_index("core") == lax.axis_index("zp")
    return jnp.where(at_home, piece, near), jnp.where(at_home, near, far)


def fetch(piece):
    return lax.ppermute(piece, ("core", "zp"), NEAR), lax.ppermute(piece, ("core", "zp"), FAR)


def gather_slice(piece):
    owners = lax.axis_size("zp")
    rows = lax.all_gather(piece, ("x", "core", "y"), axis=0, tiled=True)
    parts = lax.all_gather(rows, "zp")
    return lax.dynamic_slice_in_dim(parts, lax.axis_index("core") * (owners // 2), owners // 2, 0)


def reduce_slice(parts):
    owners = lax.axis_size("zp")
    full = jnp.zeros((owners,) + parts.shape[1:], parts.dtype)
    full = lax.dynamic_update_slice_in_dim(
        full, parts, lax.axis_index("core") * (owners // 2), axis=0
    )
    mine = lax.psum_scatter(full, "zp", scatter_dimension=0, tiled=True)[0]
    mine = lax.psum_scatter(mine, ("x", "core", "y"), scatter_dimension=0, tiled=True)
    return mine.astype(F32)


def cut_rows(fulls):
    core = lax.axis_index("core")
    same, cross = [], []
    for full in fulls:
        rows, columns = full.shape[0] // 8, full.shape[1]
        full = full.reshape(2, 2, 2, rows, columns)
        same.append(cut(lax.dynamic_index_in_dim(full, core, 1, False), "x", 0))
        cross.append(cut(lax.dynamic_index_in_dim(full, 1 - core, 1, False), "y", 1))
    return (
        [kept[0] for kept, _ in same],
        [kept[:, 0] for kept, _ in cross],
        jnp.stack([sent[0] for _, sent in same]),
        jnp.stack([sent[:, 0] for _, sent in cross]),
    )


def cut_again(sames, crosses):
    same = [cut(value, "y", 0) for value in sames]
    cross = [cut(value, "x", 0) for value in crosses]
    return (
        [kept[0] for kept, _ in same],
        [kept[0] for kept, _ in cross],
        jnp.stack([sent[0] for _, sent in same]),
        jnp.stack([sent[0] for _, sent in cross]),
    )


def both(kept, got):
    return [
        [added(mine, other[k]) for k, mine in enumerate(values)]
        for values, other in zip(kept[0:2], got)
    ]


def home_parts(sames, crosses):
    at_home = lax.axis_index("core") == lax.axis_index("zp")
    cross = jnp.stack(crosses)
    return jnp.where(at_home, cross, jnp.stack(sames)), cross


def at_owner(near, far, sames):
    at_home = lax.axis_index("core") == lax.axis_index("zp")
    return [
        near[k].astype(F32) + jnp.where(at_home, same.astype(F32), far[k].astype(F32))
        for k, same in enumerate(sames)
    ]


def go_home(sent):
    return (
        lax.ppermute(sent[0], ("core", "zp"), HOME),
        lax.ppermute(sent[1], ("core", "zp"), FAR),
    )


def own_of_slice(value):
    owners = lax.axis_size("zp")
    core, part = lax.axis_index("core"), lax.axis_index("zp")
    other = swap(value, "core")
    share = value.shape[-1] // (owners // 2)
    wanted = jnp.where(part // (owners // 2) == core, value, other)
    return lax.dynamic_slice_in_dim(wanted, (part % (owners // 2)) * share, share, value.ndim - 1)


def slice_of_own(value, after):
    owners = lax.axis_size("zp")
    core = lax.axis_index("core")
    if owners == 2:
        other = hold(swap(value, "zp"), after)
        return jnp.where(core == lax.axis_index("zp"), value, other)[None]
    parts = lax.all_gather(value, "zp")
    return lax.dynamic_slice_in_dim(parts, core * (owners // 2), owners // 2, 0)


def per_device(
    hidden,
    cotangent,
    norm_gain,
    w_z,
    w_x,
    w_bc,
    w_dt,
    conv_x,
    conv_x_bias,
    conv_bc,
    conv_bc_bias,
    dt_bias,
    a_log,
    d_skip,
    inner_gain,
    w_out,
):
    micro, own_len, model = hidden.shape
    owners = lax.axis_size("zp")
    share = w_x.shape[1]
    own_heads = w_dt.shape[1]
    inner_full = share * 2 * owners
    states2 = w_bc.shape[1]
    halves = owners // 2
    inner = share * halves
    heads = own_heads * halves
    head_width = inner // heads
    width = inner + states2

    def matmul(left, right, contract, dtype=F32):
        return lax.dot_general(
            left, right, (contract, ((), ())), preferred_element_type=F32
        ).astype(dtype)

    def spliced(parts, sizes):
        if halves == 1:
            return parts[0]
        columns, at = [], 0
        for size, copies in sizes:
            columns += [parts[k][:, at : at + size] for k in range(halves if copies else 1)]
            at += size
        return jnp.concatenate(columns, axis=1)

    parts = range(micro)

    own = hidden.astype(F32)
    gain_in = norm_gain.astype(F32)
    r0 = lax.rsqrt(jnp.mean(own * own, axis=-1, keepdims=True) + EPS)
    filler = LANES // halves - own_heads
    own_first = jnp.concatenate(
        [w_x, w_bc, w_dt, jnp.zeros((w_dt.shape[0], filler), BF16)], axis=1
    )
    own_second = jnp.concatenate([w_z, jnp.transpose(w_out)], axis=1)
    normed_own = [(own[part : part + 1] * r0[part : part + 1] * gain_in).astype(BF16) for part in parts]
    fast = all_pairs()

    def tokens_of(value, *before):
        got = hold(swap(value, "zq"), *before)
        return value, got, swap(value, "core"), swap(got, "core")

    if fast:
        got = fetch(own_first)
    fours = [tokens_of(normed_own[0])]
    if fast:
        same, cross = fetched(own_first, *got)
        moved = hold((swap(same, "x"), swap(cross, "y")), fours[0][1])
        first, second = jnp.stack([same, moved[0]]), jnp.stack([cross, moved[1]])
        own_second = hold(own_second, fours[0][1], *moved)
        got = fetch(own_second)
        rest = swap(first, "y"), swap(second, "x")
        later = first, second
    else:
        later = (fours[0][1],)
    for part in parts[1:]:
        fours.append(tokens_of(hold(normed_own[part], fours[0][1]), *later))
        later = (fours[-1][1],)
    if fast:
        w_first = place(first, rest[0], second, rest[1])
        got = hold(got, w_first)
        same, cross = fetched(own_second, *got)
        moved = swap(same, "x"), swap(cross, "y")
    else:
        w_first = spliced(
            gather_slice(own_first), ((share, 1), (states2, 0), (own_heads, 1), (filler, 1))
        )
    normed = [joined(*four) for four in fours]
    per_head = jnp.concatenate([dt_bias, a_log, d_skip])
    per_head = jnp.pad(per_head, (0, share - 3 * own_heads))
    small = jnp.concatenate([conv_x, conv_x_bias[None], inner_gain[None]], axis=0).astype(F32)
    small = jnp.concatenate([small, per_head[None], jnp.zeros((1, share), F32)])
    small = slice_of_own(small, w_first)
    channel_rows = jnp.concatenate([small[k, 0:6] for k in range(halves)], axis=1)
    head_rows = jnp.concatenate(
        [small[k, 6, 0 : 3 * own_heads].reshape(3, own_heads) for k in range(halves)], axis=1
    )
    conv_shared = jnp.concatenate([conv_bc, conv_bc_bias[None]], axis=0).astype(F32)
    taps = jnp.pad(jnp.concatenate([channel_rows[0:5], conv_shared], axis=1), ((0, 3), (0, 0)))
    head_in = jnp.stack([head_rows[0], -jnp.exp(head_rows[1]), jnp.ones((heads,), F32)])
    head_in = jnp.pad(head_in, ((0, 5), (0, LANES - heads)))
    rows = jnp.stack([jnp.repeat(head_rows[2], head_width), channel_rows[5]])
    rows = jnp.pad(rows, ((0, 6), (0, 0)))
    spread = (
        lax.broadcasted_iota(jnp.int32, (LANES, inner), 1) // head_width
        == lax.broadcasted_iota(jnp.int32, (LANES, inner), 0)
    ).astype(BF16)

    scans = []
    for part in parts:
        xw = matmul(normed[part], w_first, ((2,), (0,)), BF16)
        scans.append((xw, shift(xw[:, -RIM:, 0:width], 1)))
        if part == 0:
            normed[-1] = hold(normed[-1], xw)
    if fast:
        moved = hold(moved, scans[0][0])
        first, second = jnp.stack([same, moved[0]]), jnp.stack([cross, moved[1]])
        got_second = first, swap(first, "y"), second, swap(second, "x")
    local = []
    for part in parts:
        before = [k[5] for k in local[-1:]]
        local.append(local_states(*scans[part], taps, head_in, spread, before))
        if part == 0:
            cot_own = hold(cotangent, local[0][5], scans[-1][1])
            cot_own = [cot_own[k : k + 1] for k in parts]
            cot_got = [swap(value, "zq") for value in cot_own]
    totals = [local[part][4] for part in parts]
    packed = [local[part][5] for part in parts]
    if fast:
        w_second = place(*hold(got_second, packed[-1]))
    else:
        w_second = spliced(
            gather_slice(hold(own_second, packed[-1])), ((share, 1), (share, 1))
        )
    w_gate, w_down = w_second[:, 0:inner], w_second[:, inner:]
    def hop(part, packed, ends, way, *before):
        if not fast:
            return packed, packed
        got = row_hop(packed, way, *before)
        return got, leave(ends, totals[part], got, spread)

    def entering(found, way, *before):
        if not fast:
            return chained(found[0], way)
        return found[0], *column_hops(found[1], way, *before)

    found = [hop(0, packed[0], local[0][3], 1, w_second)]
    gate = [
        matmul(hold(normed[part], found[0][1]), w_gate, ((2,), (0,)), BF16) for part in parts
    ]
    cot_far = (
        swap(hold(cotangent, local[0][5]), "core"),
        [swap(hold(cot_got[k], gate[k]), "core") for k in parts],
    )

    def whole_cot(part, *before):
        far = hold((cot_far[0], cot_far[1][part]), *before)
        return joined(cot_own[part], cot_got[part], far[0][part : part + 1], far[1])

    cot = [whole_cot(0, gate[-1])]

    w_down_held = hold(w_down, found[0][1])
    gm = [matmul(cot[0], w_down_held, ((2,), (0,)), BF16)]
    mixes, stats, branches, gates = [], [], [], []
    g_gate = g_down = 0.0
    tokens = ((0, 1), (0, 1))
    for part in parts:
        xbc, cumul, dt = local[part][0:3]
        before = (gm[0],) if part == 0 else (gates[part - 1][5], gm[part])
        start = entering(found[part], 1, *before)
        y, gained, enter, stat = mixer(xbc, cumul, dt, start, gate[part], gm[part], rows, spread, before)
        mixes.append((y, enter))
        other = swap(stat, "core")
        if part + 1 < micro:
            following = hold(packed[part + 1], found[part][1])
            found.append(hop(part + 1, following, local[part + 1][3], 1, y))
            cot.append(whole_cot(part + 1, found[-1][1]))
            gm.append(matmul(cot[-1], w_down, ((2,), (0,)), BF16))
            other = hold(other, cot[-1])
        else:
            g_gate = matmul(normed[0], hold(gates[0][1], y), tokens, BF16)
            other = hold(other, g_gate)
        stat = stat + jnp.flip(other, 0)
        other = swap(stat, "zq")
        branch = matmul(hold(gained, stat, gm[-1]), w_down, ((2,), (1,)), BF16)
        stats.append(stat + hold(other, branch))
        branches.append((branch, swap(branch[1], "core")))
        gates.append(
            gate_back(
                inner_full, y, xbc, gate[part], gm[part], stats[part], cumul, totals[part],
                rows, spread, [branch],
            )
        )
    back_packed = [g[5] for g in gates]

    found = [hop(0, back_packed[0], gates[0][3], -1, back_packed[-1])]
    for part in parts:
        g_down = (g_down + matmul(cot[part], hold(gates[part][2], found[0][1]), tokens)).astype(BF16)
        if part == 0:
            branch_cut = [
                cut(added(branch[0], hold(got, g_down)), "zq", 0) for branch, got in branches
            ]
            branch_sent = jnp.stack([sent for _, sent in branch_cut])
            branch_got = swap(branch_sent, "zq")
        else:
            g_gate = g_gate + matmul(normed[part], hold(gates[part][1], g_down), tokens)
    g_gate, g_down = g_gate.astype(BF16), g_down.astype(BF16)
    g_normed_gate = [matmul(hold(gates[0][1], g_gate), w_gate, ((2,), (1,)), BF16)]
    gin = entering(found[0], -1, g_normed_gate[0])
    for part in parts[1:]:
        following = hold(back_packed[part], found[part - 1][1])
        found.append(hop(part, following, gates[part][3], -1, g_normed_gate[0]))
    wait_for = [found[-1][1], branch_sent]
    if fast:
        second = cut_rows(hold([g_gate, g_down], *gin))
        moved = swap(second[2], "x"), swap(second[3], "y")
        wait_for += second[2:]

    g_first, heads_out, g_hidden, g_norm_gain = 0.0, [], [], 0.0

    def token_grad(part, kept, got):
        x, r, g = own[part], r0[part], added(kept, got, F32)
        q0 = g * gain_in
        grad = (
            cotangent[part].astype(F32) + r * q0
            - x * (r * r * r) * jnp.mean(q0 * x, axis=-1, keepdims=True)
        )
        return grad, jnp.sum(g * x * r, axis=0)

    def whole_output(*before):
        outputs = []
        for part in parts:
            square = lax.dynamic_slice_in_dim(
                stats[part][0, 0], lax.axis_index("zq") * own_len, own_len, 0
            )
            r1 = lax.rsqrt(square / inner_full + EPS)[:, None]
            got = hold(branch_got, *before)[part]
            outputs.append((own[part] + r1 * added(branch_cut[part][0], got, F32)).astype(BF16))
        return jnp.stack(outputs)

    for part in parts:
        xbc, cumul, dt = local[part][0:3]
        gmix, rim, *sums = adjoint(
            xbc, cumul, dt, gates[part][0], mixes[part][0], mixes[part][1], gin,
            *scans[part], taps, head_in, rows, spread, wait_for,
        )
        if part == micro - 1 and fast and micro > 1:
            got_home = hold(got_home, gmix)
            g_gate, g_down = at_owner(*got_home, pair[0])
            rim = hold(rim, g_gate, g_down)
        if part < micro - 1:
            gin = entering(found[part + 1], -1)
            gmix, rim, *sums = hold(
                (gmix, rim, *sums), *gin, branch_got, *(moved if fast else ())
            )
        heads_out.append(sums)
        ahead = shift(rim, -1)
        last_part = part == micro - 1
        if last_part:
            if micro > 1:
                kept, got = norm_cut
                grad, gain = token_grad(part - 1, kept, hold(got, gmix))
                g_hidden.append(grad)
                g_norm_gain = g_norm_gain + gain
                ahead = hold(ahead, grad)
        else:
            if fast:
                moved = hold(moved, gmix)
                second = cut_again(*both(second, moved))
                moved = swap(second[2], "y"), swap(second[3], "x")
        fix = jnp.stack(
            [sum(taps[k, :] * ahead[:, r - k] for k in range(r + 1)) for r in range(3)], axis=1
        )
        length = gmix.shape[1]
        last = gmix[:, length - RIM :].astype(F32)
        last = last + jnp.pad(fix, ((0, 0), (RIM - 3, 0), (0, LANES)))
        gmix = lax.dynamic_update_slice_in_dim(gmix, last.astype(BF16), length - RIM, 1)

        def for_weights(gmix):
            return (g_first + matmul(normed[part], gmix, tokens)).astype(BF16)

        def for_tokens(gmix):
            total = g_normed_gate[part] + matmul(gmix, w_first, ((2,), (1,)))
            return total.astype(BF16)

        total = for_tokens(gmix)
        other = swap(total[1], "core")
        g_first = for_weights(hold(gmix, total))
        if last_part:
            g_first = g_first.astype(BF16)
            if fast:
                first = cut_rows([g_first])
                moved_first = swap(first[2], "x"), swap(first[3], "y")
        else:
            g_normed_gate.append(
                matmul(hold(gates[part + 1][1], g_first), w_gate, ((2,), (1,)), BF16)
            )
            kept, sent = cut(added(total[0], hold(other, g_first)), "zq", 0)
            norm_cut = kept, swap(sent, "zq")
            if part == micro - 2:
                outputs = whole_output(g_normed_gate[-1], sent)
            gin = hold(gin, outputs)
            wait_for = [sent, outputs]
            if fast and part == micro - 2:
                moved = hold(moved, g_normed_gate[-1])
                pair = both(second, moved)
                home = home_parts(*pair)
                wait_for += home
                got_home = go_home(home)

    kept, sent = cut(added(total[0], hold(other, g_first, *(first[2:] if fast else ()))), "zq", 0)
    got_norm = swap(sent, "zq")
    if fast:
        first = cut_again(*both(first, hold(moved_first, sent)))
        moved = swap(first[2], "y"), swap(first[3], "x")
        got_norm = hold(got_norm, *first[2:])
        pair = both(first, hold(moved, got_norm))
        home = home_parts(*pair)
        got_home = go_home(home)
        grad, gain = token_grad(micro - 1, kept, hold(got_norm, *home))
        g_first = at_owner(*hold(got_home, grad), pair[0])[0]
    else:
        g_gate, g_down = [
            reduce_slice(jnp.stack(jnp.split(value, halves, axis=1))) for value in (g_gate.astype(BF16), g_down.astype(BF16))
        ]
        grad, gain = token_grad(micro - 1, kept, got_norm)
        g_first = reduce_slice(
            jnp.concatenate(
                [
                    jnp.stack(jnp.split(g_first[:, 0:inner], halves, axis=1)),
                    jnp.concatenate(
                        [
                            g_first[None, :, inner:width],
                            jnp.zeros((halves - 1, model, states2), BF16),
                        ]
                    ),
                    jnp.stack(jnp.split(g_first[:, width : width + heads], halves, axis=1)),
                ],
                axis=2,
            )
        )
    g_hidden = jnp.stack(g_hidden + [grad])
    g_norm_gain = g_norm_gain + gain
    g_bc = g_first[:, share : share + states2]
    if fast:
        across = lax.ppermute(g_bc, ("zp", "zq"), [(0, 3), (3, 0), (1, 2), (2, 1)])
        g_bc = (g_bc + swap(g_bc, "zq")) + (swap(g_bc, "zp") + across)
    else:
        g_bc = sum_axis(sum_axis(g_bc, "zp"), "zq")

    g_taps, g_heads, g_skip = (sum(b[k] for b in heads_out) for k in range(3))
    g_gain = sum(g[4] for g in gates)
    skip_heads = jnp.sum(g_skip[0].reshape(heads, head_width), axis=1)
    small = jnp.concatenate(
        [g_taps[0:5, 0:inner].reshape(-1), g_gain[0], g_heads[0, 0:heads], g_heads[1, 0:heads], skip_heads]
    )
    size = small.shape[0]
    packed = jnp.concatenate([small, g_taps[0:5, inner:width].reshape(-1), g_norm_gain])
    packed = sum_axis(sum_axis(packed, "x"), "y")
    packed = sum_axis(hold(packed, g_first), "zp")
    small = packed[:size]
    shared = sum_axis(sum_axis(packed[size:], "core"), "zq")
    bc_rows = shared[0 : 5 * states2].reshape(5, states2)
    channel = own_of_slice(small[0 : 6 * inner].reshape(6, inner))
    per_head = own_of_slice(small[6 * inner :].reshape(3, heads))
    return (
        outputs,
        g_hidden,
        shared[5 * states2 :],
        g_gate,
        g_first[:, 0:share],
        g_bc,
        g_first[:, share + states2 : share + states2 + own_heads],
        channel[0:4],
        channel[4],
        bc_rows[0:4],
        bc_rows[4],
        per_head[0],
        per_head[1],
        per_head[2],
        channel[5],
        jnp.transpose(g_down),
    )


def solution(mesh):
    dp, seq, tensor = (mesh.shape[name] for name in ("dp", "seq", "tensor"))
    fine = Mesh(
        mesh.devices.reshape(dp // 2, 2, seq, tensor // 2, 2), ("x", "core", "y", "zp", "zq")
    )
    data, tens = ("x", "core", "y"), ("zp", "zq")
    tokens = P(("x", "core"), ("y", "zp", "zq"), None)
    params = (
        P(),
        P(data, tens),
        P(data, tens),
        P(data, None),
        P(data, tens),
        P(None, tens),
        P(tens),
        P(),
        P(),
        P(tens),
        P(tens),
        P(tens),
        P(tens),
        P(tens, data),
    )
    return jax.shard_map(
        per_device,
        mesh=fine,
        in_specs=(tokens, tokens) + params,
        out_specs=(tokens, tokens) + params,
        check_vma=False,
    )
```
